32 devices in a mesh: seq: 8 (over z, x), stream: 4 (over y, core).
Axes of the slice: x: 2, y: 2, z: 4, core: 2. Of those that a mesh axis runs over, the one named last changes fastest.
Arguments:
- tokens: bfloat16 [4, 4096, 1024], P('stream', 'seq'), may hold values from -6 to 6
- cotangent: bfloat16 [4, 4096, 1024], P('stream', 'seq'), may hold values from -6 to 6
- lengths: int32 [4, 4], P('stream'), may hold values from 64 to 3072, as said below
- order: int32 [4, 4], P('stream'), may hold values from 0 to 3, each once within a row
- weights: float32 [12, 1024, 1024], P(None, 'seq')
- momentum: float32 [12, 1024, 1024], P(None, 'seq')
- small_params: float32 [13312], P('seq')
- moment_one: float32 [13312], P('seq'), may hold values from -40 to 40
- moment_two: float32 [13312], P('seq'), may hold values from 163.84 to 3276.8
Outputs:
- block_out: bfloat16 [4, 4096, 1024], P('stream', 'seq')
- input_grad: float32 [4, 4096, 1024], P('stream', 'seq')
- new_weights: float32 [12, 1024, 1024], P(None, 'seq')
- new_momentum: float32 [12, 1024, 1024], P(None, 'seq')
- new_small: float32 [13312], P('seq')
- new_moment_one: float32 [13312], P('seq')
- new_moment_two: float32 [13312], P('seq')
The draws below stay inside these ranges and needn't reach their ends.
Inputs may be any that keep to these rules, and one draw needn't show every extreme that they name: Each row holds the four lengths 48 * 64, 768, 192 and 64 in some order; they sum to 4096. `order`: each row is a permutation of 0 to 3.
All inputs are finite; a program needn't handle non-finite values.
Results may differ from the reference program's by a relative error of at most 0.006.
The reference program's roundings to bfloat16 on the way count: a program that leaves them out, or rounds other values in their place, can miss the bound.
Values may be sent and summed in bfloat16 or wider, within the bound.
A program may use at most 384 MiB of HBM per device.

```python
import math
import jax
import jax.numpy as jnp
from jax import lax

D = 1024
HEADS = 16
HEAD_DIM = 64
FF = 4096
GROUP = 512
IMAGES = 4
STEP = 10
UNITS = 12
LENGTH = 4096
STREAMS = 4


def unit_table(first, second, third, fourth, fifth, sixth, blocks):
    index = jnp.arange(4 + 2 * blocks)
    table = jnp.where(index < 2, first, jnp.where(index == 2, second, jnp.where(index == 3, third, fourth)))
    table = jnp.where(index >= 4 + blocks, fifth, table)
    return table * sixth


def base_draw(key, shape):
    return jax.random.normal(key, shape, jnp.float32)


def draw_lengths(key, part):
    key = jax.random.fold_in(key, 14)
    shares = jnp.array([48, 12, 3, 1], dtype=jnp.int32) * (LENGTH // 64)
    keys = jax.random.split(key, STREAMS)
    picks = jax.vmap(lambda one: jax.random.permutation(one, 4))(keys)
    return shares[picks].astype(jnp.int32)


def draw_weights(key, part):
    key = jax.random.fold_in(key, 11)
    blocks = FF // D
    base = base_draw(key, (UNITS, D, D))
    scales = unit_table(D ** (-0.5), D ** (-0.5), 8.0 * D ** (-0.5), D ** (-0.5), FF ** (-0.5), 1.0, blocks)
    return base * scales[:, None, None]


def draw_momentum(key, part):
    key = jax.random.fold_in(key, 12)
    blocks = FF // D
    base = base_draw(key, (UNITS, D, D))
    scales = unit_table(0.05, 0.15, 0.05, 0.3, 0.6, float(STREAMS * LENGTH) ** 0.5, blocks)
    return base * scales[:, None, None]


def draw_small_params(key, part):
    key = jax.random.fold_in(key, 13)
    total = 9 * D + FF
    base = jnp.clip(base_draw(key, (total,)), -4.0, 4.0)
    index = jnp.arange(total)
    gains = (index < D) | (index >= 2 * D) & (index < 3 * D)
    return jnp.where(gains, 1.0 + 0.1 * base, 0.3 * base)


def raised(entries, rng, source, target, blocks, factor):
    owner, partner = [(jnp.arange(entries.shape[position]) // (entries.shape[position] // blocks)).reshape([-1 if axis == position else 1 for axis in range(entries.ndim)]) for position in (source, target)]
    chosen = jax.random.permutation(rng, blocks)[partner]
    strong = (owner == chosen) | (owner == (partner + blocks // 2) % blocks)
    return jnp.where(strong, factor * entries, entries)


def shard_levels(rng, extent, cuts, low, high):
    level, own = 1.0, jax.random.fold_in(rng, 6)
    for position, parts in cuts:
        heights = jnp.exp(jax.random.uniform(jax.random.fold_in(own, position), (parts,), jnp.float32, low / len(cuts), high / len(cuts)))
        level = level * jnp.repeat(heights, extent[position] // parts).reshape([-1 if axis == position else 1 for axis in range(len(extent))])
    return level


def normal_values(stream_key, shape, scale, limit, cuts=(), kind=jnp.bfloat16):
    entries = scale * jax.random.normal(stream_key, shape, jnp.float32)
    if cuts:
        entries = entries * shard_levels(stream_key, shape, cuts, -0.22, 0.18)
    return jnp.clip(entries, -limit, limit).astype(kind)


def heavy_noise(key, dims, deviation, bound, cuts, heavy, kind=jnp.bfloat16):
    drawn = deviation * jax.random.normal(key, dims, jnp.float32)
    if cuts:
        drawn = drawn * shard_levels(key, dims, cuts, -0.22, 0.18)
    return jnp.clip(raised(drawn, jax.random.fold_in(key, 3), *heavy), -bound, bound).astype(kind)


def setup_inputs(seed: int = 0) -> dict:
    key_of = jax.random.split(jax.random.key(seed), 10)
    return {
        "tokens": normal_values(key_of[0], (STREAMS, LENGTH, D), 1.0, 6.0, ((0, 4), (1, 8))),
        "cotangent": heavy_noise(key_of[1], (STREAMS, LENGTH, D), 1.0, 6.0, ((0, 4), (1, 8)), (1, 2, 8, 2.0)),
        "lengths": draw_lengths(jax.random.fold_in(key_of[9], 71), 0),
        "order": jax.vmap(lambda own: jax.random.permutation(own, IMAGES))(jax.random.split(key_of[3], STREAMS)).reshape((STREAMS, IMAGES)).astype(jnp.int32),
        "weights": draw_weights(jax.random.fold_in(key_of[9], 71), 0),
        "momentum": draw_momentum(jax.random.fold_in(key_of[9], 71), 0),
        "small_params": draw_small_params(jax.random.fold_in(key_of[9], 71), 0),
        "moment_one": normal_values(key_of[7], (9 * D + FF,), (0.05 * (STREAMS * LENGTH) ** 0.5), 40.0, ((0, 8),), jnp.float32),
        "moment_two": jnp.clip(jnp.exp(math.log(3276.8) - 2.9957323 * jax.random.uniform(key_of[8], (9 * D + FF,), jnp.float32) ** shard_levels(key_of[8], (9 * D + FF,), ((0, 8),), -0.2, 0.2)), 163.84, 3276.8),
    }


@jax.custom_vjp
def low(v):
    return lax.optimization_barrier(v.astype(jnp.bfloat16)).astype(jnp.float32)

@jax.custom_vjp
def low_back(v):
    return v

def low_keep(v):
    return (low(v), None)

def low_pass(kept, grad):
    return (grad,)

def back_keep(v):
    return (v, None)

def back_low(kept, grad):
    return (low(grad),)
low.defvjp(low_keep, low_pass)
low_back.defvjp(back_keep, back_low)
highest = lax.Precision.HIGHEST

def matmul(left, right):
    return jnp.dot(left, right, precision=highest, preferred_element_type=jnp.float32)

def layer_norm(values, gain, offset):
    center = values - lax.optimization_barrier(jnp.mean(values, axis=-1, keepdims=True))
    spread = lax.optimization_barrier(jnp.mean(center * center, axis=-1, keepdims=True))
    return center * lax.rsqrt(spread + 1e-05) * gain + offset

def feature(values):
    return jax.nn.elu(values) + 1.0

def segment_of(lengths_row, order_row, positions):
    places = jnp.arange(lengths_row.shape[0], dtype=jnp.int32)
    packed = lax.optimization_barrier(jnp.sum(jnp.where(order_row[:, None] == places[None, :], lengths_row[None, :], 0), axis=1))
    ends = jnp.cumsum(packed).astype(jnp.int32)
    return lax.optimization_barrier(jnp.sum((positions[:, None] >= ends[None, :]).astype(jnp.int32), axis=1)).astype(jnp.int32)

def split_small(vector, width):
    pieces = [vector[index * width:(index + 1) * width] for index in range(9)]
    return pieces + [vector[9 * width:]]

def unit_rates(blocks):
    return jnp.array([0.5, 0.5, 0.5, 4.0] + [0.5] * blocks + [0.25] * blocks, dtype=jnp.float32)

def attention_block(carry, inputs):
    state, total = carry
    query, key_feat, value, segment, before = inputs
    offsets = jnp.arange(segment.shape[0], dtype=jnp.int32)
    keep = ((offsets[None, :] <= offsets[:, None]) & (segment[:, None] == segment[None, :])).astype(jnp.float32)
    scores = low_back(jnp.einsum('thd,shd->hts', query, key_feat, precision=highest) * keep[None])
    denom = lax.optimization_barrier(jnp.sum(scores, axis=2)).T
    numer = jnp.einsum('hts,she->the', low(scores), value, precision=highest)
    incoming = (segment == before).astype(jnp.float32)
    numer = numer + incoming[:, None, None] * jnp.einsum('thd,hde->the', query, state, precision=highest)
    denom = denom + incoming[:, None] * jnp.einsum('thd,hd->th', query, total, precision=highest)
    ratio = low(low_back(numer) / denom[:, :, None])
    finals = (segment == segment[-1]).astype(jnp.float32)
    passes = (segment[-1] == before).astype(jnp.float32)
    keys_last = key_feat * finals[:, None, None]
    new_state = jnp.einsum('shd,she->hde', keys_last, value, precision=highest) + passes * state
    new_total = lax.optimization_barrier(jnp.sum(keys_last, axis=0)) + passes * total
    return ((new_state, new_total), ratio)

def stream_forward(tokens_row, wl, spl, segment, before):
    blocks = FF // D
    gain_one, bias_one, gain_two, bias_two, bias_q, bias_k, bias_v, bias_o, bias_down, bias_up = split_small(spl, D)
    w_up = jnp.concatenate([wl[4 + index] for index in range(blocks)], axis=1)
    w_down = wl[4 + blocks:].reshape(FF, D)
    normed = low(layer_norm(tokens_row, gain_one, bias_one))
    query = low(feature(low_back(matmul(normed, wl[0]) + bias_q)))
    keys = low(feature(low_back(matmul(normed, wl[1]) + bias_k)))
    values = low(low_back(matmul(normed, wl[2]) + bias_v))
    count = LENGTH // GROUP
    layout = (count, GROUP, HEADS, HEAD_DIM)
    start_state = (jnp.zeros((HEADS, HEAD_DIM, HEAD_DIM), jnp.float32), jnp.zeros((HEADS, HEAD_DIM), jnp.float32))
    stepper = jax.checkpoint(attention_block)
    _, ratios = lax.scan(stepper, start_state, (query.reshape(layout), keys.reshape(layout), values.reshape(layout), segment.reshape(count, GROUP), before))
    attended = ratios.reshape(LENGTH, D)
    resid = tokens_row + low_back(matmul(attended, wl[3]) + bias_o)
    hidden = low(layer_norm(resid, gain_two, bias_two))
    active = low(jax.nn.gelu(low_back(matmul(hidden, w_up) + bias_up)))
    return resid + matmul(active, w_down) + bias_down

def orthogonalize(matrix):
    current = matrix / (jnp.sqrt(jnp.sum(matrix * matrix)) + 1e-07)
    for turn in range(5):
        gram = matmul(current, current.T)
        poly = -4.775 * gram + 2.0315 * matmul(gram, gram)
        current = 3.4445 * current + matmul(poly, current)
    return current

def reference(tokens, cotangent, lengths, order, weights, momentum, small_params, moment_one, moment_two):
    positions = jnp.arange(LENGTH, dtype=jnp.int32)
    starts = jnp.arange(LENGTH // GROUP, dtype=jnp.int32) * GROUP - 1
    segments = [segment_of(lengths[index], order[index], positions) for index in range(STREAMS)]
    befores = [segment_of(lengths[index], order[index], starts) for index in range(STREAMS)]

    def forward(weight_all, small_all, inputs):
        wl = low(weight_all)
        spl = low(small_all)
        return jnp.stack([stream_forward(inputs[index], wl, spl, segments[index], befores[index]) for index in range(STREAMS)])
    outputs, pull = jax.vjp(forward, weights, small_params, tokens.astype(jnp.float32))
    grad_w, grad_s, grad_in = pull(cotangent.astype(jnp.float32))
    new_momentum = 0.5 * momentum + grad_w
    update = lax.map(orthogonalize, new_momentum)
    rates = unit_rates(FF // D)
    new_weights = weights - rates[:, None, None] * (update + 0.01 * weights)
    first_new = 0.9 * moment_one + 0.1 * grad_s
    second_new = 0.95 * moment_two + 0.05 * grad_s * grad_s
    adjusted = first_new / (1.0 - 0.9 ** STEP) / (jnp.sqrt(second_new / (1.0 - 0.95 ** STEP)) + 1e-08)
    new_small = small_params - 0.05 * (adjusted + 0.01 * small_params)
    return (outputs.astype(jnp.bfloat16), grad_in, new_weights, new_momentum, new_small, first_new, second_new)
```

```python
import functools

import jax
import jax.numpy as jnp
from jax import lax
from jax.experimental import pallas as pl
from jax.experimental.pallas import tpu as pltpu
from jax.sharding import PartitionSpec as P

MESH = pl.DeviceIdType.MESH
DMA = pltpu.SemaphoreType.DMA
ANY = pl.BlockSpec(memory_space=pl.ANY)
VMEM = pl.BlockSpec(memory_space=pltpu.VMEM)
VMEM_LIMIT = 62 << 20


def places():
    seq = lax.axis_index("seq")
    stream = lax.axis_index("stream")
    return seq // 2, seq % 2, stream // 2, stream % 2


def device(z, x, y, c):
    return {"seq": z * 2 + x, "stream": y * 2 + c}


def greet(peers):
    barrier = pltpu.get_barrier_semaphore()
    for peer in peers:
        pl.semaphore_signal(barrier, inc=1, device_id=peer, device_id_type=MESH)
    pl.semaphore_wait(barrier, len(peers))


def remote(source, target, sent, received, peer):
    return pltpu.make_async_remote_copy(
        src_ref=source,
        dst_ref=target,
        send_sem=sent,
        recv_sem=received,
        device_id=peer,
        device_id_type=MESH,
    )


def others_along_seq(z, x, y, c, count):
    straight = [device(lax.rem(z + k, count), x, y, c) for k in range(1, count)]
    across = [device(lax.rem(z + k, count), 1 - x, y, c) for k in range(count)]
    return straight, across


def gather_kernel(
    count, w_ref, small_ref, out_ref, small_out, own_sem, zs, zr, ps, pr, ss, sr
):
    batches = w_ref.shape[0]
    z, x, y, c = places()
    straight, across = others_along_seq(z, x, y, c, count)
    pair = [device(z, 1 - x, y, c), device(z, x, 1 - y, c), device(z, x, y, 1 - c)]
    greet(straight + across + pair[1:])
    small = []
    for k, peer in enumerate(straight + across):
        small.append(remote(small_ref, small_out.at[z * 2 + x], ss.at[k], sr.at[k], peer))
        small[-1].start()
    own = [
        pltpu.make_async_copy(w_ref, out_ref.at[:, :, :, z, x], own_sem.at[0]),
        pltpu.make_async_copy(small_ref, small_out.at[z * 2 + x], own_sem.at[1]),
    ]
    spread = {}

    def send_own(b):
        for k in range(1, count):
            spread[b, k] = remote(
                w_ref.at[b, y, c], out_ref.at[b, y, c, z, x],
                zs.at[b, k - 1], zr.at[b, k - 1], straight[k - 1],
            )
            spread[b, k].start()

    send_own(0)
    for copy in own:
        copy.start()
    first, second, third = [], [], []
    total = batches * count

    def send(kept, phase, index, source, target, peer):
        kept.append(remote(source, target, ps.at[phase, index], pr.at[phase, index], peer))
        kept[-1].start()

    for step in range(total + 3):
        index = step
        if index < total:
            b, k = divmod(index, count)
            there = lax.rem(z - k + count, count)
            if k == 0:
                send(first, 0, index, w_ref.at[b, y, c], out_ref.at[b, y, c, z, x], pair[0])
            else:
                spread[b, k].wait_recv()
                block = out_ref.at[b, y, c, there, x]
                send(first, 0, index, block, block, pair[(k + b) % 2])
            if k == min(1, count - 1) and b + 1 < batches:
                send_own(b + 1)
        index = step - 1
        if 0 <= index < total:
            b, k = divmod(index, count)
            there = lax.rem(z - k + count, count)
            first[index].wait_recv()
            if k == 0:
                block, peer = out_ref.at[b, y, c, z, 1 - x], pair[1]
            elif (k + b) % 2 == 0:
                block, peer = out_ref.at[b, y, c, there], pair[1]
            else:
                block, peer = out_ref.at[b, :, c, there, x], pair[0]
            send(second, 1, index, block, block, peer)
        index = step - 2
        if 0 <= index < total:
            b, k = divmod(index, count)
            there = lax.rem(z - k + count, count)
            second[index].wait_recv()
            block = out_ref.at[b, :, c, z, 1 - x] if k == 0 else out_ref.at[b, :, c, there]
            send(third, 2, index, block, block, pair[2])
        index = step - 3
        if 0 <= index < total:
            third[index].wait_recv()
    for copy in list(spread.values()) + first + second + third:
        copy.wait_send()
    for copy in small + own:
        copy.wait()


def gather(weights, small, nseq):
    units, rows, width = weights.shape
    count = nseq // 2
    batches = units // 4
    steps = batches * count
    out, small_out = pl.pallas_call(
        functools.partial(gather_kernel, count),
        out_shape=(
            jax.ShapeDtypeStruct((batches, 2, 2, count, 2, rows, width), weights.dtype),
            jax.ShapeDtypeStruct((nseq,) + small.shape, small.dtype),
        ),
        in_specs=[VMEM, VMEM],
        out_specs=[ANY, VMEM],
        scratch_shapes=[
            DMA((2,)),
            DMA((batches, count - 1)),
            DMA((batches, count - 1)),
            DMA((3, steps)),
            DMA((3, steps)),
            DMA((nseq - 1,)),
            DMA((nseq - 1,)),
        ],
        compiler_params=pltpu.CompilerParams(
            collective_id=0, has_side_effects=True, vmem_limit_bytes=VMEM_LIMIT
        ),
    )(weights.reshape(batches, 2, 2, rows, width), small)
    return out.reshape(units, nseq * rows, width), small_out


CHUNK = 32


def add_into(target, left, right):
    rows = target.shape[-2]

    def body(index, carry):
        span = pl.ds(pl.multiple_of(index * CHUNK, CHUNK), CHUNK)
        total = left[span, :].astype(jnp.float32) + right[span, :].astype(jnp.float32)
        target[span, :] = total.astype(target.dtype)
        return carry

    lax.fori_loop(0, rows // CHUNK, body, 0)


def reduce_kernel(
    count, wide_ref, low_ref, small_ref, out_ref, small_out,
    core_wide, core_low, own_wide, own_low, fs_wide, fs_low, fr_wide, fr_low, kept_first,
    ss_wide, ss_low, sr_wide, sr_low, kept_second, zs_wide, zs_low, zr_wide, zr_low,
    sm_recv, sm_part, sm_pair,
    load_sem, cs, cr, fs, fr, es, er, zs, zr, ms, mr,
):
    z, x, y, c = places()
    straight, across = others_along_seq(z, x, y, c, count)
    pair = [device(z, 1 - x, y, c), device(z, x, 1 - y, c), device(z, x, y, 1 - c)]
    greet(straight + across + pair[1:])
    wide_count, low_count = wide_ref.shape[0], low_ref.shape[0]
    order = [("low", b) for b in reversed(range(low_count))] + [
        ("wide", b) for b in range(wide_count)
    ]
    steps = [(kind, b, k) for kind, b in order for k in range(count)]
    total = len(steps)
    small = []
    seqs = [lax.rem(z + k, count) * 2 + x for k in range(1, count)] + [
        lax.rem(z + k, count) * 2 + 1 - x for k in range(count)
    ]
    for k, (peer, there) in enumerate(zip(straight + across, seqs)):
        small.append(remote(small_ref.at[there], sm_recv.at[k], ms.at[k], mr.at[k], peer))
        small[-1].start()

    def at(index):
        kind, b, k = steps[index]
        there = lax.rem(z + 1 + k, count)
        source = wide_ref if kind == "wide" else low_ref
        slot = b * count + k
        return kind, b, k, there, source, slot

    loads, cores, firsts, seconds, spread = [], [], [], [], {}
    ring = 3

    def pick(kind, wide, low):
        return wide if kind == "wide" else low

    def start_core(index):
        kind, b, k, there, source, slot = at(index)
        target = pick(kind, core_wide, core_low).at[slot]
        copy = remote(source.at[b, :, 1 - c, there], target, cs.at[index], cr.at[index], pair[2])
        copy.start()
        cores.append(copy)

    def start_load(index):
        kind, b, k, there, source, slot = at(index)
        target = pick(kind, own_wide, own_low).at[index % 2]
        copy = pltpu.make_async_copy(source.at[b, :, c, there], target, load_sem.at[index])
        copy.start()
        loads.append(copy)

    for index in range(min(3, total)):
        start_core(index)
    start_load(0)
    for step in range(total + 3):
        index = step
        if index < total:
            kind, b, k, there, source, slot = at(index)
            if index + 1 < total:
                start_load(index + 1)
            if index + 3 < total:
                start_core(index + 3)
            loads[index].wait()
            cores[index].wait_recv()
            own = pick(kind, own_wide, own_low).at[index % 2]
            got = pick(kind, core_wide, core_low).at[slot]
            if index >= ring:
                firsts[index - ring].wait_send()
            out = pick(kind, fs_wide, fs_low).at[index % ring]
            kept = kept_first.at[index % ring]
            for j in range(2):
                if k % 2 == 0:
                    add_into(out.at[j], own.at[1 - y, j], got.at[1 - y, j])
                    add_into(kept.at[j], own.at[y, j], got.at[y, j])
                else:
                    add_into(out.at[j], own.at[j, 1 - x], got.at[j, 1 - x])
                    add_into(kept.at[j], own.at[j, x], got.at[j, x])
            target = pick(kind, fr_wide, fr_low).at[slot]
            copy = remote(out, target, fs.at[index], fr.at[index], pair[1 - k % 2])
            copy.start()
            firsts.append(copy)
        index = step - 1
        if 0 <= index < total:
            kind, b, k, there, source, slot = at(index)
            firsts[index].wait_recv()
            kept = kept_first.at[index % ring]
            got = pick(kind, fr_wide, fr_low).at[slot]
            if index >= ring:
                seconds[index - ring].wait_send()
            out = pick(kind, ss_wide, ss_low).at[index % ring]
            mine = x if k % 2 == 0 else y
            add_into(out, kept.at[1 - mine], got.at[1 - mine])
            add_into(kept_second.at[index % ring], kept.at[mine], got.at[mine])
            target = pick(kind, sr_wide, sr_low).at[slot]
            copy = remote(out, target, es.at[index], er.at[index], pair[k % 2])
            copy.start()
            seconds.append(copy)
        index = step - 2
        if 0 <= index < total:
            kind, b, k, there, source, slot = at(index)
            seconds[index].wait_recv()
            got = pick(kind, sr_wide, sr_low).at[slot]
            batch = b if kind == "wide" else wide_count + b
            if k < count - 1:
                out = pick(kind, zs_wide, zs_low).at[b, k]
                add_into(out, kept_second.at[index % ring], got)
                target = pick(kind, zr_wide, zr_low).at[b, k]
                spread[index] = remote(out, target, zs.at[batch, k], zr.at[batch, k], straight[k])
                spread[index].start()
            else:
                add_into(out_ref.at[batch], kept_second.at[index % ring], got)
        index = step - 3
        if 0 <= index < total:
            kind, b, k, there, source, slot = at(index)
            if k == count - 1:
                batch = b if kind == "wide" else wide_count + b
                for j in range(count - 1):
                    spread[index - (count - 1) + j].wait_recv()
                    add_into(out_ref.at[batch], out_ref.at[batch], pick(kind, zr_wide, zr_low).at[b, j])
    part = small_ref[z * 2 + x]
    for k, copy in enumerate(small):
        copy.wait_recv()
        part = part + sm_recv[k]
    sm_part[0] = part
    tail = []
    for j in range(2):
        copy = remote(sm_part.at[j], sm_pair.at[j], ms.at[len(small) + j], mr.at[len(small) + j], pair[1 + j])
        copy.start()
        copy.wait_recv()
        tail.append(copy)
        if j == 0:
            sm_part[1] = sm_part[0] + sm_pair[0]
        else:
            small_out[...] = sm_part[1] + sm_pair[1]
    for copy in small + tail + cores + firsts[-ring:] + seconds[-ring:] + list(spread.values()):
        copy.wait_send()


def reduce_rows(wide, low, small, nseq):
    count = nseq // 2
    wide_count, low_count = wide.shape[0] // 4, low.shape[0] // 4
    width = wide.shape[-1]
    rows = wide.shape[1] // nseq
    batches = wide_count + low_count
    steps = batches * count
    wide = wide.reshape(wide_count, 2, 2, count, 2, rows, width)
    low = low.reshape(low_count, 2, 2, count, 2, rows, width)
    f32, bf16 = jnp.float32, jnp.bfloat16
    V = pltpu.VMEM
    nw, nl = wide_count * count, low_count * count
    return pl.pallas_call(
        functools.partial(reduce_kernel, count),
        out_shape=(
            jax.ShapeDtypeStruct((batches, rows, width), f32),
            jax.ShapeDtypeStruct(small.shape[1:], f32),
        ),
        in_specs=[ANY, ANY, VMEM],
        out_specs=[VMEM, VMEM],
        scratch_shapes=[
            V((nw, 2, 2, rows, width), f32),
            V((nl, 2, 2, rows, width), bf16),
            V((2, 2, 2, rows, width), f32),
            V((2, 2, 2, rows, width), bf16),
            V((3, 2, rows, width), f32),
            V((3, 2, rows, width), bf16),
            V((nw, 2, rows, width), f32),
            V((nl, 2, rows, width), bf16),
            V((3, 2, rows, width), f32),
            V((3, rows, width), f32),
            V((3, rows, width), bf16),
            V((nw, rows, width), f32),
            V((nl, rows, width), bf16),
            V((3, rows, width), f32),
            V((wide_count, count - 1, rows, width), f32),
            V((low_count, count - 1, rows, width), bf16),
            V((wide_count, count - 1, rows, width), f32),
            V((low_count, count - 1, rows, width), bf16),
            V((nseq - 1,) + small.shape[1:], f32),
            V((2,) + small.shape[1:], f32),
            V((2,) + small.shape[1:], f32),
            DMA((steps,)),
            DMA((steps,)),
            DMA((steps,)),
            DMA((steps,)),
            DMA((steps,)),
            DMA((steps,)),
            DMA((steps,)),
            DMA((batches, count - 1)),
            DMA((batches, count - 1)),
            DMA((nseq + 1,)),
            DMA((nseq + 1,)),
        ],
        compiler_params=pltpu.CompilerParams(
            collective_id=1, has_side_effects=True, vmem_limit_bytes=VMEM_LIMIT
        ),
    )(wide, low, small)


SHIFTS = (0.0, 0.0, 0.1, 0.7, 0.7)
FINE = (False, False, False, True, True)
BAND = 256


def split_two(values):
    high = values.astype(jnp.bfloat16)
    return high, (values - high.astype(jnp.float32)).astype(jnp.bfloat16)


def dot(left, right, transposed=False):
    dims = (((1,), (1 if transposed else 0,)), ((), ()))
    return lax.dot_general(left, right, dims, preferred_element_type=jnp.float32)


def orthogonalize(full, xh, xl, gram, gram_low):
    size = full.shape[0]
    bands = size // BAND

    def span(index):
        return pl.ds(pl.multiple_of(index * BAND, BAND), BAND)

    def square(index, total):
        part = full[span(index), :]
        return total + jnp.sum(part * part)

    norm = jnp.sqrt(lax.fori_loop(0, bands, square, jnp.float32(0.0)))
    scale = 1.0 / (norm + 1e-07)

    def begin(index, carry):
        part = full[span(index), :] * scale
        full[span(index), :] = part
        xh[0, span(index), :] = part.astype(jnp.bfloat16)
        return carry

    lax.fori_loop(0, bands, begin, 0)
    for turn in range(len(SHIFTS)):
        shift, fine = SHIFTS[turn], FINE[turn]
        now, later = turn % 2, 1 - turn % 2
        more = turn + 1 < len(SHIFTS) and FINE[turn + 1]

        def form(index, carry):
            rows = span(index)
            left = xh[now, rows, :]
            block = dot(left, xh[now], True)
            if fine:
                block += dot(left, xl[now], True) + dot(xl[now, rows, :], xh[now], True)
            if shift:
                across = lax.broadcasted_iota(jnp.int32, block.shape, 1)
                down = lax.broadcasted_iota(jnp.int32, block.shape, 0) + index * BAND
                block = jnp.where(across == down, block - shift, block)
            gram[rows, :] = block
            gram_low[rows, :] = block.astype(jnp.bfloat16)
            return carry

        lax.fori_loop(0, bands, form, 0)
        linear = -4.775 + 2.0 * 2.0315 * shift
        scaled = 3.4445 - 4.775 * shift + 2.0315 * shift * shift

        def advance(index, carry):
            rows = span(index)
            poly = linear * gram[rows, :] + 2.0315 * dot(gram_low[rows, :], gram_low[...])
            if fine:
                high, low = split_two(poly)
                step = dot(high, xh[now]) + dot(high, xl[now]) + dot(low, xh[now])
            else:
                step = dot(poly.astype(jnp.bfloat16), xh[now])
            moved = scaled * full[rows, :] + step
            full[rows, :] = moved
            if more:
                high, low = split_two(moved)
                xh[later, rows, :] = high
                xl[later, rows, :] = low
            else:
                xh[later, rows, :] = moved.astype(jnp.bfloat16)
            return carry

        lax.fori_loop(0, bands, advance, 0)
    return len(SHIFTS) % 2


def muon_kernel(
    count, g_ref, mom_ref, all_ref, rows_ref,
    mom_own, moved, full, xh, xl, gram, gram_low,
    load_sem, own_sem, ms, mr, ys, yr, os_, or_, fs, fr, gs, gr,
):
    z, x, y, c = places()
    seq = z * 2 + x
    nseq = count * 2
    batches, rows, width = g_ref.shape
    straight, across = others_along_seq(z, x, y, c, count)
    pair = [device(z, x, 1 - y, c), device(z, x, y, 1 - c)]
    greet(straight + across + pair)
    load = pltpu.make_async_copy(mom_ref.at[:, y, c], mom_own, load_sem)
    load.start()
    keep = pltpu.make_async_copy(g_ref, all_ref.at[:, y, c], own_sem.at[0])
    keep.start()
    load.wait()
    owner = [2 * b + c + 1 for b in range(batches)]

    def block(where):
        return full.at[pl.ds(pl.multiple_of(where * rows, rows), rows)]

    for b in range(batches):
        for j in range(rows // CHUNK):
            span = slice(j * CHUNK, (j + 1) * CHUNK)
            moved[b, span, :] = 0.5 * mom_own[b, span, :] + g_ref[b, span, :]

        @pl.when(seq != owner[b])
        def _():
            remote(
                moved.at[b], block(seq), ms.at[b], mr.at[seq],
                {"seq": owner[b], "stream": y * 2 + c},
            ).start()

        @pl.when(seq == owner[b])
        def _():
            pltpu.make_async_copy(moved.at[b], block(seq), own_sem.at[1]).start()

    over = remote(g_ref, all_ref.at[:, y, c], ys.at[0], yr.at[0], pair[0])
    over.start()
    is_owner = (seq == owner[0]) | (seq == owner[1]) | (seq == owner[2])

    @pl.when(is_owner)
    def _():
        pltpu.make_async_copy(moved.at[0], block(seq), own_sem.at[1]).wait()
        for k in range(1, nseq):
            there = lax.rem(seq + k, nseq)
            remote(moved.at[0], block(there), ms.at[0], mr.at[there], pair[0]).wait_recv()
        orthogonalize(full, xh, xl, gram, gram_low)

    final = len(SHIFTS) % 2

    def result(where):
        return xh.at[final, pl.ds(pl.multiple_of(where * rows, rows), rows)]

    for b in range(batches):
        target = rows_ref.at[b, y, c]

        @pl.when(seq == owner[b])
        def _():
            pltpu.make_async_copy(result(seq), target, own_sem.at[2]).start()
            for k in range(1, nseq):
                there = lax.rem(seq + k, nseq)
                remote(
                    result(there), target, os_.at[k - 1], or_.at[b],
                    {"seq": there, "stream": y * 2 + c},
                ).start()

    keep.wait()
    over.wait_recv()
    share = remote(all_ref.at[:, :, c], all_ref.at[:, :, c], ys.at[1], yr.at[1], pair[1])
    share.start()
    hops = []
    for b in range(batches):
        target = rows_ref.at[b, y, c]

        @pl.when(seq == owner[b])
        def _():
            pltpu.make_async_copy(result(seq), target, own_sem.at[2]).wait()

        @pl.when(seq != owner[b])
        def _():
            remote(result(seq), target, os_.at[0], or_.at[b], pair[0]).wait_recv()

        hop = remote(target, target, fs.at[b], fr.at[b], pair[0])
        hop.start()
        hops.append(hop)
    lasts = []
    for b in range(batches):
        hops[b].wait_recv()
        target = rows_ref.at[b, :, c]
        last = remote(target, target, gs.at[b], gr.at[b], pair[1])
        last.start()
        lasts.append(last)
    for last in lasts:
        last.wait_recv()
    share.wait_recv()
    for copy in [over, share] + hops + lasts:
        copy.wait_send()
    for b in range(batches):

        @pl.when(seq != owner[b])
        def _():
            remote(moved.at[b], block(seq), ms.at[b], mr.at[seq], pair[0]).wait_send()

        @pl.when(seq == owner[b])
        def _():
            for k in range(1, nseq):
                there = lax.rem(seq + k, nseq)
                remote(result(there), rows_ref.at[b, y, c], os_.at[k - 1], or_.at[b], pair[0]).wait_send()


def muon(sums, momentum, nseq):
    count = nseq // 2
    batches, rows, width = sums.shape
    units = momentum.shape[0]
    f32, bf16 = jnp.float32, jnp.bfloat16
    V = pltpu.VMEM
    whole, ortho = pl.pallas_call(
        functools.partial(muon_kernel, count),
        out_shape=(
            jax.ShapeDtypeStruct((batches, 2, 2, rows, width), f32),
            jax.ShapeDtypeStruct((batches, 2, 2, rows, width), bf16),
        ),
        in_specs=[VMEM, ANY],
        out_specs=[ANY, ANY],
        scratch_shapes=[
            V((batches, rows, width), f32),
            V((batches, rows, width), f32),
            V((width, width), f32),
            V((2, width, width), bf16),
            V((2, width, width), bf16),
            V((width, width), f32),
            V((width, width), bf16),
            DMA,
            DMA((3,)),
            DMA((batches,)),
            DMA((nseq,)),
            DMA((2,)),
            DMA((2,)),
            DMA((nseq - 1,)),
            DMA((batches,)),
            DMA((batches,)),
            DMA((batches,)),
            DMA((batches,)),
            DMA((batches,)),
        ],
        compiler_params=pltpu.CompilerParams(
            collective_id=2, has_side_effects=True, vmem_limit_bytes=VMEM_LIMIT
        ),
    )(sums, momentum.reshape(batches, 2, 2, rows, width))
    return whole.reshape(units, rows, width), ortho.reshape(units, rows, width)


D = 1024
HEADS = 16
HEAD_DIM = 64
FF = 4096
STEP = 10


highest = lax.Precision.HIGHEST


def passed_along(array, axis, by):
    count = lax.axis_size(axis)
    pairs = [(i, i + by) for i in range(count) if 0 <= i + by < count]
    return lax.ppermute(array, axis, pairs)


def layer_norm(values, gain, offset):
    center = values - jnp.mean(values, axis=-1, keepdims=True)
    spread = jnp.mean(center * center, axis=-1, keepdims=True)
    return center * lax.rsqrt(spread + 1e-05) * gain + offset


def feature(values):
    return jax.nn.elu(values) + 1.0


def segment_of(lengths_row, order_row, positions):
    places = jnp.arange(lengths_row.shape[0], dtype=jnp.int32)
    packed = jnp.sum(
        jnp.where(order_row[:, None] == places[None, :], lengths_row[None, :], 0), axis=1
    )
    ends = jnp.cumsum(packed)
    return jnp.sum((positions[:, None] >= ends[None, :]).astype(jnp.int32), axis=1)


def split_small(vector, width):
    pieces = [vector[index * width : (index + 1) * width] for index in range(9)]
    return pieces + [vector[9 * width :]]


def unit_rates(blocks):
    return jnp.array([0.5, 0.5, 0.5, 4.0] + [0.5] * blocks + [0.25] * blocks, dtype=jnp.float32)


def pack_state(matrix, totals, passes):
    flags = jnp.zeros_like(totals[:, None, :]) + passes
    return jnp.concatenate([matrix, totals[:, None, :], flags], axis=1)


def combine_states(earlier, later):
    scale = later[:, -1:, :]
    head_rows = later[:, :-1, :] + scale * earlier[:, :-1, :]
    return jnp.concatenate([head_rows, earlier[:, -1:, :] * scale], axis=1)


def relay_forward(own):

    def forward_turn(turn, running):
        return passed_along(combine_states(running, own), "seq", 1)

    arriving = lax.fori_loop(0, lax.axis_size("seq") - 1, forward_turn, jnp.zeros_like(own))
    return arriving


def relay_backward(own):

    def backward_turn(turn, running):
        return passed_along(combine_states(running, own).astype(jnp.bfloat16), "seq", -1).astype(
            jnp.float32
        )

    leaving = lax.fori_loop(0, lax.axis_size("seq") - 1, backward_turn, jnp.zeros_like(own))
    return leaving


def padded(vector):
    short = 2048 - vector.shape[-1]
    edges = [(0, 0)] * (vector.ndim - 1) + [(0, short)]
    return jnp.pad(vector, edges).reshape(vector.shape[:-1] + (16, 128))


def local(
    tokens, cotangent, lengths, order, weights, momentum, small_params, moment_one, moment_two
):
    group = tokens.shape[1]
    width = tokens.shape[2]
    heads = HEADS
    depth = HEAD_DIM
    blocks = FF // D
    units = weights.shape[0]
    nseq = lax.axis_size("seq")
    share = small_params.shape[0]
    gathered, small_low = gather(
        weights.astype(jnp.bfloat16), padded(small_params.astype(jnp.bfloat16)), nseq
    )
    small_low = small_low.reshape(nseq, 2048)[:, :share].reshape(nseq * share)
    small = small_low.astype(jnp.float32)
    gain_one, bias_one, gain_two, bias_two, bias_q, bias_k, bias_v, bias_o, bias_down, bias_up = (
        split_small(small, width)
    )
    w_query = gathered[0]
    w_key = gathered[1]
    w_value = gathered[2]
    w_out = gathered[3]
    w_up = gathered[4 : 4 + blocks]
    w_down = gathered[4 + blocks :].reshape(blocks * width, width)
    start = lax.axis_index("seq") * group
    positions = start + jnp.arange(group, dtype=jnp.int32)
    segment = segment_of(lengths[0], order[0], positions)
    before = segment_of(lengths[0], order[0], jnp.reshape(start - 1, (1,)))[0]
    offsets = jnp.arange(group, dtype=jnp.int32)
    keep = ((offsets[None, :] <= offsets[:, None]) & (segment[:, None] == segment[None, :])).astype(
        jnp.float32
    )
    incoming = (segment == before).astype(jnp.float32)
    finals = (segment == segment[-1]).astype(jnp.float32)
    passes = (segment[-1] == before).astype(jnp.float32)
    inputs = tokens[0].astype(jnp.float32)
    normed = layer_norm(inputs, gain_one, bias_one).astype(jnp.bfloat16)
    query_pre = jnp.dot(normed, w_query, preferred_element_type=jnp.float32) + bias_q
    key_pre = jnp.dot(normed, w_key, preferred_element_type=jnp.float32) + bias_k
    value_pre = jnp.dot(normed, w_value, preferred_element_type=jnp.float32) + bias_v
    query_low = feature(query_pre).astype(jnp.bfloat16).reshape(group, heads, depth)
    key_low = feature(key_pre).astype(jnp.bfloat16).reshape(group, heads, depth)
    value_low = value_pre.astype(jnp.bfloat16).reshape(group, heads, depth)
    scores = (
        jnp.einsum("thd,shd->hts", query_low, key_low, preferred_element_type=jnp.float32)
        * keep[None]
    )
    denom = jnp.sum(scores, axis=2).T
    scores_low = scores.astype(jnp.bfloat16)
    numer = jnp.einsum("hts,she->the", scores_low, value_low, preferred_element_type=jnp.float32)
    keys_last = key_low * finals.astype(jnp.bfloat16)[:, None, None]
    own_state = jnp.einsum("shd,she->hde", keys_last, value_low, preferred_element_type=jnp.float32)
    own_total = jnp.sum(keys_last.astype(jnp.float32), axis=0)
    arriving = relay_forward(pack_state(own_state, own_total, passes))
    state_in = arriving[:, :depth, :]
    total_in = arriving[:, depth, :]
    query_wide = query_low.astype(jnp.float32)
    numer = numer + incoming[:, None, None] * jnp.einsum(
        "thd,hde->the", query_wide, state_in, precision=highest
    )
    denom = denom + incoming[:, None] * jnp.einsum(
        "thd,hd->th", query_wide, total_in, precision=highest
    )
    attended = (numer / denom[:, :, None]).reshape(group, width).astype(jnp.bfloat16)
    resid = inputs + jnp.dot(attended, w_out, preferred_element_type=jnp.float32) + bias_o
    hidden = layer_norm(resid, gain_two, bias_two).astype(jnp.bfloat16)
    up_pre = (
        jnp.einsum("td,jdf->tjf", hidden, w_up, preferred_element_type=jnp.float32).reshape(
            group, blocks * width
        )
        + bias_up
    )
    active = jax.nn.gelu(up_pre).astype(jnp.bfloat16)
    output = resid + jnp.dot(active, w_down, preferred_element_type=jnp.float32) + bias_down
    block_out = output.astype(jnp.bfloat16)[None]
    grad_out = cotangent[0]
    grad_down = jnp.einsum("tf,td->fd", active, grad_out, preferred_element_type=jnp.float32)
    grad_bias_down = jnp.sum(grad_out.astype(jnp.float32), axis=0)
    grad_active = jnp.einsum("td,fd->tf", grad_out, w_down, preferred_element_type=jnp.float32)
    _, gelu_pull = jax.vjp(jax.nn.gelu, up_pre)
    grad_up_low = gelu_pull(grad_active)[0].astype(jnp.bfloat16)
    grad_up_blocks = grad_up_low.reshape(group, blocks, width)
    grad_w_up = jnp.einsum(
        "td,tjf->jdf", hidden, grad_up_blocks, preferred_element_type=jnp.float32
    )
    grad_bias_up = jnp.sum(grad_up_low.astype(jnp.float32), axis=0)
    grad_hidden = jnp.einsum(
        "tjf,jdf->td", grad_up_blocks, w_up, preferred_element_type=jnp.float32
    )
    _, norm_two_pull = jax.vjp(layer_norm, resid, gain_two, bias_two)
    grad_resid_norm, grad_gain_two, grad_bias_two = norm_two_pull(grad_hidden)
    grad_resid = grad_out.astype(jnp.float32) + grad_resid_norm
    grad_branch = grad_resid.astype(jnp.bfloat16)
    grad_w_out = jnp.einsum("tk,td->kd", attended, grad_branch, preferred_element_type=jnp.float32)
    grad_bias_o = jnp.sum(grad_branch.astype(jnp.float32), axis=0)
    grad_ratio = jnp.einsum(
        "td,kd->tk", grad_branch, w_out, preferred_element_type=jnp.float32
    ).reshape(group, heads, depth)
    grad_numer = (grad_ratio / denom[:, :, None]).astype(jnp.bfloat16)
    grad_denom = -jnp.sum(grad_ratio * numer, axis=2) / (denom * denom)
    grad_scores = jnp.einsum(
        "the,she->hts", grad_numer, value_low, preferred_element_type=jnp.float32
    )
    grad_scores_low = ((grad_scores + grad_denom.T[:, :, None]) * keep[None]).astype(jnp.bfloat16)
    grad_query = jnp.einsum(
        "hts,shd->thd", grad_scores_low, key_low, preferred_element_type=jnp.float32
    )
    grad_key = jnp.einsum(
        "hts,thd->shd", grad_scores_low, query_low, preferred_element_type=jnp.float32
    )
    grad_value = jnp.einsum(
        "hts,the->she", scores_low, grad_numer, preferred_element_type=jnp.float32
    )
    numer_grad_wide = grad_numer.astype(jnp.float32)
    grad_query = grad_query + incoming[:, None, None] * (
        jnp.einsum("the,hde->thd", numer_grad_wide, state_in, precision=highest)
        + grad_denom[:, :, None] * total_in[None]
    )
    query_masked = query_low * incoming.astype(jnp.bfloat16)[:, None, None]
    grad_state_in = jnp.einsum(
        "thd,the->hde", query_masked, grad_numer, preferred_element_type=jnp.float32
    )
    grad_total_in = jnp.einsum(
        "thd,th->hd", query_wide * incoming[:, None, None], grad_denom, precision=highest
    )
    leaving = relay_backward(pack_state(grad_state_in, grad_total_in, passes))
    grad_state = leaving[:, :depth, :]
    grad_total = leaving[:, depth, :]
    value_wide = value_low.astype(jnp.float32)
    key_wide = key_low.astype(jnp.float32)
    grad_key = grad_key + finals[:, None, None] * (
        jnp.einsum("she,hde->shd", value_wide, grad_state, precision=highest) + grad_total[None]
    )
    grad_value = grad_value + finals[:, None, None] * jnp.einsum(
        "shd,hde->she", key_wide, grad_state, precision=highest
    )
    _, query_pull = jax.vjp(feature, query_pre)
    _, key_pull = jax.vjp(feature, key_pre)
    grad_query_low = query_pull(grad_query.reshape(group, width))[0].astype(jnp.bfloat16)
    grad_key_low = key_pull(grad_key.reshape(group, width))[0].astype(jnp.bfloat16)
    grad_value_low = grad_value.reshape(group, width).astype(jnp.bfloat16)
    grad_w_query = jnp.einsum(
        "tk,tj->kj", normed, grad_query_low, preferred_element_type=jnp.float32
    )
    grad_w_key = jnp.einsum("tk,tj->kj", normed, grad_key_low, preferred_element_type=jnp.float32)
    grad_w_value = jnp.einsum(
        "tk,tj->kj", normed, grad_value_low, preferred_element_type=jnp.float32
    )
    grad_bias_q = jnp.sum(grad_query_low.astype(jnp.float32), axis=0)
    grad_bias_k = jnp.sum(grad_key_low.astype(jnp.float32), axis=0)
    grad_bias_v = jnp.sum(grad_value_low.astype(jnp.float32), axis=0)
    grad_normed = jnp.einsum(
        "tj,kj->tk", grad_query_low, w_query, preferred_element_type=jnp.float32
    )
    grad_normed = grad_normed + jnp.einsum(
        "tj,kj->tk", grad_key_low, w_key, preferred_element_type=jnp.float32
    )
    grad_normed = grad_normed + jnp.einsum(
        "tj,kj->tk", grad_value_low, w_value, preferred_element_type=jnp.float32
    )
    _, norm_one_pull = jax.vjp(layer_norm, inputs, gain_one, bias_one)
    grad_inputs_norm, grad_gain_one, grad_bias_one = norm_one_pull(grad_normed)
    input_grad = (grad_resid + grad_inputs_norm)[None]
    grad_wide = jnp.stack([grad_w_query, grad_w_key, grad_w_value, grad_w_out])
    grad_low = jnp.concatenate(
        [grad_w_up, grad_down.reshape(blocks, width, width)], axis=0
    ).astype(jnp.bfloat16)
    grad_small = jnp.concatenate(
        [
            grad_gain_one,
            grad_bias_one,
            grad_gain_two,
            grad_bias_two,
            grad_bias_q,
            grad_bias_k,
            grad_bias_v,
            grad_bias_o,
            grad_bias_down,
            grad_bias_up,
        ]
    )
    sums, row_small = reduce_rows(
        grad_wide, grad_low, padded(grad_small.reshape(nseq, share)), nseq
    )
    row_small = row_small.reshape(2048)[:share]
    row_units, update = muon(sums, momentum, nseq)
    new_momentum = 0.5 * momentum + row_units
    update = update.astype(jnp.float32)
    rates = unit_rates(blocks)
    new_weights = weights - rates[:, None, None] * (update + 0.01 * weights)
    first_new = 0.9 * moment_one + 0.1 * row_small
    second_new = 0.95 * moment_two + 0.05 * row_small * row_small
    adjusted = first_new / (1.0 - 0.9**STEP) / (jnp.sqrt(second_new / (1.0 - 0.95**STEP)) + 1e-08)
    new_small = small_params - 0.05 * (adjusted + 0.01 * small_params)
    return (block_out, input_grad, new_weights, new_momentum, new_small, first_new, second_new)


def solution(mesh):
    in_specs = (
        P("stream", "seq", None),
        P("stream", "seq", None),
        P("stream", None),
        P("stream", None),
        P(None, "seq", None),
        P(None, "seq", None),
        P("seq"),
        P("seq"),
        P("seq"),
    )
    out_specs = (
        P("stream", "seq", None),
        P("stream", "seq", None),
        P(None, "seq", None),
        P(None, "seq", None),
        P("seq"),
        P("seq"),
        P("seq"),
    )
    return jax.shard_map(local, mesh=mesh, in_specs=in_specs, out_specs=out_specs, check_vma=False)
```

```python
import functools

import jax
import jax.numpy as jnp
from jax import lax
from jax.experimental import pallas as pl
from jax.experimental.pallas import tpu as pltpu
from jax.sharding import PartitionSpec as P

MESH = pl.DeviceIdType.MESH
DMA = pltpu.SemaphoreType.DMA
ANY = pl.BlockSpec(memory_space=pl.ANY)
VMEM = pl.BlockSpec(memory_space=pltpu.VMEM)
VMEM_LIMIT = 62 << 20


def places():
    seq = lax.axis_index("seq")
    stream = lax.axis_index("stream")
    return seq // 2, seq % 2, stream // 2, stream % 2


def device(z, x, y, c):
    return {"seq": z * 2 + x, "stream": y * 2 + c}


def greet(peers):
    barrier = pltpu.get_barrier_semaphore()
    for peer in peers:
        pl.semaphore_signal(barrier, inc=1, device_id=peer, device_id_type=MESH)
    pl.semaphore_wait(barrier, len(peers))


def remote(source, target, sent, received, peer):
    return pltpu.make_async_remote_copy(
        src_ref=source,
        dst_ref=target,
        send_sem=sent,
        recv_sem=received,
        device_id=peer,
        device_id_type=MESH,
    )


def others_along_seq(z, x, y, c, count):
    straight = [device(lax.rem(z + k, count), x, y, c) for k in range(1, count)]
    across = [device(lax.rem(z + k, count), 1 - x, y, c) for k in range(count)]
    return straight, across


CHUNK = 32


def add_into(target, left, right):
    rows = target.shape[-2]

    def body(index, carry):
        span = pl.ds(pl.multiple_of(index * CHUNK, CHUNK), CHUNK)
        total = left[span, :].astype(jnp.float32) + right[span, :].astype(jnp.float32)
        target[span, :] = total.astype(target.dtype)
        return carry

    lax.fori_loop(0, rows // CHUNK, body, 0)


def reduce_kernel(
    count, wide_ref, low_ref, small_ref, out_ref, small_out,
    core_wide, core_low, own_wide, own_low, fs_wide, fs_low, fr_wide, fr_low, kept_first,
    ss_wide, ss_low, sr_wide, sr_low, kept_second, zs_wide, zs_low, zr_wide, zr_low,
    sm_recv, sm_part, sm_pair,
    load_sem, cs, cr, fs, fr, es, er, zs, zr, ms, mr,
):
    z, x, y, c = places()
    straight, across = others_along_seq(z, x, y, c, count)
    pair = [device(z, 1 - x, y, c), device(z, x, 1 - y, c), device(z, x, y, 1 - c)]
    greet(straight + across + pair[1:])
    wide_count, low_count = wide_ref.shape[0], low_ref.shape[0]
    order = [("low", b) for b in reversed(range(low_count))] + [
        ("wide", b) for b in range(wide_count)
    ]
    steps = [(kind, b, k) for kind, b in order for k in range(count)]
    total = len(steps)
    small = []
    seqs = [lax.rem(z + k, count) * 2 + x for k in range(1, count)] + [
        lax.rem(z + k, count) * 2 + 1 - x for k in range(count)
    ]
    for k, (peer, there) in enumerate(zip(straight + across, seqs)):
        small.append(remote(small_ref.at[there], sm_recv.at[k], ms.at[k], mr.at[k], peer))
        small[-1].start()

    def at(index):
        kind, b, k = steps[index]
        there = lax.rem(z + 1 + k, count)
        source = wide_ref if kind == "wide" else low_ref
        slot = b * count + k
        return kind, b, k, there, source, slot

    loads, cores, firsts, seconds, spread = [], [], [], [], {}
    ring = 3

    def pick(kind, wide, low):
        return wide if kind == "wide" else low

    def start_core(index):
        kind, b, k, there, source, slot = at(index)
        target = pick(kind, core_wide, core_low).at[slot]
        copy = remote(source.at[b, :, 1 - c, there], target, cs.at[index], cr.at[index], pair[2])
        copy.start()
        cores.append(copy)

    def start_load(index):
        kind, b, k, there, source, slot = at(index)
        target = pick(kind, own_wide, own_low).at[index % 2]
        copy = pltpu.make_async_copy(source.at[b, :, c, there], target, load_sem.at[index])
        copy.start()
        loads.append(copy)

    for index in range(min(3, total)):
        start_core(index)
    start_load(0)
    for step in range(total + 3):
        index = step
        if index < total:
            kind, b, k, there, source, slot = at(index)
            if index + 1 < total:
                start_load(index + 1)
            if index + 3 < total:
                start_core(index + 3)
            loads[index].wait()
            cores[index].wait_recv()
            own = pick(kind, own_wide, own_low).at[index % 2]
            got = pick(kind, core_wide, core_low).at[slot]
            if index >= ring:
                firsts[index - ring].wait_send()
            out = pick(kind, fs_wide, fs_low).at[index % ring]
            kept = kept_first.at[index % ring]
            for j in range(2):
                if k % 2 == 0:
                    add_into(out.at[j], own.at[1 - y, j], got.at[1 - y, j])
                    add_into(kept.at[j], own.at[y, j], got.at[y, j])
                else:
                    add_into(out.at[j], own.at[j, 1 - x], got.at[j, 1 - x])
                    add_into(kept.at[j], own.at[j, x], got.at[j, x])
            target = pick(kind, fr_wide, fr_low).at[slot]
            copy = remote(out, target, fs.at[index], fr.at[index], pair[1 - k % 2])
            copy.start()
            firsts.append(copy)
        index = step - 1
        if 0 <= index < total:
            kind, b, k, there, source, slot = at(index)
            firsts[index].wait_recv()
            kept = kept_first.at[index % ring]
            got = pick(kind, fr_wide, fr_low).at[slot]
            if index >= ring:
                seconds[index - ring].wait_send()
            out = pick(kind, ss_wide, ss_low).at[index % ring]
            mine = x if k % 2 == 0 else y
            add_into(out, kept.at[1 - mine], got.at[1 - mine])
            add_into(kept_second.at[index % ring], kept.at[mine], got.at[mine])
            target = pick(kind, sr_wide, sr_low).at[slot]
            copy = remote(out, target, es.at[index], er.at[index], pair[k % 2])
            copy.start()
            seconds.append(copy)
        index = step - 2
        if 0 <= index < total:
            kind, b, k, there, source, slot = at(index)
            seconds[index].wait_recv()
            got = pick(kind, sr_wide, sr_low).at[slot]
            batch = b if kind == "wide" else wide_count + b
            if k < count - 1:
                out = pick(kind, zs_wide, zs_low).at[b, k]
                add_into(out, kept_second.at[index % ring], got)
                target = pick(kind, zr_wide, zr_low).at[b, k]
                spread[index] = remote(out, target, zs.at[batch, k], zr.at[batch, k], straight[k])
                spread[index].start()
            else:
                add_into(out_ref.at[batch], kept_second.at[index % ring], got)
        index = step - 3
        if 0 <= index < total:
            kind, b, k, there, source, slot = at(index)
            if k == count - 1:
                batch = b if kind == "wide" else wide_count + b
                for j in range(count - 1):
                    spread[index - (count - 1) + j].wait_recv()
                    add_into(out_ref.at[batch], out_ref.at[batch], pick(kind, zr_wide, zr_low).at[b, j])
    part = small_ref[z * 2 + x]
    for k, copy in enumerate(small):
        copy.wait_recv()
        part = part + sm_recv[k]
    sm_part[0] = part
    tail = []
    for j in range(2):
        copy = remote(sm_part.at[j], sm_pair.at[j], ms.at[len(small) + j], mr.at[len(small) + j], pair[1 + j])
        copy.start()
        copy.wait_recv()
        tail.append(copy)
        if j == 0:
            sm_part[1] = sm_part[0] + sm_pair[0]
        else:
            small_out[...] = sm_part[1] + sm_pair[1]
    for copy in small + tail + cores + firsts[-ring:] + seconds[-ring:] + list(spread.values()):
        copy.wait_send()


def reduce_rows(wide, low, small, nseq):
    count = nseq // 2
    wide_count, low_count = wide.shape[0] // 4, low.shape[0] // 4
    width = wide.shape[-1]
    rows = wide.shape[1] // nseq
    batches = wide_count + low_count
    steps = batches * count
    wide = wide.reshape(wide_count, 2, 2, count, 2, rows, width)
    low = low.reshape(low_count, 2, 2, count, 2, rows, width)
    f32, bf16 = jnp.float32, jnp.bfloat16
    V = pltpu.VMEM
    nw, nl = wide_count * count, low_count * count
    return pl.pallas_call(
        functools.partial(reduce_kernel, count),
        out_shape=(
            jax.ShapeDtypeStruct((batches, rows, width), f32),
            jax.ShapeDtypeStruct(small.shape[1:], f32),
        ),
        in_specs=[ANY, ANY, VMEM],
        out_specs=[VMEM, VMEM],
        scratch_shapes=[
            V((nw, 2, 2, rows, width), f32),
            V((nl, 2, 2, rows, width), bf16),
            V((2, 2, 2, rows, width), f32),
            V((2, 2, 2, rows, width), bf16),
            V((3, 2, rows, width), f32),
            V((3, 2, rows, width), bf16),
            V((nw, 2, rows, width), f32),
            V((nl, 2, rows, width), bf16),
            V((3, 2, rows, width), f32),
            V((3, rows, width), f32),
            V((3, rows, width), bf16),
            V((nw, rows, width), f32),
            V((nl, rows, width), bf16),
            V((3, rows, width), f32),
            V((wide_count, count - 1, rows, width), f32),
            V((low_count, count - 1, rows, width), bf16),
            V((wide_count, count - 1, rows, width), f32),
            V((low_count, count - 1, rows, width), bf16),
            V((nseq - 1,) + small.shape[1:], f32),
            V((2,) + small.shape[1:], f32),
            V((2,) + small.shape[1:], f32),
            DMA((steps,)),
            DMA((steps,)),
            DMA((steps,)),
            DMA((steps,)),
            DMA((steps,)),
            DMA((steps,)),
            DMA((steps,)),
            DMA((batches, count - 1)),
            DMA((batches, count - 1)),
            DMA((nseq + 1,)),
            DMA((nseq + 1,)),
        ],
        compiler_params=pltpu.CompilerParams(
            collective_id=1, has_side_effects=True, vmem_limit_bytes=VMEM_LIMIT
        ),
    )(wide, low, small)


SHIFTS = (0.0, 0.0, 0.1, 0.7, 0.7)
FINE = (False, False, False, True, True)
BAND = 256


def split_two(values):
    high = values.astype(jnp.bfloat16)
    return high, (values - high.astype(jnp.float32)).astype(jnp.bfloat16)


def dot(left, right, transposed=False):
    dims = (((1,), (1 if transposed else 0,)), ((), ()))
    return lax.dot_general(left, right, dims, preferred_element_type=jnp.float32)


def orthogonalize(full, xh, xl, gram, gram_low):
    size = full.shape[0]
    bands = size // BAND

    def span(index):
        return pl.ds(pl.multiple_of(index * BAND, BAND), BAND)

    def square(index, total):
        part = full[span(index), :]
        return total + jnp.sum(part * part)

    norm = jnp.sqrt(lax.fori_loop(0, bands, square, jnp.float32(0.0)))
    scale = 1.0 / (norm + 1e-07)

    def begin(index, carry):
        part = full[span(index), :] * scale
        full[span(index), :] = part
        xh[0, span(index), :] = part.astype(jnp.bfloat16)
        return carry

    lax.fori_loop(0, bands, begin, 0)
    for turn in range(len(SHIFTS)):
        shift, fine = SHIFTS[turn], FINE[turn]
        now, later = turn % 2, 1 - turn % 2
        more = turn + 1 < len(SHIFTS) and FINE[turn + 1]

        def form(index, carry):
            rows = span(index)
            left = xh[now, rows, :]
            block = dot(left, xh[now], True)
            if fine:
                block += dot(left, xl[now], True) + dot(xl[now, rows, :], xh[now], True)
            if shift:
                across = lax.broadcasted_iota(jnp.int32, block.shape, 1)
                down = lax.broadcasted_iota(jnp.int32, block.shape, 0) + index * BAND
                block = jnp.where(across == down, block - shift, block)
            gram[rows, :] = block
            gram_low[rows, :] = block.astype(jnp.bfloat16)
            return carry

        lax.fori_loop(0, bands, form, 0)
        linear = -4.775 + 2.0 * 2.0315 * shift
        scaled = 3.4445 - 4.775 * shift + 2.0315 * shift * shift

        def advance(index, carry):
            rows = span(index)
            poly = linear * gram[rows, :] + 2.0315 * dot(gram_low[rows, :], gram_low[...])
            if fine:
                high, low = split_two(poly)
                step = dot(high, xh[now]) + dot(high, xl[now]) + dot(low, xh[now])
            else:
                step = dot(poly.astype(jnp.bfloat16), xh[now])
            moved = scaled * full[rows, :] + step
            full[rows, :] = moved
            if more:
                high, low = split_two(moved)
                xh[later, rows, :] = high
                xl[later, rows, :] = low
            else:
                xh[later, rows, :] = moved.astype(jnp.bfloat16)
            return carry

        lax.fori_loop(0, bands, advance, 0)
    return len(SHIFTS) % 2


def muon_kernel(
    count, g_ref, mom_ref, all_ref, rows_ref,
    mom_own, moved, full, xh, xl, gram, gram_low,
    load_sem, own_sem, ms, mr, ys, yr, os_, or_, fs, fr, gs, gr,
):
    z, x, y, c = places()
    seq = z * 2 + x
    nseq = count * 2
    batches, rows, width = g_ref.shape
    straight, across = others_along_seq(z, x, y, c, count)
    pair = [device(z, x, 1 - y, c), device(z, x, y, 1 - c)]
    greet(straight + across + pair)
    load = pltpu.make_async_copy(mom_ref.at[:, y, c], mom_own, load_sem)
    load.start()
    keep = pltpu.make_async_copy(g_ref, all_ref.at[:, y, c], own_sem.at[0])
    keep.start()
    load.wait()
    owner = [2 * b + c + 1 for b in range(batches)]

    def block(where):
        return full.at[pl.ds(pl.multiple_of(where * rows, rows), rows)]

    for b in range(batches):
        for j in range(rows // CHUNK):
            span = slice(j * CHUNK, (j + 1) * CHUNK)
            moved[b, span, :] = 0.5 * mom_own[b, span, :] + g_ref[b, span, :]

        @pl.when(seq != owner[b])
        def _():
            remote(
                moved.at[b], block(seq), ms.at[b], mr.at[seq],
                {"seq": owner[b], "stream": y * 2 + c},
            ).start()

        @pl.when(seq == owner[b])
        def _():
            pltpu.make_async_copy(moved.at[b], block(seq), own_sem.at[1]).start()

    over = remote(g_ref, all_ref.at[:, y, c], ys.at[0], yr.at[0], pair[0])
    over.start()
    is_owner = (seq == owner[0]) | (seq == owner[1]) | (seq == owner[2])

    @pl.when(is_owner)
    def _():
        pltpu.make_async_copy(moved.at[0], block(seq), own_sem.at[1]).wait()
        for k in range(1, nseq):
            there = lax.rem(seq + k, nseq)
            remote(moved.at[0], block(there), ms.at[0], mr.at[there], pair[0]).wait_recv()
        orthogonalize(full, xh, xl, gram, gram_low)

    final = len(SHIFTS) % 2

    def result(where):
        return xh.at[final, pl.ds(pl.multiple_of(where * rows, rows), rows)]

    for b in range(batches):
        target = rows_ref.at[b, y, c]

        @pl.when(seq == owner[b])
        def _():
            pltpu.make_async_copy(result(seq), target, own_sem.at[2]).start()
            for k in range(1, nseq):
                there = lax.rem(seq + k, nseq)
                remote(
                    result(there), target, os_.at[k - 1], or_.at[b],
                    {"seq": there, "stream": y * 2 + c},
                ).start()

    keep.wait()
    over.wait_recv()
    share = remote(all_ref.at[:, :, c], all_ref.at[:, :, c], ys.at[1], yr.at[1], pair[1])
    share.start()
    hops = []
    for b in range(batches):
        target = rows_ref.at[b, y, c]

        @pl.when(seq == owner[b])
        def _():
            pltpu.make_async_copy(result(seq), target, own_sem.at[2]).wait()

        @pl.when(seq != owner[b])
        def _():
            remote(result(seq), target, os_.at[0], or_.at[b], pair[0]).wait_recv()

        hop = remote(target, target, fs.at[b], fr.at[b], pair[0])
        hop.start()
        hops.append(hop)
    lasts = []
    for b in range(batches):
        hops[b].wait_recv()
        target = rows_ref.at[b, :, c]
        last = remote(target, target, gs.at[b], gr.at[b], pair[1])
        last.start()
        lasts.append(last)
    for last in lasts:
        last.wait_recv()
    share.wait_recv()
    for copy in [over, share] + hops + lasts:
        copy.wait_send()
    for b in range(batches):

        @pl.when(seq != owner[b])
        def _():
            remote(moved.at[b], block(seq), ms.at[b], mr.at[seq], pair[0]).wait_send()

        @pl.when(seq == owner[b])
        def _():
            for k in range(1, nseq):
                there = lax.rem(seq + k, nseq)
                remote(result(there), rows_ref.at[b, y, c], os_.at[k - 1], or_.at[b], pair[0]).wait_send()


def muon(sums, momentum, nseq):
    count = nseq // 2
    batches, rows, width = sums.shape
    units = momentum.shape[0]
    f32, bf16 = jnp.float32, jnp.bfloat16
    V = pltpu.VMEM
    whole, ortho = pl.pallas_call(
        functools.partial(muon_kernel, count),
        out_shape=(
            jax.ShapeDtypeStruct((batches, 2, 2, rows, width), f32),
            jax.ShapeDtypeStruct((batches, 2, 2, rows, width), bf16),
        ),
        in_specs=[VMEM, ANY],
        out_specs=[ANY, ANY],
        scratch_shapes=[
            V((batches, rows, width), f32),
            V((batches, rows, width), f32),
            V((width, width), f32),
            V((2, width, width), bf16),
            V((2, width, width), bf16),
            V((width, width), f32),
            V((width, width), bf16),
            DMA,
            DMA((3,)),
            DMA((batches,)),
            DMA((nseq,)),
            DMA((2,)),
            DMA((2,)),
            DMA((nseq - 1,)),
            DMA((batches,)),
            DMA((batches,)),
            DMA((batches,)),
            DMA((batches,)),
            DMA((batches,)),
        ],
        compiler_params=pltpu.CompilerParams(
            collective_id=2, has_side_effects=True, vmem_limit_bytes=VMEM_LIMIT
        ),
    )(sums, momentum.reshape(batches, 2, 2, rows, width))
    return whole.reshape(units, rows, width), ortho.reshape(units, rows, width)


HALF = 64
PAIR = 128


def matrix(w_ref, batch, index):
    block = w_ref[batch, index // 2, index % 2]
    return block.reshape(block.shape[0] * block.shape[1] * block.shape[2], block.shape[3])


def norm_rows(values, gain, offset):
    center = values - jnp.mean(values, axis=-1, keepdims=True)
    spread = jnp.mean(center * center, axis=-1, keepdims=True)
    return center * lax.rsqrt(spread + 1e-05) * gain + offset


def lanes_of(head):
    lane = lax.broadcasted_iota(jnp.int32, (1, PAIR), 1)
    return (lane // HALF) == head


def block_diagonal():
    row = lax.broadcasted_iota(jnp.int32, (PAIR, PAIR), 0)
    lane = lax.broadcasted_iota(jnp.int32, (PAIR, PAIR), 1)
    return (row // HALF) == (lane // HALF)


def pair_span(index):
    return pl.ds(pl.multiple_of(index * PAIR, PAIR), PAIR)


def band_span(index):
    return pl.ds(pl.multiple_of(index * BAND, BAND), BAND)


def dot_down(left, right):
    return lax.dot_general(left, right, (((0,), (0,)), ((), ())), preferred_element_type=jnp.float32)


def pack_message(left_ref, right_ref, scale_ref, row_ref, message):
    diagonal = block_diagonal()
    for j in range(4):
        parts = []
        for p in (2 * j, 2 * j + 1):
            lanes = slice(p * PAIR, (p + 1) * PAIR)
            scale = scale_ref[...]
            left = (left_ref[:, lanes].astype(jnp.float32) * scale).astype(jnp.bfloat16)
            parts.append(dot_down(left, right_ref[:, lanes]))
            if row_ref is None:
                total = jnp.sum(left.astype(jnp.float32), axis=0, keepdims=True)
            else:
                total = jnp.sum(left.astype(jnp.float32) * row_ref[:, lanes], axis=0, keepdims=True)
            for half in range(2):
                message[half, 256 + p : 257 + p, :] = total
        block = jnp.where(diagonal, parts[0], pltpu.roll(parts[1], HALF, 1))
        message[j // 2, (j % 2) * PAIR : (j % 2 + 1) * PAIR, :] = block


def unpack_message(message, p):
    diagonal = block_diagonal()
    j = p // 2
    block = message[j // 2, (j % 2) * PAIR : (j % 2 + 1) * PAIR, :]
    if p % 2:
        block = pltpu.roll(block, HALF, 1)
    block = jnp.where(diagonal, block, 0.0)
    row = message[0, 256 + p : 257 + p, :]
    column = jnp.transpose(jnp.broadcast_to(row, (PAIR, PAIR)))
    return block, jnp.where(diagonal, column, 0.0)


class Relay:
    def __init__(self, count, coef, own, across, part, spread, total, result, sems, places_):
        self.count, self.coef, self.own, self.across = count, coef, own, across
        self.part, self.spread, self.total, self.result = part, spread, total, result
        self.send, self.recv = sems
        self.z, self.x, self.y, self.c = places_
        self.pair = device(self.z, 1 - self.x, self.y, self.c)

    def swap(self):
        self.first = remote(self.own, self.across, self.send.at[0], self.recv.at[0], self.pair)
        self.first.start()

    def spread_out(self):
        self.first.wait_recv()
        self.part[...] = self.coef[0] * self.own[self.x] + self.coef[1] * self.across[self.x]
        self.copies = []
        for k in range(1, self.count):
            peer = device(lax.rem(self.z + k, self.count), self.x, self.y, self.c)
            copy = remote(self.part, self.spread.at[k - 1], self.send.at[k], self.recv.at[k], peer)
            copy.start()
            self.copies.append(copy)

    def join(self):
        total = jnp.zeros_like(self.part)
        for k, copy in enumerate(self.copies):
            copy.wait_recv()
            total = total + self.coef[4 + k] * self.spread[k]
        self.total[self.x] = total
        half = self.total.at[self.x]
        self.last = remote(half, half, self.send.at[self.count], self.recv.at[self.count], self.pair)
        self.last.start()

    def finish(self):
        self.last.wait_recv()
        for half in range(2):
            self.result[half] = self.coef[2] * self.total[half] + self.coef[3] * self.across[half]

    def wait_sends(self):
        for copy in [self.first, self.last] + self.copies:
            copy.wait_send()


def head_scores(q_ref, k_ref, keep_ref, lanes, head, band):
    rows = slice(band * BAND, (band + 1) * BAND)
    upto = slice(0, (band + 1) * BAND)
    query = jnp.where(lanes_of(head), q_ref[rows, lanes], 0)
    return dot(query, k_ref[upto, lanes], True) * keep_ref[rows, upto]


def attend_pair(p, q_ref, k_ref, v_ref, keep_ref, num_ref, den_ref):
    lanes = pair_span(p)
    group = q_ref.shape[0]
    value = v_ref[:, lanes]
    first = lanes_of(0)
    for band in range(group // BAND):
        rows = slice(band * BAND, (band + 1) * BAND)
        sums, totals = [], []
        for head in range(2):
            scores = head_scores(q_ref, k_ref, keep_ref, lanes, head, band)
            totals.append(jnp.sum(scores, axis=1, keepdims=True))
            sums.append(dot(scores.astype(jnp.bfloat16), value[: (band + 1) * BAND]))
        num_ref[rows, lanes] = jnp.where(first, sums[0], sums[1])
        den_ref[rows, lanes] = jnp.where(first, totals[0], totals[1])


def image_ends(lengths_ref, order_ref):
    images = lengths_ref.shape[1]
    ends, running = [], jnp.int32(0)
    for j in range(images):
        for i in range(images):
            running = running + jnp.where(order_ref[0, j] == i, lengths_ref[0, i], 0)
        ends.append(running)
    return ends


def segment_at(ends, positions):
    found = jnp.zeros_like(positions)
    for end in ends:
        found = found + jnp.where(positions >= end, 1, 0)
    return found


def same(left, right):
    return jnp.where(left == right, 1.0, 0.0)


def fill_masks(ends, start, group, keep_ref, flags_ref):
    for band in range(group // BAND):
        rows = slice(band * BAND, (band + 1) * BAND)
        down = lax.broadcasted_iota(jnp.int32, (BAND, group), 0) + band * BAND
        along = lax.broadcasted_iota(jnp.int32, (BAND, group), 1)
        mine = segment_at(ends, down + start)
        theirs = segment_at(ends, along + start)
        keep_ref[rows, :] = jnp.where(along <= down, same(mine, theirs), 0.0)
        narrow = mine[:, :PAIR]
        flags_ref[0, rows, :] = same(narrow, segment_at(ends, start - 1))
        flags_ref[1, rows, :] = same(narrow, segment_at(ends, start + group - 1))


def pass_at(ends, block, group):
    return same(segment_at(ends, block * group + group - 1), segment_at(ends, block * group - 1))


def forward_factors(ends, group, count, z, x):
    both = [pass_at(ends, 2 * z, group), pass_at(ends, 2 * z + 1, group)]
    near = [jnp.where(x == 0, both[1], 1.0), jnp.where(x == 0, 1.0, both[1])]
    near += [jnp.where(x == 0, 1.0, both[0]), jnp.where(x == 0, 0.0, 1.0)]
    running, far = jnp.float32(1.0), []
    for k in range(1, count):
        far.append(jnp.where(z - k >= 0, running, 0.0))
        there = jnp.maximum(z - k, 0)
        running = running * pass_at(ends, 2 * there, group) * pass_at(ends, 2 * there + 1, group)
    return near + far


def backward_factors(ends, group, count, z, x):
    both = [pass_at(ends, 2 * z, group), pass_at(ends, 2 * z + 1, group)]
    near = [jnp.where(x == 0, 1.0, both[0]), jnp.where(x == 0, both[0], 1.0)]
    near += [jnp.where(x == 0, both[1], 1.0), jnp.where(x == 0, 1.0, 0.0)]
    running, ahead = jnp.float32(1.0), []
    for k in range(1, count):
        ahead.append(jnp.where(z + k < count, running, 0.0))
        there = jnp.minimum(z + k, count - 1)
        running = running * pass_at(ends, 2 * there, group) * pass_at(ends, 2 * there + 1, group)
    return near + ahead[::-1]


def forward_kernel(
    count, aligned, x_ref, w_ref, small_ref, lengths_ref, order_ref,
    w_out, out_ref, rows_ref, low_ref, pre_ref, ratio_ref, left_ref, resid_ref, up_ref, act_ref, state_ref,
    w_all, stage, small_in, keep, flags, h1, q, k, v, num, den, o, resid, h2, act, turned, act_turned, message, across, part, spread, total_ref, state,
    load_sem, out_sem, zs, zr, ps, pr, ss, sr, rs, rr,
):
    z, x, y, c = places()
    straight, far = others_along_seq(z, x, y, c, count)
    pair = [device(z, 1 - x, y, c), device(z, x, 1 - y, c), device(z, x, y, 1 - c)]
    batches = w_ref.shape[0]
    rows, width = w_ref.shape[3:]
    group = x_ref.shape[0]
    bands = group // BAND
    loads = []
    for b in range(batches):
        for i in range(4):
            copy = pltpu.make_async_copy(
                w_ref.at[b, i // 2, i % 2],
                stage.at[b, pl.ds(i * rows, rows)],
                load_sem.at[b, i],
            )
            copy.start()
            loads.append(copy)
    greet(straight + far + pair[1:])
    small = []
    if aligned:
        for j, peer in enumerate(straight + far):
            small.append(remote(small_ref, small_in.at[z * 2 + x], ss.at[j], sr.at[j], peer))
            small[-1].start()
        small_in[z * 2 + x] = small_ref[...]
    spread_w = {}

    def cast_own(b):
        for i in range(4):
            loads[b * 4 + i].wait()
            for j in range(rows // CHUNK):
                span = slice(j * CHUNK, (j + 1) * CHUNK)
                at = slice(i * rows + j * CHUNK, i * rows + (j + 1) * CHUNK)
                w_all[b, i // 2, i % 2, z, x, span, :] = stage[b, at, :].astype(jnp.bfloat16)

    def send_own(b):
        for j in range(1, count):
            block = w_all.at[b, y, c, z, x]
            spread_w[b, j] = remote(block, block, zs.at[b, j - 1], zr.at[b, j - 1], straight[j - 1])
            spread_w[b, j].start()

    first, second, third, outs, waited = [], [], [], [], []
    plan = [(b, 0) for b in range(batches)]
    plan += [(b, j) for b in range(batches) for j in range(1, count)]
    total = len(plan)

    def send(kept, phase, index, block, peer):
        kept.append(remote(block, block, ps.at[phase, index], pr.at[phase, index], peer))
        kept[-1].start()

    def put_out(source, target):
        copy = pltpu.make_async_copy(source, target, out_sem.at[len(outs)])
        copy.start()
        outs.append(copy)
        return copy

    def tick(step):
        index = step
        if index < total:
            b, j = plan[index]
            there = lax.rem(z - j + count, count)
            if j:
                spread_w[b, j].wait_recv()
            send(first, 0, index, w_all.at[b, y, c, there, x], pair[(j + b) % 2 if j else 0])
            if j == min(1, count - 1) and b + 1 < batches:
                send_own(b + 1)
        index = step - 1
        if 0 <= index < total:
            b, j = plan[index]
            there = lax.rem(z - j + count, count)
            first[index].wait_recv()
            if j == 0:
                send(second, 1, index, w_all.at[b, y, c, z, 1 - x], pair[1])
            elif (j + b) % 2 == 0:
                send(second, 1, index, w_all.at[b, y, c, there], pair[1])
            else:
                send(second, 1, index, w_all.at[b, :, c, there, x], pair[0])
        index = step - 2
        if 0 <= index < total:
            b, j = plan[index]
            there = lax.rem(z - j + count, count)
            second[index].wait_recv()
            block = w_all.at[b, :, c, z, 1 - x] if j == 0 else w_all.at[b, :, c, there]
            send(third, 2, index, block, pair[2])
        index = step - 3
        if 0 <= index < total:
            b, j = plan[index]
            there = lax.rem(z - j + count, count)
            third[index].wait_recv()
            put_out(w_all.at[b, :, :, there], w_out.at[b, :, :, there])

    cast_own(0)
    send_own(0)
    tick(0)
    for b in range(1, batches):
        cast_own(b)
        tick(b)
    if aligned:
        for copy in small:
            copy.wait_recv()
        share_rows = 13 * 1024 // 128 // (count * 2)
        for j in range(13 * 8):
            rows_ref[j // 8 : j // 8 + 1, (j % 8) * 128 : (j % 8 + 1) * 128] = small_in[
                j // share_rows, j % share_rows : j % share_rows + 1, :
            ]
    else:
        rows_ref[0:13, :] = small_ref[...]

    def vector(index):
        return rows_ref[index : index + 1, :]

    def norm_one(i, carry):
        span = band_span(i)
        value = norm_rows(x_ref[span, :].astype(jnp.float32), vector(0), vector(1))
        h1[span, :] = value.astype(jnp.bfloat16)
        turned[0, :, span] = jnp.transpose(value).astype(jnp.bfloat16)
        return carry

    lax.fori_loop(0, bands, norm_one, 0)
    ends = image_ends(lengths_ref, order_ref)
    fill_masks(ends, (z * 2 + x) * group, group, keep, flags)
    factors = forward_factors(ends, group, count, z, x)
    ready = batches + count - 1 + 3
    for step in range(batches, ready):
        tick(step)

    def project(i, carry):
        span = band_span(i)
        left = h1[span, :]
        for index, low in ((0, q), (1, k)):
            pre = dot(left, matrix(w_all, 0, index)) + vector(4 + index)
            stage[index, span, :] = pre
            low[span, :] = jnp.where(pre > 0, pre + 1.0, jnp.exp(jnp.minimum(pre, 0.0))).astype(jnp.bfloat16)
        v[span, :] = (dot(left, matrix(w_all, 0, 2)) + vector(6)).astype(jnp.bfloat16)
        return carry

    lax.fori_loop(0, bands, project, 0)
    pack_message(k, v, flags.at[1], None, message)
    relay = Relay(count, factors, message, across, part, spread, total_ref, state, (rs, rr), (z, x, y, c))
    relay.swap()
    stored = [put_out(stage.at[0], pre_ref.at[0]), put_out(stage.at[1], pre_ref.at[1]), None]
    for index, low in enumerate((q, k, v)):
        put_out(low, low_ref.at[index])

    def attend(p, carry):
        attend_pair(p, q, k, v, keep, num, den)
        return carry

    pairs = width // PAIR
    step = ready
    lax.fori_loop(0, pairs // 4, attend, 0)
    tick(step)
    relay.spread_out()
    lax.fori_loop(pairs // 4, pairs // 2, attend, 0)
    tick(step + 1)
    lax.fori_loop(pairs // 2, pairs, attend, 0)
    relay.join()
    tick(step + 2)
    relay.finish()
    put_out(state, state_ref)
    for p in range(pairs):
        block, column = unpack_message(state, p)
        high, low = split_two(jnp.concatenate([block, column], axis=1))
        lanes = slice(p * PAIR, (p + 1) * PAIR)
        for i in range(bands):
            span = slice(i * BAND, (i + 1) * BAND)
            query = q[span, lanes]
            both = dot(query, high) + dot(query, low)
            flag = flags[0, span, :]
            top = num[span, lanes] + flag * both[:, :PAIR]
            bottom = den[span, lanes] + flag * both[:, PAIR:]
            num[span, lanes] = top
            den[span, lanes] = bottom
            o[span, lanes] = (top / bottom).astype(jnp.bfloat16)
    put_out(num, ratio_ref.at[0])
    put_out(den, ratio_ref.at[1])

    def close(i, carry):
        span = band_span(i)
        value = x_ref[span, :].astype(jnp.float32) + dot(o[span, :], matrix(w_all, 0, 3)) + vector(7)
        resid[span, :] = value
        hidden = norm_rows(value, vector(2), vector(3))
        h2[span, :] = hidden.astype(jnp.bfloat16)
        turned[2, :, span] = jnp.transpose(hidden).astype(jnp.bfloat16)
        turned[1, :, span] = jnp.transpose(o[span, :].astype(jnp.float32)).astype(jnp.bfloat16)
        return carry

    lax.fori_loop(0, bands, close, 0)
    put_out(turned, left_ref)
    put_out(resid, resid_ref)
    step = step + 3
    ready = batches + 2 * (count - 1) + 3
    while step < ready:
        tick(step)
        step += 1
    blocks = act.shape[0]
    turned_out = []
    for j in range(blocks):
        if j > 1:
            turned_out[j - 2].wait()
            waited.append(turned_out[j - 2])
        if stored[j % 3] is not None:
            stored[j % 3].wait()
            waited.append(stored[j % 3])

        def expand(i, carry):
            span = band_span(i)
            pre = dot(h2[span, :], matrix(w_all, 1, j)) + vector(9 + j)
            stage[j % 3, span, :] = pre
            value = jax.nn.gelu(pre)
            act[j, span, :] = value.astype(jnp.bfloat16)
            act_turned[j % 2, :, span] = jnp.transpose(value).astype(jnp.bfloat16)
            return carry

        lax.fori_loop(0, bands, expand, 0)
        stored[j % 3] = put_out(stage.at[j % 3], up_ref.at[j])
        turned_out.append(put_out(act_turned.at[j % 2], act_ref.at[j]))
        if step < total + 3:
            tick(step)
            step += 1
    while step < total + 3:
        tick(step)
        step += 1

    def project_down(i, carry):
        span = band_span(i)
        value = resid[span, :] + vector(8)
        for j in range(blocks):
            value += dot(act[j, span, :], matrix(w_all, 2, j))
        out_ref[span, :] = value.astype(jnp.bfloat16)
        return carry

    lax.fori_loop(0, bands, project_down, 0)
    for copy in outs:
        if not any(copy is other for other in waited):
            copy.wait()
    for copy in list(spread_w.values()) + first + second + third + small:
        copy.wait_send()
    relay.wait_sends()


def forward(x, weights, small, lengths, order, nseq, aligned):
    group, width = x.shape
    units, rows, _ = weights.shape
    count, batches = nseq // 2, units // 4
    steps = batches * count
    f32, bf16 = jnp.float32, jnp.bfloat16
    V, S = pltpu.VMEM, jax.ShapeDtypeStruct
    blocks = 4
    smem = pl.BlockSpec(memory_space=pltpu.SMEM)
    message = (2, 264, PAIR)
    return pl.pallas_call(
        functools.partial(forward_kernel, count, aligned),
        out_shape=(
            S((batches, 2, 2, count, 2, rows, width), bf16),
            S((group, width), bf16),
            S((16, width), f32),
            S((3, group, width), bf16),
            S((2, group, width), f32),
            S((2, group, width), f32),
            S((3, width, group), bf16),
            S((group, width), f32),
            S((blocks, group, width), f32),
            S((blocks, width, group), bf16),
            S(message, f32),
        ),
        in_specs=[VMEM, ANY, VMEM, smem, smem],
        out_specs=[ANY, VMEM, VMEM] + [ANY] * 8,
        scratch_shapes=[
            V((batches, 2, 2, count, 2, rows, width), bf16),
            V((3, group, width), f32),
            V(((nseq,) if aligned else ()) + small.shape, f32),
            V((group, group), f32),
            V((2, group, PAIR), f32),
            V((group, width), bf16),
            V((group, width), bf16),
            V((group, width), bf16),
            V((group, width), bf16),
            V((group, width), f32),
            V((group, width), f32),
            V((group, width), bf16),
            V((group, width), f32),
            V((group, width), bf16),
            V((blocks, group, width), bf16),
            V((3, width, group), bf16),
            V((2, width, group), bf16),
            V(message, f32),
            V(message, f32),
            V(message[1:], f32),
            V((count - 1,) + message[1:], f32),
            V(message, f32),
            V(message, f32),
            DMA((batches, 4)),
            DMA((steps + 20,)),
            DMA((batches, count - 1)),
            DMA((batches, count - 1)),
            DMA((3, steps)),
            DMA((3, steps)),
            DMA((nseq - 1,)),
            DMA((nseq - 1,)),
            DMA((count + 1,)),
            DMA((count + 1,)),
        ],
        compiler_params=pltpu.CompilerParams(
            collective_id=0, has_side_effects=True, vmem_limit_bytes=VMEM_LIMIT
        ),
    )(x, weights.reshape(batches, 2, 2, rows, width), small, lengths, order)


D = 1024
HEADS = 16
HEAD_DIM = 64
FF = 4096
STEP = 10


highest = lax.Precision.HIGHEST


def passed_along(array, axis, by):
    count = lax.axis_size(axis)
    pairs = [(i, i + by) for i in range(count) if 0 <= i + by < count]
    return lax.ppermute(array, axis, pairs)


def layer_norm(values, gain, offset):
    center = values - jnp.mean(values, axis=-1, keepdims=True)
    spread = jnp.mean(center * center, axis=-1, keepdims=True)
    return center * lax.rsqrt(spread + 1e-05) * gain + offset


def feature(values):
    return jax.nn.elu(values) + 1.0


def segment_of(lengths_row, order_row, positions):
    places = jnp.arange(lengths_row.shape[0], dtype=jnp.int32)
    packed = jnp.sum(
        jnp.where(order_row[:, None] == places[None, :], lengths_row[None, :], 0), axis=1
    )
    ends = jnp.cumsum(packed)
    return jnp.sum((positions[:, None] >= ends[None, :]).astype(jnp.int32), axis=1)


def split_small(vector, width):
    pieces = [vector[index * width : (index + 1) * width] for index in range(9)]
    return pieces + [vector[9 * width :]]


def unit_rates(blocks):
    return jnp.array([0.5, 0.5, 0.5, 4.0] + [0.5] * blocks + [0.25] * blocks, dtype=jnp.float32)


def pack_state(matrix, totals, passes):
    flags = jnp.zeros_like(totals[:, None, :]) + passes
    return jnp.concatenate([matrix, totals[:, None, :], flags], axis=1)


def combine_states(earlier, later):
    scale = later[:, -1:, :]
    head_rows = later[:, :-1, :] + scale * earlier[:, :-1, :]
    return jnp.concatenate([head_rows, earlier[:, -1:, :] * scale], axis=1)


def relay_forward(own):

    def forward_turn(turn, running):
        return passed_along(combine_states(running, own), "seq", 1)

    arriving = lax.fori_loop(0, lax.axis_size("seq") - 1, forward_turn, jnp.zeros_like(own))
    return arriving


def relay_backward(own):

    def backward_turn(turn, running):
        return passed_along(combine_states(running, own).astype(jnp.bfloat16), "seq", -1).astype(
            jnp.float32
        )

    leaving = lax.fori_loop(0, lax.axis_size("seq") - 1, backward_turn, jnp.zeros_like(own))
    return leaving


def padded(vector):
    short = 2048 - vector.shape[-1]
    edges = [(0, 0)] * (vector.ndim - 1) + [(0, short)]
    return jnp.pad(vector, edges).reshape(vector.shape[:-1] + (16, 128))


def local(
    tokens, cotangent, lengths, order, weights, momentum, small_params, moment_one, moment_two
):
    group = tokens.shape[1]
    width = tokens.shape[2]
    heads = HEADS
    depth = HEAD_DIM
    blocks = FF // D
    units = weights.shape[0]
    nseq = lax.axis_size("seq")
    share = small_params.shape[0]
    rounded = lax.reduce_precision(small_params, 8, 7)
    aligned = share % 128 == 0
    if aligned:
        shared = padded(rounded)
    else:
        shared = lax.all_gather(rounded, "seq", axis=0, tiled=True).reshape(-1, width)
    (gathered, block_out, rows, low, pre, ratio, left, resid, up, act, state) = forward(
        tokens[0], weights, shared, lengths, order, nseq, aligned
    )
    block_out = block_out[None]
    gathered = gathered.reshape(units, width, width)
    w_query, w_key, w_value, w_out = gathered[0], gathered[1], gathered[2], gathered[3]
    w_up = gathered[4 : 4 + blocks]
    w_down = gathered[4 + blocks :].reshape(blocks * width, width)
    gain_one, bias_one, gain_two, bias_two = rows[0], rows[1], rows[2], rows[3]
    start = lax.axis_index("seq") * group
    positions = start + jnp.arange(group, dtype=jnp.int32)
    segment = segment_of(lengths[0], order[0], positions)
    before = segment_of(lengths[0], order[0], jnp.reshape(start - 1, (1,)))[0]
    offsets = jnp.arange(group, dtype=jnp.int32)
    keep = ((offsets[None, :] <= offsets[:, None]) & (segment[:, None] == segment[None, :])).astype(
        jnp.float32
    )
    incoming = (segment == before).astype(jnp.float32)
    finals = (segment == segment[-1]).astype(jnp.float32)
    passes = (segment[-1] == before).astype(jnp.float32)
    inputs = tokens[0].astype(jnp.float32)
    normed = left[0].T
    query_low, key_low, value_low = [low[i].reshape(group, heads, depth) for i in range(3)]
    query_pre, key_pre = pre[0], pre[1]
    numer = ratio[0].reshape(group, heads, depth)
    denom = ratio[1].reshape(group, heads, depth)[:, :, 0]
    attended, hidden = left[1].T, left[2].T
    scores_low = (
        jnp.einsum("thd,shd->hts", query_low, key_low, preferred_element_type=jnp.float32)
        * keep[None]
    ).astype(jnp.bfloat16)
    query_wide = query_low.astype(jnp.float32)
    quads = state[:, :256].reshape(4, 128, 128)
    state_in = jnp.stack(
        [quads[:, :64, :64], quads[:, 64:, 64:], quads[:, :64, 64:], quads[:, 64:, :64]], axis=1
    ).reshape(heads, depth, depth)
    total_in = state[0, 256:].reshape(heads, depth)
    up_pre = up.transpose(1, 0, 2).reshape(group, blocks * width)
    active = act.transpose(2, 0, 1).reshape(group, blocks * width)
    grad_out = cotangent[0]
    grad_down = jnp.einsum("tf,td->fd", active, grad_out, preferred_element_type=jnp.float32)
    grad_bias_down = jnp.sum(grad_out.astype(jnp.float32), axis=0)
    grad_active = jnp.einsum("td,fd->tf", grad_out, w_down, preferred_element_type=jnp.float32)
    _, gelu_pull = jax.vjp(jax.nn.gelu, up_pre)
    grad_up_low = gelu_pull(grad_active)[0].astype(jnp.bfloat16)
    grad_up_blocks = grad_up_low.reshape(group, blocks, width)
    grad_w_up = jnp.einsum(
        "td,tjf->jdf", hidden, grad_up_blocks, preferred_element_type=jnp.float32
    )
    grad_bias_up = jnp.sum(grad_up_low.astype(jnp.float32), axis=0)
    grad_hidden = jnp.einsum(
        "tjf,jdf->td", grad_up_blocks, w_up, preferred_element_type=jnp.float32
    )
    _, norm_two_pull = jax.vjp(layer_norm, resid, gain_two, bias_two)
    grad_resid_norm, grad_gain_two, grad_bias_two = norm_two_pull(grad_hidden)
    grad_resid = grad_out.astype(jnp.float32) + grad_resid_norm
    grad_branch = grad_resid.astype(jnp.bfloat16)
    grad_w_out = jnp.einsum("tk,td->kd", attended, grad_branch, preferred_element_type=jnp.float32)
    grad_bias_o = jnp.sum(grad_branch.astype(jnp.float32), axis=0)
    grad_ratio = jnp.einsum(
        "td,kd->tk", grad_branch, w_out, preferred_element_type=jnp.float32
    ).reshape(group, heads, depth)
    grad_numer = (grad_ratio / denom[:, :, None]).astype(jnp.bfloat16)
    grad_denom = -jnp.sum(grad_ratio * numer, axis=2) / (denom * denom)
    grad_scores = jnp.einsum(
        "the,she->hts", grad_numer, value_low, preferred_element_type=jnp.float32
    )
    grad_scores_low = ((grad_scores + grad_denom.T[:, :, None]) * keep[None]).astype(jnp.bfloat16)
    grad_query = jnp.einsum(
        "hts,shd->thd", grad_scores_low, key_low, preferred_element_type=jnp.float32
    )
    grad_key = jnp.einsum(
        "hts,thd->shd", grad_scores_low, query_low, preferred_element_type=jnp.float32
    )
    grad_value = jnp.einsum(
        "hts,the->she", scores_low, grad_numer, preferred_element_type=jnp.float32
    )
    numer_grad_wide = grad_numer.astype(jnp.float32)
    grad_query = grad_query + incoming[:, None, None] * (
        jnp.einsum("the,hde->thd", numer_grad_wide, state_in, precision=highest)
        + grad_denom[:, :, None] * total_in[None]
    )
    query_masked = query_low * incoming.astype(jnp.bfloat16)[:, None, None]
    grad_state_in = jnp.einsum(
        "thd,the->hde", query_masked, grad_numer, preferred_element_type=jnp.float32
    )
    grad_total_in = jnp.einsum(
        "thd,th->hd", query_wide * incoming[:, None, None], grad_denom, precision=highest
    )
    leaving = relay_backward(pack_state(grad_state_in, grad_total_in, passes))
    grad_state = leaving[:, :depth, :]
    grad_total = leaving[:, depth, :]
    value_wide = value_low.astype(jnp.float32)
    key_wide = key_low.astype(jnp.float32)
    grad_key = grad_key + finals[:, None, None] * (
        jnp.einsum("she,hde->shd", value_wide, grad_state, precision=highest) + grad_total[None]
    )
    grad_value = grad_value + finals[:, None, None] * jnp.einsum(
        "shd,hde->she", key_wide, grad_state, precision=highest
    )
    _, query_pull = jax.vjp(feature, query_pre)
    _, key_pull = jax.vjp(feature, key_pre)
    grad_query_low = query_pull(grad_query.reshape(group, width))[0].astype(jnp.bfloat16)
    grad_key_low = key_pull(grad_key.reshape(group, width))[0].astype(jnp.bfloat16)
    grad_value_low = grad_value.reshape(group, width).astype(jnp.bfloat16)
    grad_w_query = jnp.einsum(
        "tk,tj->kj", normed, grad_query_low, preferred_element_type=jnp.float32
    )
    grad_w_key = jnp.einsum("tk,tj->kj", normed, grad_key_low, preferred_element_type=jnp.float32)
    grad_w_value = jnp.einsum(
        "tk,tj->kj", normed, grad_value_low, preferred_element_type=jnp.float32
    )
    grad_bias_q = jnp.sum(grad_query_low.astype(jnp.float32), axis=0)
    grad_bias_k = jnp.sum(grad_key_low.astype(jnp.float32), axis=0)
    grad_bias_v = jnp.sum(grad_value_low.astype(jnp.float32), axis=0)
    grad_normed = jnp.einsum(
        "tj,kj->tk", grad_query_low, w_query, preferred_element_type=jnp.float32
    )
    grad_normed = grad_normed + jnp.einsum(
        "tj,kj->tk", grad_key_low, w_key, preferred_element_type=jnp.float32
    )
    grad_normed = grad_normed + jnp.einsum(
        "tj,kj->tk", grad_value_low, w_value, preferred_element_type=jnp.float32
    )
    _, norm_one_pull = jax.vjp(layer_norm, inputs, gain_one, bias_one)
    grad_inputs_norm, grad_gain_one, grad_bias_one = norm_one_pull(grad_normed)
    input_grad = (grad_resid + grad_inputs_norm)[None]
    grad_wide = jnp.stack([grad_w_query, grad_w_key, grad_w_value, grad_w_out])
    grad_low = jnp.concatenate(
        [grad_w_up, grad_down.reshape(blocks, width, width)], axis=0
    ).astype(jnp.bfloat16)
    grad_small = jnp.concatenate(
        [
            grad_gain_one,
            grad_bias_one,
            grad_gain_two,
            grad_bias_two,
            grad_bias_q,
            grad_bias_k,
            grad_bias_v,
            grad_bias_o,
            grad_bias_down,
            grad_bias_up,
        ]
    )
    sums, row_small = reduce_rows(
        grad_wide, grad_low, padded(grad_small.reshape(nseq, share)), nseq
    )
    row_small = row_small.reshape(2048)[:share]
    row_units, update = muon(sums, momentum, nseq)
    new_momentum = 0.5 * momentum + row_units
    update = update.astype(jnp.float32)
    rates = unit_rates(blocks)
    new_weights = weights - rates[:, None, None] * (update + 0.01 * weights)
    first_new = 0.9 * moment_one + 0.1 * row_small
    second_new = 0.95 * moment_two + 0.05 * row_small * row_small
    adjusted = first_new / (1.0 - 0.9**STEP) / (jnp.sqrt(second_new / (1.0 - 0.95**STEP)) + 1e-08)
    new_small = small_params - 0.05 * (adjusted + 0.01 * small_params)
    return (block_out, input_grad, new_weights, new_momentum, new_small, first_new, second_new)


def solution(mesh):
    in_specs = (
        P("stream", "seq", None),
        P("stream", "seq", None),
        P("stream", None),
        P("stream", None),
        P(None, "seq", None),
        P(None, "seq", None),
        P("seq"),
        P("seq"),
        P("seq"),
    )
    out_specs = (
        P("stream", "seq", None),
        P("stream", "seq", None),
        P(None, "seq", None),
        P(None, "seq", None),
        P("seq"),
        P("seq"),
        P("seq"),
    )
    return jax.shard_map(local, mesh=mesh, in_specs=in_specs, out_specs=out_specs, check_vma=False)
```

```python
import functools

import jax
import jax.numpy as jnp
from jax import lax
from jax.experimental import pallas as pl
from jax.experimental.pallas import tpu as pltpu
from jax.sharding import PartitionSpec as P

MESH = pl.DeviceIdType.MESH
DMA = pltpu.SemaphoreType.DMA
ANY = pl.BlockSpec(memory_space=pl.ANY)
VMEM = pl.BlockSpec(memory_space=pltpu.VMEM)
VMEM_LIMIT = 62 << 20


def places():
    seq = lax.axis_index("seq")
    stream = lax.axis_index("stream")
    return seq // 2, seq % 2, stream // 2, stream % 2


def device(z, x, y, c):
    return {"seq": z * 2 + x, "stream": y * 2 + c}


def greet(peers):
    barrier = pltpu.get_barrier_semaphore()
    for peer in peers:
        pl.semaphore_signal(barrier, inc=1, device_id=peer, device_id_type=MESH)
    pl.semaphore_wait(barrier, len(peers))


def remote(source, target, sent, received, peer):
    return pltpu.make_async_remote_copy(
        src_ref=source,
        dst_ref=target,
        send_sem=sent,
        recv_sem=received,
        device_id=peer,
        device_id_type=MESH,
    )


def others_along_seq(z, x, y, c, count):
    straight = [device(lax.rem(z + k, count), x, y, c) for k in range(1, count)]
    across = [device(lax.rem(z + k, count), 1 - x, y, c) for k in range(count)]
    return straight, across


CHUNK = 32


SHIFTS = (0.0, 0.0, 0.1, 0.7, 0.7)
FINE = (False, False, False, True, True)
BAND = 256


def split_two(values):
    high = values.astype(jnp.bfloat16)
    return high, (values - high.astype(jnp.float32)).astype(jnp.bfloat16)


def dot(left, right, transposed=False):
    dims = (((1,), (1 if transposed else 0,)), ((), ()))
    return lax.dot_general(left, right, dims, preferred_element_type=jnp.float32)


def orthogonalize(full, xh, xl, gram, gram_low):
    size = full.shape[0]
    bands = size // BAND

    def span(index):
        return pl.ds(pl.multiple_of(index * BAND, BAND), BAND)

    def square(index, total):
        part = full[span(index), :]
        return total + jnp.sum(part * part)

    norm = jnp.sqrt(lax.fori_loop(0, bands, square, jnp.float32(0.0)))
    scale = 1.0 / (norm + 1e-07)

    def begin(index, carry):
        part = full[span(index), :] * scale
        full[span(index), :] = part
        xh[0, span(index), :] = part.astype(jnp.bfloat16)
        return carry

    lax.fori_loop(0, bands, begin, 0)
    for turn in range(len(SHIFTS)):
        shift, fine = SHIFTS[turn], FINE[turn]
        now, later = turn % 2, 1 - turn % 2
        more = turn + 1 < len(SHIFTS) and FINE[turn + 1]

        def form(index, carry):
            rows = span(index)
            left = xh[now, rows, :]
            block = dot(left, xh[now], True)
            if fine:
                block += dot(left, xl[now], True) + dot(xl[now, rows, :], xh[now], True)
            if shift:
                across = lax.broadcasted_iota(jnp.int32, block.shape, 1)
                down = lax.broadcasted_iota(jnp.int32, block.shape, 0) + index * BAND
                block = jnp.where(across == down, block - shift, block)
            gram[rows, :] = block
            gram_low[rows, :] = block.astype(jnp.bfloat16)
            return carry

        lax.fori_loop(0, bands, form, 0)
        linear = -4.775 + 2.0 * 2.0315 * shift
        scaled = 3.4445 - 4.775 * shift + 2.0315 * shift * shift

        def advance(index, carry):
            rows = span(index)
            poly = linear * gram[rows, :] + 2.0315 * dot(gram_low[rows, :], gram_low[...])
            if fine:
                high, low = split_two(poly)
                step = dot(high, xh[now]) + dot(high, xl[now]) + dot(low, xh[now])
            else:
                step = dot(poly.astype(jnp.bfloat16), xh[now])
            moved = scaled * full[rows, :] + step
            full[rows, :] = moved
            if more:
                high, low = split_two(moved)
                xh[later, rows, :] = high
                xl[later, rows, :] = low
            else:
                xh[later, rows, :] = moved.astype(jnp.bfloat16)
            return carry

        lax.fori_loop(0, bands, advance, 0)
    return len(SHIFTS) % 2


def muon_kernel(
    count, g_ref, mom_ref, all_ref, rows_ref,
    mom_own, moved, full, xh, xl, gram, gram_low,
    load_sem, own_sem, ms, mr, ys, yr, os_, or_, fs, fr, gs, gr,
):
    z, x, y, c = places()
    seq = z * 2 + x
    nseq = count * 2
    batches, rows, width = g_ref.shape
    straight, across = others_along_seq(z, x, y, c, count)
    pair = [device(z, x, 1 - y, c), device(z, x, y, 1 - c)]
    greet(straight + across + pair)
    load = pltpu.make_async_copy(mom_ref.at[:, y, c], mom_own, load_sem)
    load.start()
    keep = pltpu.make_async_copy(g_ref, all_ref.at[:, y, c], own_sem.at[0])
    keep.start()
    load.wait()
    owner = [2 * b + c + 1 for b in range(batches)]

    def block(where):
        return full.at[pl.ds(pl.multiple_of(where * rows, rows), rows)]

    for b in range(batches):
        for j in range(rows // CHUNK):
            span = slice(j * CHUNK, (j + 1) * CHUNK)
            moved[b, span, :] = 0.5 * mom_own[b, span, :] + g_ref[b, span, :]

        @pl.when(seq != owner[b])
        def _():
            remote(
                moved.at[b], block(seq), ms.at[b], mr.at[seq],
                {"seq": owner[b], "stream": y * 2 + c},
            ).start()

        @pl.when(seq == owner[b])
        def _():
            pltpu.make_async_copy(moved.at[b], block(seq), own_sem.at[1]).start()

    over = remote(g_ref, all_ref.at[:, y, c], ys.at[0], yr.at[0], pair[0])
    over.start()
    is_owner = (seq == owner[0]) | (seq == owner[1]) | (seq == owner[2])

    @pl.when(is_owner)
    def _():
        pltpu.make_async_copy(moved.at[0], block(seq), own_sem.at[1]).wait()
        for k in range(1, nseq):
            there = lax.rem(seq + k, nseq)
            remote(moved.at[0], block(there), ms.at[0], mr.at[there], pair[0]).wait_recv()
        orthogonalize(full, xh, xl, gram, gram_low)

    final = len(SHIFTS) % 2

    def result(where):
        return xh.at[final, pl.ds(pl.multiple_of(where * rows, rows), rows)]

    for b in range(batches):
        target = rows_ref.at[b, y, c]

        @pl.when(seq == owner[b])
        def _():
            pltpu.make_async_copy(result(seq), target, own_sem.at[2]).start()
            for k in range(1, nseq):
                there = lax.rem(seq + k, nseq)
                remote(
                    result(there), target, os_.at[k - 1], or_.at[b],
                    {"seq": there, "stream": y * 2 + c},
                ).start()

    keep.wait()
    over.wait_recv()
    share = remote(all_ref.at[:, :, c], all_ref.at[:, :, c], ys.at[1], yr.at[1], pair[1])
    share.start()
    hops = []
    for b in range(batches):
        target = rows_ref.at[b, y, c]

        @pl.when(seq == owner[b])
        def _():
            pltpu.make_async_copy(result(seq), target, own_sem.at[2]).wait()

        @pl.when(seq != owner[b])
        def _():
            remote(result(seq), target, os_.at[0], or_.at[b], pair[0]).wait_recv()

        hop = remote(target, target, fs.at[b], fr.at[b], pair[0])
        hop.start()
        hops.append(hop)
    lasts = []
    for b in range(batches):
        hops[b].wait_recv()
        target = rows_ref.at[b, :, c]
        last = remote(target, target, gs.at[b], gr.at[b], pair[1])
        last.start()
        lasts.append(last)
    for last in lasts:
        last.wait_recv()
    share.wait_recv()
    for copy in [over, share] + hops + lasts:
        copy.wait_send()
    for b in range(batches):

        @pl.when(seq != owner[b])
        def _():
            remote(moved.at[b], block(seq), ms.at[b], mr.at[seq], pair[0]).wait_send()

        @pl.when(seq == owner[b])
        def _():
            for k in range(1, nseq):
                there = lax.rem(seq + k, nseq)
                remote(result(there), rows_ref.at[b, y, c], os_.at[k - 1], or_.at[b], pair[0]).wait_send()


def muon(sums, momentum, nseq):
    count = nseq // 2
    batches, rows, width = sums.shape
    units = momentum.shape[0]
    f32, bf16 = jnp.float32, jnp.bfloat16
    V = pltpu.VMEM
    whole, ortho = pl.pallas_call(
        functools.partial(muon_kernel, count),
        out_shape=(
            jax.ShapeDtypeStruct((batches, 2, 2, rows, width), f32),
            jax.ShapeDtypeStruct((batches, 2, 2, rows, width), bf16),
        ),
        in_specs=[VMEM, ANY],
        out_specs=[ANY, ANY],
        scratch_shapes=[
            V((batches, rows, width), f32),
            V((batches, rows, width), f32),
            V((width, width), f32),
            V((2, width, width), bf16),
            V((2, width, width), bf16),
            V((width, width), f32),
            V((width, width), bf16),
            DMA,
            DMA((3,)),
            DMA((batches,)),
            DMA((nseq,)),
            DMA((2,)),
            DMA((2,)),
            DMA((nseq - 1,)),
            DMA((batches,)),
            DMA((batches,)),
            DMA((batches,)),
            DMA((batches,)),
            DMA((batches,)),
        ],
        compiler_params=pltpu.CompilerParams(
            collective_id=2, has_side_effects=True, vmem_limit_bytes=VMEM_LIMIT
        ),
    )(sums, momentum.reshape(batches, 2, 2, rows, width))
    return whole.reshape(units, rows, width), ortho.reshape(units, rows, width)


HALF = 64
PAIR = 128


def matrix(w_ref, batch, index):
    block = w_ref[batch, index // 2, index % 2]
    return block.reshape(block.shape[0] * block.shape[1] * block.shape[2], block.shape[3])


def norm_rows(values, gain, offset):
    center = values - jnp.mean(values, axis=-1, keepdims=True)
    spread = jnp.mean(center * center, axis=-1, keepdims=True)
    return center * lax.rsqrt(spread + 1e-05) * gain + offset


def lanes_of(head):
    lane = lax.broadcasted_iota(jnp.int32, (1, PAIR), 1)
    return (lane // HALF) == head


def block_diagonal():
    row = lax.broadcasted_iota(jnp.int32, (PAIR, PAIR), 0)
    lane = lax.broadcasted_iota(jnp.int32, (PAIR, PAIR), 1)
    return (row // HALF) == (lane // HALF)


def pair_span(index):
    return pl.ds(pl.multiple_of(index * PAIR, PAIR), PAIR)


def band_span(index):
    return pl.ds(pl.multiple_of(index * BAND, BAND), BAND)


def dot_down(left, right):
    return lax.dot_general(left, right, (((0,), (0,)), ((), ())), preferred_element_type=jnp.float32)


def pack_message(left_ref, right_ref, scale_ref, row_ref, message):
    diagonal = block_diagonal()
    for j in range(4):
        parts = []
        for p in (2 * j, 2 * j + 1):
            lanes = slice(p * PAIR, (p + 1) * PAIR)
            scale = scale_ref[...]
            left = (left_ref[:, lanes].astype(jnp.float32) * scale).astype(jnp.bfloat16)
            parts.append(dot_down(left, right_ref[:, lanes]))
            if row_ref is None:
                total = jnp.sum(left.astype(jnp.float32), axis=0, keepdims=True)
            else:
                total = jnp.sum(left.astype(jnp.float32) * row_ref[:, lanes], axis=0, keepdims=True)
            for half in range(2):
                message[half, 256 + p : 257 + p, :] = total
        block = jnp.where(diagonal, parts[0], pltpu.roll(parts[1], HALF, 1))
        message[j // 2, (j % 2) * PAIR : (j % 2 + 1) * PAIR, :] = block


def unpack_message(message, p):
    diagonal = block_diagonal()
    j = p // 2
    block = message[j // 2, (j % 2) * PAIR : (j % 2 + 1) * PAIR, :]
    if p % 2:
        block = pltpu.roll(block, HALF, 1)
    block = jnp.where(diagonal, block, 0.0)
    row = message[0, 256 + p : 257 + p, :]
    column = jnp.transpose(jnp.broadcast_to(row, (PAIR, PAIR)))
    return block, jnp.where(diagonal, column, 0.0)


class Relay:
    def __init__(self, count, coef, own, across, part, spread, total, result, sems, places_):
        self.count, self.coef, self.own, self.across = count, coef, own, across
        self.part, self.spread, self.total, self.result = part, spread, total, result
        self.send, self.recv = sems
        self.z, self.x, self.y, self.c = places_
        self.pair = device(self.z, 1 - self.x, self.y, self.c)

    def swap(self):
        self.first = remote(self.own, self.across, self.send.at[0], self.recv.at[0], self.pair)
        self.first.start()

    def spread_out(self):
        self.first.wait_recv()
        self.part[...] = self.coef[0] * self.own[self.x] + self.coef[1] * self.across[self.x]
        self.copies = []
        for k in range(1, self.count):
            peer = device(lax.rem(self.z + k, self.count), self.x, self.y, self.c)
            copy = remote(self.part, self.spread.at[k - 1], self.send.at[k], self.recv.at[k], peer)
            copy.start()
            self.copies.append(copy)

    def join(self):
        total = jnp.zeros_like(self.part)
        for k, copy in enumerate(self.copies):
            copy.wait_recv()
            total = total + self.coef[4 + k] * self.spread[k]
        self.total[self.x] = total
        half = self.total.at[self.x]
        self.last = remote(half, half, self.send.at[self.count], self.recv.at[self.count], self.pair)
        self.last.start()

    def finish(self):
        self.last.wait_recv()
        for half in range(2):
            self.result[half] = self.coef[2] * self.total[half] + self.coef[3] * self.across[half]

    def wait_sends(self):
        for copy in [self.first, self.last] + self.copies:
            copy.wait_send()


def head_scores(q_ref, k_ref, keep_ref, lanes, head, band):
    rows = slice(band * BAND, (band + 1) * BAND)
    upto = slice(0, (band + 1) * BAND)
    query = jnp.where(lanes_of(head), q_ref[rows, lanes], 0)
    return dot(query, k_ref[upto, lanes], True) * keep_ref[rows, upto]


def attend_pair(p, q_ref, k_ref, v_ref, keep_ref, num_ref, den_ref):
    lanes = pair_span(p)
    group = q_ref.shape[0]
    value = v_ref[:, lanes]
    first = lanes_of(0)
    for band in range(group // BAND):
        rows = slice(band * BAND, (band + 1) * BAND)
        sums, totals = [], []
        for head in range(2):
            scores = head_scores(q_ref, k_ref, keep_ref, lanes, head, band)
            totals.append(jnp.sum(scores, axis=1, keepdims=True))
            sums.append(dot(scores.astype(jnp.bfloat16), value[: (band + 1) * BAND]))
        num_ref[rows, lanes] = jnp.where(first, sums[0], sums[1])
        den_ref[rows, lanes] = jnp.where(first, totals[0], totals[1])


def image_ends(lengths_ref, order_ref):
    images = lengths_ref.shape[1]
    ends, running = [], jnp.int32(0)
    for j in range(images):
        for i in range(images):
            running = running + jnp.where(order_ref[0, j] == i, lengths_ref[0, i], 0)
        ends.append(running)
    return ends


def segment_at(ends, positions):
    found = jnp.zeros_like(positions)
    for end in ends:
        found = found + jnp.where(positions >= end, 1, 0)
    return found


def same(left, right):
    return jnp.where(left == right, 1.0, 0.0)


def fill_masks(ends, start, group, keep_ref, flags_ref):
    for band in range(group // BAND):
        rows = slice(band * BAND, (band + 1) * BAND)
        down = lax.broadcasted_iota(jnp.int32, (BAND, group), 0) + band * BAND
        along = lax.broadcasted_iota(jnp.int32, (BAND, group), 1)
        mine = segment_at(ends, down + start)
        theirs = segment_at(ends, along + start)
        keep_ref[rows, :] = jnp.where(along <= down, same(mine, theirs), 0.0)
        narrow = mine[:, :PAIR]
        flags_ref[0, rows, :] = same(narrow, segment_at(ends, start - 1))
        flags_ref[1, rows, :] = same(narrow, segment_at(ends, start + group - 1))


def pass_at(ends, block, group):
    return same(segment_at(ends, block * group + group - 1), segment_at(ends, block * group - 1))


def forward_factors(ends, group, count, z, x):
    both = [pass_at(ends, 2 * z, group), pass_at(ends, 2 * z + 1, group)]
    near = [jnp.where(x == 0, both[1], 1.0), jnp.where(x == 0, 1.0, both[1])]
    near += [jnp.where(x == 0, 1.0, both[0]), jnp.where(x == 0, 0.0, 1.0)]
    running, far = jnp.float32(1.0), []
    for k in range(1, count):
        far.append(jnp.where(z - k >= 0, running, 0.0))
        there = jnp.maximum(z - k, 0)
        running = running * pass_at(ends, 2 * there, group) * pass_at(ends, 2 * there + 1, group)
    return near + far


def backward_factors(ends, group, count, z, x):
    both = [pass_at(ends, 2 * z, group), pass_at(ends, 2 * z + 1, group)]
    near = [jnp.where(x == 0, 1.0, both[0]), jnp.where(x == 0, both[0], 1.0)]
    near += [jnp.where(x == 0, both[1], 1.0), jnp.where(x == 0, 1.0, 0.0)]
    running, ahead = jnp.float32(1.0), []
    for k in range(1, count):
        ahead.append(jnp.where(z + k < count, running, 0.0))
        there = jnp.minimum(z + k, count - 1)
        running = running * pass_at(ends, 2 * there, group) * pass_at(ends, 2 * there + 1, group)
    return near + ahead[::-1]


def forward_kernel(
    count, aligned, x_ref, w_ref, small_ref, lengths_ref, order_ref,
    w_out, out_ref, rows_ref, low_ref, pre_ref, ratio_ref, left_ref, resid_ref, up_ref, act_ref, state_ref,
    w_all, stage, small_in, keep, flags, h1, q, k, v, num, den, o, resid, h2, act, turned, act_turned, message, across, part, spread, total_ref, state,
    load_sem, out_sem, zs, zr, ps, pr, ss, sr, rs, rr,
):
    z, x, y, c = places()
    straight, far = others_along_seq(z, x, y, c, count)
    pair = [device(z, 1 - x, y, c), device(z, x, 1 - y, c), device(z, x, y, 1 - c)]
    batches = w_ref.shape[0]
    rows, width = w_ref.shape[3:]
    group = x_ref.shape[0]
    bands = group // BAND
    loads = []
    for b in range(batches):
        for i in range(4):
            copy = pltpu.make_async_copy(
                w_ref.at[b, i // 2, i % 2],
                stage.at[b, pl.ds(i * rows, rows)],
                load_sem.at[b, i],
            )
            copy.start()
            loads.append(copy)
    greet(straight + far + pair[1:])
    small = []
    if aligned:
        for j, peer in enumerate(straight + far):
            small.append(remote(small_ref, small_in.at[z * 2 + x], ss.at[j], sr.at[j], peer))
            small[-1].start()
        small_in[z * 2 + x] = small_ref[...]
    spread_w = {}

    def cast_own(b):
        for i in range(4):
            loads[b * 4 + i].wait()
            for j in range(rows // CHUNK):
                span = slice(j * CHUNK, (j + 1) * CHUNK)
                at = slice(i * rows + j * CHUNK, i * rows + (j + 1) * CHUNK)
                w_all[b, i // 2, i % 2, z, x, span, :] = stage[b, at, :].astype(jnp.bfloat16)

    def send_own(b):
        for j in range(1, count):
            block = w_all.at[b, y, c, z, x]
            spread_w[b, j] = remote(block, block, zs.at[b, j - 1], zr.at[b, j - 1], straight[j - 1])
            spread_w[b, j].start()

    first, second, third, outs, waited = [], [], [], [], []
    plan = [(b, 0) for b in range(batches)]
    plan += [(b, j) for b in range(batches) for j in range(1, count)]
    total = len(plan)

    def send(kept, phase, index, block, peer):
        kept.append(remote(block, block, ps.at[phase, index], pr.at[phase, index], peer))
        kept[-1].start()

    def put_out(source, target):
        copy = pltpu.make_async_copy(source, target, out_sem.at[len(outs)])
        copy.start()
        outs.append(copy)
        return copy

    def tick(step):
        index = step
        if index < total:
            b, j = plan[index]
            there = lax.rem(z - j + count, count)
            if j:
                spread_w[b, j].wait_recv()
            send(first, 0, index, w_all.at[b, y, c, there, x], pair[(j + b) % 2 if j else 0])
            if j == min(1, count - 1) and b + 1 < batches:
                send_own(b + 1)
        index = step - 1
        if 0 <= index < total:
            b, j = plan[index]
            there = lax.rem(z - j + count, count)
            first[index].wait_recv()
            if j == 0:
                send(second, 1, index, w_all.at[b, y, c, z, 1 - x], pair[1])
            elif (j + b) % 2 == 0:
                send(second, 1, index, w_all.at[b, y, c, there], pair[1])
            else:
                send(second, 1, index, w_all.at[b, :, c, there, x], pair[0])
        index = step - 2
        if 0 <= index < total:
            b, j = plan[index]
            there = lax.rem(z - j + count, count)
            second[index].wait_recv()
            block = w_all.at[b, :, c, z, 1 - x] if j == 0 else w_all.at[b, :, c, there]
            send(third, 2, index, block, pair[2])
        index = step - 3
        if 0 <= index < total:
            b, j = plan[index]
            there = lax.rem(z - j + count, count)
            third[index].wait_recv()
            put_out(w_all.at[b, :, :, there], w_out.at[b, :, :, there])

    cast_own(0)
    send_own(0)
    tick(0)
    for b in range(1, batches):
        cast_own(b)
        tick(b)
    if aligned:
        for copy in small:
            copy.wait_recv()
        share_rows = 13 * 1024 // 128 // (count * 2)
        for j in range(13 * 8):
            rows_ref[j // 8 : j // 8 + 1, (j % 8) * 128 : (j % 8 + 1) * 128] = small_in[
                j // share_rows, j % share_rows : j % share_rows + 1, :
            ]
    else:
        rows_ref[0:13, :] = small_ref[...]

    def vector(index):
        return rows_ref[index : index + 1, :]

    def norm_one(i, carry):
        span = band_span(i)
        value = norm_rows(x_ref[span, :].astype(jnp.float32), vector(0), vector(1))
        h1[span, :] = value.astype(jnp.bfloat16)
        turned[0, :, span] = jnp.transpose(value).astype(jnp.bfloat16)
        return carry

    lax.fori_loop(0, bands, norm_one, 0)
    ends = image_ends(lengths_ref, order_ref)
    fill_masks(ends, (z * 2 + x) * group, group, keep, flags)
    factors = forward_factors(ends, group, count, z, x)
    ready = batches + count - 1 + 3
    for step in range(batches, ready):
        tick(step)

    def project(i, carry):
        span = band_span(i)
        left = h1[span, :]
        for index, low in ((0, q), (1, k)):
            pre = dot(left, matrix(w_all, 0, index)) + vector(4 + index)
            stage[index, span, :] = pre
            low[span, :] = jnp.where(pre > 0, pre + 1.0, jnp.exp(jnp.minimum(pre, 0.0))).astype(jnp.bfloat16)
        v[span, :] = (dot(left, matrix(w_all, 0, 2)) + vector(6)).astype(jnp.bfloat16)
        return carry

    lax.fori_loop(0, bands, project, 0)
    pack_message(k, v, flags.at[1], None, message)
    relay = Relay(count, factors, message, across, part, spread, total_ref, state, (rs, rr), (z, x, y, c))
    relay.swap()
    stored = [put_out(stage.at[0], pre_ref.at[0]), put_out(stage.at[1], pre_ref.at[1]), None]
    for index, low in enumerate((q, k, v)):
        put_out(low, low_ref.at[index])

    def attend(p, carry):
        attend_pair(p, q, k, v, keep, num, den)
        return carry

    pairs = width // PAIR
    step = ready
    lax.fori_loop(0, pairs // 4, attend, 0)
    tick(step)
    relay.spread_out()
    lax.fori_loop(pairs // 4, pairs // 2, attend, 0)
    tick(step + 1)
    lax.fori_loop(pairs // 2, pairs, attend, 0)
    relay.join()
    tick(step + 2)
    relay.finish()
    put_out(state, state_ref)
    for p in range(pairs):
        block, column = unpack_message(state, p)
        high, low = split_two(jnp.concatenate([block, column], axis=1))
        lanes = slice(p * PAIR, (p + 1) * PAIR)
        for i in range(bands):
            span = slice(i * BAND, (i + 1) * BAND)
            query = q[span, lanes]
            both = dot(query, high) + dot(query, low)
            flag = flags[0, span, :]
            top = num[span, lanes] + flag * both[:, :PAIR]
            bottom = den[span, lanes] + flag * both[:, PAIR:]
            num[span, lanes] = top
            den[span, lanes] = bottom
            o[span, lanes] = (top / bottom).astype(jnp.bfloat16)
    put_out(num, ratio_ref.at[0])
    put_out(den, ratio_ref.at[1])

    def close(i, carry):
        span = band_span(i)
        value = x_ref[span, :].astype(jnp.float32) + dot(o[span, :], matrix(w_all, 0, 3)) + vector(7)
        resid[span, :] = value
        hidden = norm_rows(value, vector(2), vector(3))
        h2[span, :] = hidden.astype(jnp.bfloat16)
        turned[2, :, span] = jnp.transpose(hidden).astype(jnp.bfloat16)
        turned[1, :, span] = jnp.transpose(o[span, :].astype(jnp.float32)).astype(jnp.bfloat16)
        return carry

    lax.fori_loop(0, bands, close, 0)
    put_out(turned, left_ref)
    put_out(resid, resid_ref)
    step = step + 3
    ready = batches + 2 * (count - 1) + 3
    while step < ready:
        tick(step)
        step += 1
    blocks = act.shape[0]
    turned_out = []
    for j in range(blocks):
        if j > 1:
            turned_out[j - 2].wait()
            waited.append(turned_out[j - 2])
        if stored[j % 3] is not None:
            stored[j % 3].wait()
            waited.append(stored[j % 3])

        def expand(i, carry):
            span = band_span(i)
            pre = dot(h2[span, :], matrix(w_all, 1, j)) + vector(9 + j)
            stage[j % 3, span, :] = pre
            value = jax.nn.gelu(pre)
            act[j, span, :] = value.astype(jnp.bfloat16)
            act_turned[j % 2, :, span] = jnp.transpose(value).astype(jnp.bfloat16)
            return carry

        lax.fori_loop(0, bands, expand, 0)
        stored[j % 3] = put_out(stage.at[j % 3], up_ref.at[j])
        turned_out.append(put_out(act_turned.at[j % 2], act_ref.at[j]))
        if step < total + 3:
            tick(step)
            step += 1
    while step < total + 3:
        tick(step)
        step += 1

    def project_down(i, carry):
        span = band_span(i)
        value = resid[span, :] + vector(8)
        for j in range(blocks):
            value += dot(act[j, span, :], matrix(w_all, 2, j))
        out_ref[span, :] = value.astype(jnp.bfloat16)
        return carry

    lax.fori_loop(0, bands, project_down, 0)
    for copy in outs:
        if not any(copy is other for other in waited):
            copy.wait()
    for copy in list(spread_w.values()) + first + second + third + small:
        copy.wait_send()
    relay.wait_sends()


def forward(x, weights, small, lengths, order, nseq, aligned):
    group, width = x.shape
    units, rows, _ = weights.shape
    count, batches = nseq // 2, units // 4
    steps = batches * count
    f32, bf16 = jnp.float32, jnp.bfloat16
    V, S = pltpu.VMEM, jax.ShapeDtypeStruct
    blocks = 4
    smem = pl.BlockSpec(memory_space=pltpu.SMEM)
    message = (2, 264, PAIR)
    return pl.pallas_call(
        functools.partial(forward_kernel, count, aligned),
        out_shape=(
            S((batches, 2, 2, count, 2, rows, width), bf16),
            S((group, width), bf16),
            S((16, width), f32),
            S((3, group, width), bf16),
            S((2, group, width), f32),
            S((2, group, width), f32),
            S((3, width, group), bf16),
            S((group, width), f32),
            S((blocks, group, width), f32),
            S((blocks, width, group), bf16),
            S(message, f32),
        ),
        in_specs=[VMEM, ANY, VMEM, smem, smem],
        out_specs=[ANY, VMEM, VMEM] + [ANY] * 8,
        scratch_shapes=[
            V((batches, 2, 2, count, 2, rows, width), bf16),
            V((3, group, width), f32),
            V(((nseq,) if aligned else ()) + small.shape, f32),
            V((group, group), f32),
            V((2, group, PAIR), f32),
            V((group, width), bf16),
            V((group, width), bf16),
            V((group, width), bf16),
            V((group, width), bf16),
            V((group, width), f32),
            V((group, width), f32),
            V((group, width), bf16),
            V((group, width), f32),
            V((group, width), bf16),
            V((blocks, group, width), bf16),
            V((3, width, group), bf16),
            V((2, width, group), bf16),
            V(message, f32),
            V(message, f32),
            V(message[1:], f32),
            V((count - 1,) + message[1:], f32),
            V(message, f32),
            V(message, f32),
            DMA((batches, 4)),
            DMA((steps + 20,)),
            DMA((batches, count - 1)),
            DMA((batches, count - 1)),
            DMA((3, steps)),
            DMA((3, steps)),
            DMA((nseq - 1,)),
            DMA((nseq - 1,)),
            DMA((count + 1,)),
            DMA((count + 1,)),
        ],
        compiler_params=pltpu.CompilerParams(
            collective_id=0, has_side_effects=True, vmem_limit_bytes=VMEM_LIMIT
        ),
    )(x, weights.reshape(batches, 2, 2, rows, width), small, lengths, order)


def gelu_slope(values):
    cube = 0.044715 * values * values
    bend = jnp.tanh(0.7978845608028654 * values * (1.0 + cube))
    return 0.5 * (1.0 + bend) + 0.5 * values * (1.0 - bend * bend) * (
        0.7978845608028654 * (1.0 + 3.0 * cube)
    )


def norm_back(values, upstream, gain):
    center = values - jnp.mean(values, axis=-1, keepdims=True)
    spread = jnp.mean(center * center, axis=-1, keepdims=True)
    scale = lax.rsqrt(spread + 1e-05)
    unit = center * scale
    inner = upstream * gain
    back = inner - jnp.mean(inner, axis=-1, keepdims=True)
    back = scale * (back - unit * jnp.mean(inner * unit, axis=-1, keepdims=True))
    return back, unit


def pick_message(message, p):
    down = pl.ds(pl.multiple_of(((p // 2) % 2) * PAIR, PAIR), PAIR)
    block = message[p // 4, down, :]
    block = jnp.where(p % 2 == 1, pltpu.roll(block, HALF, 1), block)
    block = jnp.where(block_diagonal(), block, 0.0)
    return split_two(block), message[0, pl.ds(256 + p, 1), :]


class Sums:
    def __init__(self, count, place, wide, product, bufs, sems, sums_ref):
        self.count = count
        self.z, self.x, self.y, self.c = z, x, y, c = place
        self.wide, self.product, self.sums_ref = wide, product, sums_ref
        (self.core_out, self.core_in, self.own, self.first_out, self.first_in, self.kept_one,
         self.second_out, self.second_in, self.kept_two, self.far_out, self.far_in) = bufs
        (self.cs, self.cr, self.fs, self.fr, self.es, self.er, self.zs, self.zr,
         self.credit_core, self.credit_first, self.credit_second) = sems
        self.pair = [device(z, 1 - x, y, c), device(z, x, 1 - y, c), device(z, x, y, 1 - c)]
        self.steps = [(b, k) for b in (2, 1, 0) for k in range(count)]
        self.total = len(self.steps)
        self.cores, self.firsts, self.seconds, self.fars = [], [], [], {}
        self.rows = sums_ref.shape[1]

    def there(self, i):
        return lax.rem(self.z + 1 + self.steps[i][1], self.count)

    def parts(self, i):
        return (0, 1) if self.steps[i][0] in self.wide else (0,)

    def span(self, ref, i):
        return ref if len(self.parts(i)) == 2 else ref.at[pl.ds(0, 1)]

    def give(self, semaphore, peer):
        pl.semaphore_signal(semaphore, inc=1, device_id=peer, device_id_type=MESH)

    def store(self, value, targets):
        high = value.astype(jnp.bfloat16)
        targets[0][...] = high
        if len(targets) == 2:
            targets[1][...] = (value - high.astype(jnp.float32)).astype(jnp.bfloat16)

    def add(self, i, base, got, send, keep):
        def body(index, carry):
            at = pl.ds(pl.multiple_of(index * CHUNK, CHUNK), CHUNK)
            value = base[at, :]
            for part in got:
                value = value + part[at, :].astype(jnp.float32)
            if keep is not None:
                keep[at, :] = value
            else:
                self.store(value, [ref.at[at] for ref in send])
            return carry

        lax.fori_loop(0, self.rows // CHUNK, body, 0)

    def stage_a(self, i):
        slot = i % 2
        batch = self.steps[i][0]
        if i >= 2:
            self.cores[i - 2].wait_send()
        for yy in range(2):
            value = self.product(i, batch, yy, 1 - self.c)
            for xx in range(2):
                rows = slice(xx * self.rows, (xx + 1) * self.rows)
                self.store(value[rows], [self.core_out.at[slot, h, yy, xx] for h in self.parts(i)])
        if i >= 2:
            pl.semaphore_wait(self.credit_core, 1)
        source, target = self.span(self.core_out.at[slot], i), self.span(self.core_in.at[slot], i)
        self.cores.append(remote(source, target, self.cs.at[i], self.cr.at[i], self.pair[2]))
        self.cores[i].start()
        for yy in range(2):
            value = self.product(i, batch, yy, self.c)
            for xx in range(2):
                self.own[yy, xx] = value[xx * self.rows : (xx + 1) * self.rows]

    def stage_b(self, i):
        slot = i % 2
        k = self.steps[i][1]
        x, y = self.x, self.y
        self.cores[i].wait_recv()
        if i >= 3:
            self.firsts[i - 3].wait_send()
        out = self.first_out.at[i % 3]
        for j in range(2):
            away, near = ((1 - y, j), (y, j)) if k % 2 == 0 else ((j, 1 - x), (j, x))
            for at, send, keep in (
                (away, [out.at[h, j] for h in self.parts(i)], None),
                (near, None, self.kept_one.at[j]),
            ):
                got = [self.core_in.at[slot, h, at[0], at[1]] for h in self.parts(i)]
                self.add(i, self.own.at[at[0], at[1]], got, send, keep)
        if i + 2 < self.total:
            self.give(self.credit_core, self.pair[2])
        if i >= 4:
            pl.semaphore_wait(self.credit_first.at[i % 2], 1)
        peer = self.pair[1 - k % 2]
        source, target = self.span(out, i), self.span(self.first_in.at[i % 4], i)
        self.firsts.append(remote(source, target, self.fs.at[i], self.fr.at[i], peer))
        self.firsts[i].start()

    def stage_c(self, i):
        k = self.steps[i][1]
        mine = self.x if k % 2 == 0 else self.y
        self.firsts[i].wait_recv()
        if i >= 3:
            self.seconds[i - 3].wait_send()
        out = self.second_out.at[i % 3]
        got = self.first_in.at[i % 4]
        self.add(i, self.kept_one.at[1 - mine], [got.at[h, 1 - mine] for h in self.parts(i)],
                 [out.at[h] for h in self.parts(i)], None)
        self.add(i, self.kept_one.at[mine], [got.at[h, mine] for h in self.parts(i)], None, self.kept_two)
        if i + 4 < self.total:
            self.give(self.credit_first.at[i % 2], self.pair[1 - k % 2])
        if i >= 4:
            pl.semaphore_wait(self.credit_second.at[i % 2], 1)
        source, target = self.span(out, i), self.span(self.second_in.at[i % 4], i)
        self.seconds.append(remote(source, target, self.es.at[i], self.er.at[i], self.pair[k % 2]))
        self.seconds[i].start()

    def stage_d(self, i):
        b, k = self.steps[i]
        self.seconds[i].wait_recv()
        got = [self.second_in.at[i % 4, h] for h in self.parts(i)]
        if k < self.count - 1:
            if i >= self.count:
                self.fars[i - self.count].wait_send()
            out = self.far_out.at[k]
            self.add(i, self.kept_two, got, [out.at[h] for h in self.parts(i)], None)
            peer = device(self.there(i), self.x, self.y, self.c)
            source, target = self.span(out, i), self.span(self.far_in.at[b, k], i)
            self.fars[i] = remote(source, target, self.zs.at[b, k], self.zr.at[b, k], peer)
            self.fars[i].start()
        else:
            self.add(i, self.kept_two, got, None, self.sums_ref.at[b])
        if i + 4 < self.total:
            self.give(self.credit_second.at[i % 2], self.pair[k % 2])

    def stage_e(self, i):
        b, k = self.steps[i]
        if k < self.count - 1:
            return
        for j in range(self.count - 1):
            self.fars[i - self.count + 1 + j].wait_recv()
            got = [self.far_in.at[b, j, h] for h in self.parts(i)]
            self.add(i, self.sums_ref.at[b], got, None, self.sums_ref.at[b])

    def tick(self, i):
        for lag, stage in ((4, self.stage_e), (3, self.stage_d), (2, self.stage_c), (1, self.stage_b), (0, self.stage_a)):
            if 0 <= i - lag < self.total:
                stage(i - lag)

    def wait_sends(self):
        for copy in self.cores[-2:] + self.firsts[-3:] + self.seconds[-3:]:
            copy.wait_send()
        for i, copy in self.fars.items():
            if i >= self.total - self.count:
                copy.wait_send()


def backward_kernel(
    count, aligned, x_ref, dy_ref, w_ref, rows_ref, low_ref, pre_ref, ratio_ref, left_ref, resid_ref, up_ref, act_ref,
    state, lengths_ref, order_ref,
    grad_ref, sums_ref, small_out,
    core_out, core_in, own, first_out, first_in, kept_one, second_out, second_in, kept_two, far_out, far_in,
    big, left, wbuf, ubuf, acc, da, dq_low, dnum, dden, keep, flags, gs,
    message, across, part, spread, total_ref, state_back, sm_send, sm_recv, sm_part, sm_pair,
    load_sem, lt_sem, cs, cr, fs, fr, es, er, zs, zr, credit_core, credit_first, credit_second, rs, rr, ms, mr,
):
    place = z, x, y, c = places()
    straight, far = others_along_seq(z, x, y, c, count)
    pair = [device(z, 1 - x, y, c), device(z, x, 1 - y, c), device(z, x, y, 1 - c)]
    group, width = x_ref.shape
    bands = group // BAND
    pairs = width // PAIR
    block_rows = 2 * sums_ref.shape[1]
    f32, bf16 = jnp.float32, jnp.bfloat16
    issued = []

    def load(source, target):
        copy = pltpu.make_async_copy(source, target, load_sem.at[len(issued)])
        copy.start()
        issued.append(copy)
        return copy

    def load_left(i):
        b = sums.steps[i][0]
        at = pl.ds(pl.multiple_of(sums.there(i) * block_rows, block_rows), block_rows)
        slot = left.at[i % 2]
        if b == 2:
            pieces = [(act_ref.at[:, at], slot)]
        elif b == 1:
            pieces = [(left_ref.at[pl.ds(2, 1), at], slot.at[pl.ds(0, 1)])]
        else:
            pieces = [(left_ref.at[pl.ds(0, 2), at], slot.at[pl.ds(0, 2)])]
        copies = [pltpu.make_async_copy(s, t, lt_sem.at[i]) for s, t in pieces]
        for copy in copies:
            copy.start()
        return copies

    lefts = {}

    def product(i, batch, yy, cc):
        unit = 2 * yy + cc
        if batch == 2:
            lhs, rhs = left[i % 2, unit], dy_ref[...]
        elif batch == 1:
            lhs, rhs = left[i % 2, 0], big[unit]
        else:
            lhs, rhs = left[i % 2, yy * cc], big[unit]
        return dot(lhs, rhs)

    sums = Sums(
        count, place, (0,), product,
        (core_out, core_in, own, first_out, first_in, kept_one, second_out, second_in, kept_two, far_out, far_in),
        (cs, cr, fs, fr, es, er, zs, zr, credit_core, credit_first, credit_second), sums_ref,
    )

    def tick(i):
        if i < sums.total:
            for copy in lefts[i]:
                copy.wait()
            if i + 1 < sums.total:
                lefts[i + 1] = load_left(i + 1)
        sums.tick(i)

    lefts[0] = load_left(0)
    blocks = big.shape[0]
    w_loads = {(2, j): load(w_ref.at[8 + j], wbuf.at[j]) for j in range(2)}
    u_loads = {j: load(up_ref.at[j], ubuf.at[j]) for j in range(2)}
    resid_load = load(resid_ref, grad_ref)
    greet(straight + far + pair[1:])
    ends = image_ends(lengths_ref, order_ref)
    fill_masks(ends, (z * 2 + x) * group, group, keep, flags)
    factors = backward_factors(ends, group, count, z, x)
    gs[...] = jnp.zeros_like(gs)

    def add_row(index, value, lanes=slice(None)):
        gs[index : index + 1, lanes] = gs[index : index + 1, lanes] + jnp.sum(
            value.astype(f32), axis=0, keepdims=True
        )

    def unit_of(slot):
        return wbuf[slot].reshape(width, width)

    for i in range(bands):
        add_row(8, dy_ref[i * BAND : (i + 1) * BAND, :])
    for j in range(blocks):
        tick(j)
        w_loads[2, j].wait()
        u_loads[j].wait()

        def hidden_back(i, carry):
            span = band_span(i)
            back = dot(dy_ref[span, :], unit_of(j % 2), True)
            back = (back * gelu_slope(ubuf[j % 2, span, :])).astype(bf16)
            big[j, span, :] = back
            add_row(9 + j, back)
            return carry

        lax.fori_loop(0, bands, hidden_back, 0)
        if j + 2 < blocks:
            w_loads[2, j + 2] = load(w_ref.at[8 + j + 2], wbuf.at[j % 2])
            u_loads[j + 2] = load(up_ref.at[j + 2], ubuf.at[j % 2])
        else:
            w_loads[1, j - 2] = load(w_ref.at[4 + j - 2], wbuf.at[j % 2])
            u_loads[j + 2] = load(ratio_ref.at[j - 2], ubuf.at[j % 2])
    for j in range(blocks):
        if j % 2 == 0:
            tick(blocks + j // 2)
        w_loads[1, j].wait()

        def up_back(i, carry):
            span = band_span(i)
            back = dot(big[j, span, :], unit_of(j % 2), True)
            acc[span, :] = back if j == 0 else acc[span, :] + back
            return carry

        lax.fori_loop(0, bands, up_back, 0)
        if j + 2 < blocks:
            w_loads[1, j + 2] = load(w_ref.at[4 + j + 2], wbuf.at[j % 2])
        elif j + 2 == blocks:
            w_loads[0, 3] = load(w_ref.at[3], wbuf.at[0])
        else:
            low_loads = [load(low_ref.at[0], wbuf.at[1, 0]), load(low_ref.at[1], wbuf.at[1, 1])]
    resid_load.wait()
    w_loads[0, 3].wait()

    def middle_back(i, carry):
        span = band_span(i)
        upstream = acc[span, :]
        back, unit = norm_back(grad_ref[span, :], upstream, rows_ref[2:3, :])
        add_row(2, upstream * unit)
        add_row(3, upstream)
        total = dy_ref[span, :].astype(f32) + back
        grad_ref[span, :] = total
        low = total.astype(bf16)
        da[span, :] = low
        add_row(7, low)
        acc[span, :] = dot(low, unit_of(0), True)
        return carry

    lax.fori_loop(0, bands, middle_back, 0)
    low_loads.append(load(low_ref.at[2], wbuf.at[0, 0]))
    u_loads[blocks].wait()
    u_loads[blocks + 1].wait()

    def ratio_back(p, carry):
        lanes = pair_span(p)
        first = lanes_of(0)
        for i in range(bands):
            span = slice(i * BAND, (i + 1) * BAND)
            inverse = 1.0 / ubuf[1, span, lanes]
            scaled = acc[span, lanes] * inverse
            dnum[span, lanes] = scaled.astype(bf16)
            weighted = scaled * ubuf[0, span, lanes] * inverse
            one = jnp.sum(jnp.where(first, weighted, 0.0), axis=1, keepdims=True)
            two = jnp.sum(jnp.where(first, 0.0, weighted), axis=1, keepdims=True)
            dden[span, lanes] = -jnp.where(first, one, two)
        return carry

    lax.fori_loop(0, pairs, ratio_back, 0)
    for copy in low_loads:
        copy.wait()
    query, key, value = wbuf.at[1, 0], wbuf.at[1, 1], wbuf.at[0, 0]
    pack_message(query, dnum, flags.at[0], dden, message)
    relay = Relay(count, factors, message, across, part, spread, total_ref, state_back, (rs, rr), place)
    relay.swap()
    pre_load = load(pre_ref.at[0], acc)
    pre_load.wait()

    def attend_back(p, carry):
        lanes = pair_span(p)
        (state_high, state_low), totals = pick_message(state, p)
        lane = lax.broadcasted_iota(jnp.int32, (1, PAIR), 1) % HALF
        for band in range(bands):
            span = slice(band * BAND, (band + 1) * BAND)
            upto = (band + 1) * BAND
            back = dnum[span, lanes]
            below = dden[span, lanes]
            high, low = split_two(pltpu.roll(below, HALF, 1))
            extra = jnp.where(lane == 0, high, jnp.where(lane == 1, low, jnp.zeros_like(low)))
            asked = query[span, lanes]
            keys = key[0:upto, lanes]
            held = value[0:upto, lanes]
            kept = keep[span, 0:upto]
            found, key_back, value_back = [], 0.0, 0.0
            for head in range(2):
                mine = lanes_of(head)
                masked = jnp.where(mine, asked, 0)
                scores = (dot(masked, keys, True) * kept).astype(bf16)
                scores_back = dot(jnp.where(mine, back, extra), jnp.where(mine, held, 1), True)
                scores_back = (scores_back * kept).astype(bf16)
                found.append(dot(scores_back, keys))
                key_back = key_back + dot_down(scores_back, masked)
                value_back = value_back + dot_down(scores, jnp.where(mine, back, 0))
            across_blocks = dot(back, state_high, True) + dot(back, state_low, True) + below * totals
            query_back = jnp.where(lanes_of(0), found[0], found[1]) + flags[0, span, :] * across_blocks
            pre = acc[span, lanes]
            slope = jnp.where(pre > 0, 1.0, jnp.exp(jnp.minimum(pre, 0.0)))
            dq_low[span, lanes] = (query_back * slope).astype(bf16)
            for index, total in ((0, key_back), (1, value_back)):
                if band:
                    ubuf[index, 0 : upto - BAND, lanes] = (
                        ubuf[index, 0 : upto - BAND, lanes] + total[: upto - BAND]
                    )
                ubuf[index, span, lanes] = total[upto - BAND :]
        return carry

    lax.fori_loop(0, pairs // 4, attend_back, 0)
    tick(blocks + 2)
    relay.spread_out()
    lax.fori_loop(pairs // 4, pairs // 2, attend_back, 0)
    tick(blocks + 3)
    relay.join()
    lax.fori_loop(pairs // 2, pairs, attend_back, 0)
    pre_load = load(pre_ref.at[1], acc)
    for i in range(blocks + 4, sums.total - count):
        tick(i)
    relay.finish()
    pre_load.wait()

    def attend_close(p, carry):
        lanes = pair_span(p)
        (back_high, back_low), totals = pick_message(state_back, p)
        for i in range(bands):
            span = slice(i * BAND, (i + 1) * BAND)
            flag = flags[1, span, :]
            held, keys = value[span, lanes], key[span, lanes]
            key_back = ubuf[0, span, lanes] + flag * (
                dot(held, back_high, True) + dot(held, back_low, True) + totals
            )
            pre = acc[span, lanes]
            slope = jnp.where(pre > 0, 1.0, jnp.exp(jnp.minimum(pre, 0.0)))
            big[1, span, lanes] = (key_back * slope).astype(bf16)
            value_back = ubuf[1, span, lanes] + flag * (dot(keys, back_high) + dot(keys, back_low))
            big[2, span, lanes] = value_back.astype(bf16)
            big[0, span, lanes] = dq_low[span, lanes]
            big[3, span, lanes] = da[span, lanes]
        for index in range(3):
            total = jnp.sum(big[index, :, lanes].astype(f32), axis=0, keepdims=True)
            gs[4 + index : 5 + index, lanes] = total
        return carry

    lax.fori_loop(0, pairs, attend_close, 0)
    w_loads[0, 0] = load(w_ref.at[0], wbuf.at[0])
    w_loads[0, 1] = load(w_ref.at[1], wbuf.at[1])
    step = sums.total - count
    for j in range(3):
        tick(step)
        step += 1
        w_loads[0, j].wait()

        def input_back(i, carry):
            span = band_span(i)
            back = dot(big[j, span, :], unit_of(j % 2), True)
            acc[span, :] = back if j == 0 else acc[span, :] + back
            return carry

        lax.fori_loop(0, bands, input_back, 0)
        if j == 0:
            w_loads[0, 2] = load(w_ref.at[2], wbuf.at[0])

    def outer_back(i, carry):
        span = band_span(i)
        upstream = acc[span, :]
        back, unit = norm_back(x_ref[span, :].astype(f32), upstream, rows_ref[0:1, :])
        add_row(0, upstream * unit)
        add_row(1, upstream)
        grad_ref[span, :] = grad_ref[span, :] + back
        return carry

    lax.fori_loop(0, bands, outer_back, 0)
    small, tail = [], []
    if aligned:
        share_rows = 13 * 1024 // 128 // (count * 2)
        for j in range(13 * 8):
            sm_send[j // share_rows, j % share_rows : j % share_rows + 1, :] = gs[
                j // 8 : j // 8 + 1, (j % 8) * 128 : (j % 8 + 1) * 128
            ]
        seqs = [lax.rem(z + k, count) * 2 + x for k in range(1, count)]
        seqs += [lax.rem(z + k, count) * 2 + 1 - x for k in range(count)]
        for k, (peer, there) in enumerate(zip(straight + far, seqs)):
            small.append(remote(sm_send.at[there], sm_recv.at[k], ms.at[k], mr.at[k], peer))
            small[-1].start()
    while step < sums.total:
        tick(step)
        step += 1
    last = sums.total + 4
    if aligned:
        total = sm_send[z * 2 + x]
        for k, copy in enumerate(small):
            copy.wait_recv()
            total = total + sm_recv[k]
        sm_part[0] = total
        for j in range(2):
            index = len(small) + j
            copy = remote(sm_part.at[j], sm_pair.at[j], ms.at[index], mr.at[index], pair[1 + j])
            copy.start()
            tail.append(copy)
            tick(step)
            step += 1
            copy.wait_recv()
            if j == 0:
                sm_part[1] = sm_part[0] + sm_pair[0]
            else:
                small_out[...] = sm_part[1] + sm_pair[1]
    else:
        small_out[...] = gs[...]
    while step < last:
        tick(step)
        step += 1
    sums.wait_sends()
    relay.wait_sends()
    for copy in small + tail:
        copy.wait_send()


def backward(x, dy, w, rows, low, pre, ratio, left, resid, up, act, state, lengths, order, nseq, aligned):
    group, width = x.shape
    count, batches = nseq // 2, 3
    share_rows = width // nseq
    steps = batches * count
    f32, bf16 = jnp.float32, jnp.bfloat16
    V, S, R = pltpu.VMEM, jax.ShapeDtypeStruct, pltpu.SemaphoreType.REGULAR
    smem = pl.BlockSpec(memory_space=pltpu.SMEM)
    message = (2, 264, PAIR)
    blocks = up.shape[0]
    piece = (share_rows, width)
    small = (16, 128)
    return pl.pallas_call(
        functools.partial(backward_kernel, count, aligned),
        out_shape=(
            S((group, width), f32),
            S((batches,) + piece, f32),
            S(small if aligned else (16, width), f32),
        ),
        in_specs=[VMEM, VMEM, ANY, VMEM] + [ANY] * 7 + [VMEM, smem, smem],
        out_specs=[VMEM, VMEM, VMEM],
        scratch_shapes=[
            V((2, 2, 2, 2) + piece, bf16),
            V((2, 2, 2, 2) + piece, bf16),
            V((2, 2) + piece, f32),
            V((3, 2, 2) + piece, bf16),
            V((4, 2, 2) + piece, bf16),
            V((2,) + piece, f32),
            V((3, 2) + piece, bf16),
            V((4, 2) + piece, bf16),
            V(piece, f32),
            V((count - 1, 2) + piece, bf16),
            V((batches, count - 1, 2) + piece, bf16),
            V((blocks, group, width), bf16),
            V((2, blocks, 2 * share_rows, group), bf16),
            V((2, width // group, group, width), bf16),
            V((2, group, width), f32),
            V((group, width), f32),
            V((group, width), bf16),
            V((group, width), bf16),
            V((group, width), bf16),
            V((group, width), f32),
            V((group, group), f32),
            V((2, group, PAIR), f32),
            V((16, width), f32),
            V(message, f32),
            V(message, f32),
            V(message[1:], f32),
            V((count - 1,) + message[1:], f32),
            V(message, f32),
            V(message, f32),
            V((nseq,) + small, f32),
            V((nseq - 1,) + small, f32),
            V((2,) + small, f32),
            V((2,) + small, f32),
            DMA((32,)),
            DMA((steps,)),
            DMA((steps,)),
            DMA((steps,)),
            DMA((steps,)),
            DMA((steps,)),
            DMA((steps,)),
            DMA((steps,)),
            DMA((batches, count - 1)),
            DMA((batches, count - 1)),
            R,
            R((2,)),
            R((2,)),
            DMA((count + 1,)),
            DMA((count + 1,)),
            DMA((nseq + 1,)),
            DMA((nseq + 1,)),
        ],
        compiler_params=pltpu.CompilerParams(
            collective_id=1, has_side_effects=True, vmem_limit_bytes=VMEM_LIMIT
        ),
    )(x, dy, w.reshape(-1, width // group, group, width), rows, low, pre, ratio, left, resid, up, act, state, lengths, order)


STEP = 10


def padded(vector):
    short = 2048 - vector.shape[-1]
    edges = [(0, 0)] * (vector.ndim - 1) + [(0, short)]
    return jnp.pad(vector, edges).reshape(vector.shape[:-1] + (16, 128))


def local(
    tokens, cotangent, lengths, order, weights, momentum, small_params, moment_one, moment_two
):
    width = tokens.shape[2]
    nseq = lax.axis_size("seq")
    share = small_params.shape[0]
    rounded = lax.reduce_precision(small_params, 8, 7)
    aligned = share % 128 == 0
    if aligned:
        shared = padded(rounded)
    else:
        shared = lax.all_gather(rounded, "seq", axis=0, tiled=True).reshape(-1, width)
    (gathered, block_out, rows, *kept) = forward(
        tokens[0], weights, shared, lengths, order, nseq, aligned
    )
    input_grad, sums, row_small = backward(
        tokens[0], cotangent[0], gathered, rows, *kept, lengths, order, nseq, aligned
    )
    if aligned:
        row_small = row_small.reshape(2048)[:share]
    else:
        row_small = lax.psum_scatter(
            row_small[:13].reshape(-1), "seq", scatter_dimension=0, tiled=True
        )
        row_small = lax.psum(row_small, "stream")
    row_units, update = muon(sums, momentum, nseq)
    new_momentum = 0.5 * momentum + row_units
    blocks = (weights.shape[0] - 4) // 2
    rates = jnp.array([0.5] * 3 + [4.0] + [0.5] * blocks + [0.25] * blocks, dtype=jnp.float32)
    new_weights = weights - rates[:, None, None] * (update.astype(jnp.float32) + 0.01 * weights)
    first_new = 0.9 * moment_one + 0.1 * row_small
    second_new = 0.95 * moment_two + 0.05 * row_small * row_small
    adjusted = first_new / (1.0 - 0.9**STEP) / (jnp.sqrt(second_new / (1.0 - 0.95**STEP)) + 1e-08)
    new_small = small_params - 0.05 * (adjusted + 0.01 * small_params)
    return (
        block_out[None], input_grad[None], new_weights, new_momentum, new_small, first_new, second_new,
    )


def solution(mesh):
    in_specs = (
        P("stream", "seq", None),
        P("stream", "seq", None),
        P("stream", None),
        P("stream", None),
        P(None, "seq", None),
        P(None, "seq", None),
        P("seq"),
        P("seq"),
        P("seq"),
    )
    out_specs = (
        P("stream", "seq", None),
        P("stream", "seq", None),
        P(None, "seq", None),
        P(None, "seq", None),
        P("seq"),
        P("seq"),
        P("seq"),
    )
    return jax.shard_map(local, mesh=mesh, in_specs=in_specs, out_specs=out_specs, check_vma=False)
```

```python
import functools

import jax
import jax.numpy as jnp
from jax import lax
from jax.experimental import pallas as pl
from jax.experimental.pallas import tpu as pltpu
from jax.sharding import PartitionSpec as P

MESH = pl.DeviceIdType.MESH
DMA = pltpu.SemaphoreType.DMA
ANY = pl.BlockSpec(memory_space=pl.ANY)
VMEM = pl.BlockSpec(memory_space=pltpu.VMEM)
VMEM_LIMIT = 62 << 20


def places():
    seq = lax.axis_index("seq")
    stream = lax.axis_index("stream")
    return seq // 2, seq % 2, stream // 2, stream % 2


def device(z, x, y, c):
    return {"seq": z * 2 + x, "stream": y * 2 + c}


def greet(peers):
    barrier = pltpu.get_barrier_semaphore()
    for peer in peers:
        pl.semaphore_signal(barrier, inc=1, device_id=peer, device_id_type=MESH)
    pl.semaphore_wait(barrier, len(peers))


def remote(source, target, sent, received, peer):
    return pltpu.make_async_remote_copy(
        src_ref=source,
        dst_ref=target,
        send_sem=sent,
        recv_sem=received,
        device_id=peer,
        device_id_type=MESH,
    )


def others_along_seq(z, x, y, c, count):
    straight = [device(lax.rem(z + k, count), x, y, c) for k in range(1, count)]
    across = [device(lax.rem(z + k, count), 1 - x, y, c) for k in range(count)]
    return straight, across


CHUNK = 32


SHIFTS = (0.0, 0.0, 0.1, 0.7, 0.7)
FINE = (False, False, False, False, True)
BAND = 256


def split_two(values):
    high = values.astype(jnp.bfloat16)
    return high, (values - high.astype(jnp.float32)).astype(jnp.bfloat16)


def dot(left, right, transposed=False):
    dims = (((1,), (1 if transposed else 0,)), ((), ()))
    return lax.dot_general(left, right, dims, preferred_element_type=jnp.float32)


def orthogonalize(full, xh, xl, gram, gram_low):
    size = full.shape[0]
    bands = size // BAND

    def span(index):
        return pl.ds(pl.multiple_of(index * BAND, BAND), BAND)

    def square(index, total):
        part = full[span(index), :]
        return total + jnp.sum(part * part)

    norm = jnp.sqrt(lax.fori_loop(0, bands, square, jnp.float32(0.0)))
    scale = 1.0 / (norm + 1e-07)

    def begin(index, carry):
        part = full[span(index), :] * scale
        full[span(index), :] = part
        xh[0, span(index), :] = part.astype(jnp.bfloat16)
        return carry

    lax.fori_loop(0, bands, begin, 0)
    for turn in range(len(SHIFTS)):
        shift, fine = SHIFTS[turn], FINE[turn]
        now, later = turn % 2, 1 - turn % 2
        more = turn + 1 < len(SHIFTS) and FINE[turn + 1]

        def form(index, carry):
            rows = span(index)
            left = xh[now, rows, :]
            block = dot(left, xh[now], True)
            if fine:
                block += dot(left, xl[now], True) + dot(xl[now, rows, :], xh[now], True)
            if shift:
                across = lax.broadcasted_iota(jnp.int32, block.shape, 1)
                down = lax.broadcasted_iota(jnp.int32, block.shape, 0) + index * BAND
                block = jnp.where(across == down, block - shift, block)
            gram[rows, :] = block
            gram_low[rows, :] = block.astype(jnp.bfloat16)
            return carry

        lax.fori_loop(0, bands, form, 0)
        linear = -4.775 + 2.0 * 2.0315 * shift
        scaled = 3.4445 - 4.775 * shift + 2.0315 * shift * shift

        def advance(index, carry):
            rows = span(index)
            poly = linear * gram[rows, :] + 2.0315 * dot(gram_low[rows, :], gram_low[...])
            if fine:
                high, low = split_two(poly)
                step = dot(high, xh[now]) + dot(high, xl[now]) + dot(low, xh[now])
            else:
                step = dot(poly.astype(jnp.bfloat16), xh[now])
            moved = scaled * full[rows, :] + step
            full[rows, :] = moved
            if more:
                high, low = split_two(moved)
                xh[later, rows, :] = high
                xl[later, rows, :] = low
            else:
                xh[later, rows, :] = moved.astype(jnp.bfloat16)
            return carry

        lax.fori_loop(0, bands, advance, 0)
    return len(SHIFTS) % 2


def muon_kernel(
    count, g_ref, mom_ref, all_ref, rows_ref,
    mom_own, moved, full, xh, xl, gram, gram_low,
    load_sem, own_sem, ms, mr, ys, yr, os_, or_, fs, fr, gs, gr,
):
    z, x, y, c = places()
    seq = z * 2 + x
    nseq = count * 2
    batches, rows, width = g_ref.shape
    straight, across = others_along_seq(z, x, y, c, count)
    pair = [device(z, x, 1 - y, c), device(z, x, y, 1 - c)]
    greet(straight + across + pair)
    load = pltpu.make_async_copy(mom_ref.at[:, y, c], mom_own, load_sem)
    load.start()
    keep = pltpu.make_async_copy(g_ref, all_ref.at[:, y, c], own_sem.at[0])
    keep.start()
    load.wait()
    owner = [2 * b + c + 1 for b in range(batches)]

    def block(where):
        return full.at[pl.ds(pl.multiple_of(where * rows, rows), rows)]

    for b in range(batches):
        for j in range(rows // CHUNK):
            span = slice(j * CHUNK, (j + 1) * CHUNK)
            moved[b, span, :] = 0.5 * mom_own[b, span, :] + g_ref[b, span, :]

        @pl.when(seq != owner[b])
        def _():
            remote(
                moved.at[b], block(seq), ms.at[b], mr.at[seq],
                {"seq": owner[b], "stream": y * 2 + c},
            ).start()

        @pl.when(seq == owner[b])
        def _():
            pltpu.make_async_copy(moved.at[b], block(seq), own_sem.at[1]).start()

    over = remote(g_ref, all_ref.at[:, y, c], ys.at[0], yr.at[0], pair[0])
    over.start()
    is_owner = (seq == owner[0]) | (seq == owner[1]) | (seq == owner[2])

    @pl.when(is_owner)
    def _():
        pltpu.make_async_copy(moved.at[0], block(seq), own_sem.at[1]).wait()
        for k in range(1, nseq):
            there = lax.rem(seq + k, nseq)
            remote(moved.at[0], block(there), ms.at[0], mr.at[there], pair[0]).wait_recv()
        orthogonalize(full, xh, xl, gram, gram_low)

    final = len(SHIFTS) % 2

    def result(where):
        return xh.at[final, pl.ds(pl.multiple_of(where * rows, rows), rows)]

    for b in range(batches):
        target = rows_ref.at[b, y, c]

        @pl.when(seq == owner[b])
        def _():
            pltpu.make_async_copy(result(seq), target, own_sem.at[2]).start()
            for k in range(1, nseq):
                there = lax.rem(seq + k, nseq)
                remote(
                    result(there), target, os_.at[k - 1], or_.at[b],
                    {"seq": there, "stream": y * 2 + c},
                ).start()

    keep.wait()
    over.wait_recv()
    share = remote(all_ref.at[:, :, c], all_ref.at[:, :, c], ys.at[1], yr.at[1], pair[1])
    share.start()
    hops = []
    for b in range(batches):
        target = rows_ref.at[b, y, c]

        @pl.when(seq == owner[b])
        def _():
            pltpu.make_async_copy(result(seq), target, own_sem.at[2]).wait()

        @pl.when(seq != owner[b])
        def _():
            remote(result(seq), target, os_.at[0], or_.at[b], pair[0]).wait_recv()

        hop = remote(target, target, fs.at[b], fr.at[b], pair[0])
        hop.start()
        hops.append(hop)
    lasts = []
    for b in range(batches):
        hops[b].wait_recv()
        target = rows_ref.at[b, :, c]
        last = remote(target, target, gs.at[b], gr.at[b], pair[1])
        last.start()
        lasts.append(last)
    for last in lasts:
        last.wait_recv()
    share.wait_recv()
    for copy in [over, share] + hops + lasts:
        copy.wait_send()
    for b in range(batches):

        @pl.when(seq != owner[b])
        def _():
            remote(moved.at[b], block(seq), ms.at[b], mr.at[seq], pair[0]).wait_send()

        @pl.when(seq == owner[b])
        def _():
            for k in range(1, nseq):
                there = lax.rem(seq + k, nseq)
                remote(result(there), rows_ref.at[b, y, c], os_.at[k - 1], or_.at[b], pair[0]).wait_send()


def muon(sums, momentum, nseq):
    count = nseq // 2
    batches, rows, width = sums.shape
    units = momentum.shape[0]
    f32, bf16 = jnp.float32, jnp.bfloat16
    V = pltpu.VMEM
    whole, ortho = pl.pallas_call(
        functools.partial(muon_kernel, count),
        out_shape=(
            jax.ShapeDtypeStruct((batches, 2, 2, rows, width), f32),
            jax.ShapeDtypeStruct((batches, 2, 2, rows, width), bf16),
        ),
        in_specs=[VMEM, ANY],
        out_specs=[ANY, ANY],
        scratch_shapes=[
            V((batches, rows, width), f32),
            V((batches, rows, width), f32),
            V((width, width), f32),
            V((2, width, width), bf16),
            V((2, width, width), bf16),
            V((width, width), f32),
            V((width, width), bf16),
            DMA,
            DMA((3,)),
            DMA((batches,)),
            DMA((nseq,)),
            DMA((2,)),
            DMA((2,)),
            DMA((nseq - 1,)),
            DMA((batches,)),
            DMA((batches,)),
            DMA((batches,)),
            DMA((batches,)),
            DMA((batches,)),
        ],
        compiler_params=pltpu.CompilerParams(
            collective_id=2, has_side_effects=True, vmem_limit_bytes=VMEM_LIMIT
        ),
    )(sums, momentum.reshape(batches, 2, 2, rows, width))
    return whole.reshape(units, rows, width), ortho.reshape(units, rows, width)


HALF = 64
PAIR = 128


def matrix(w_ref, batch, index):
    block = w_ref[batch, index // 2, index % 2]
    return block.reshape(block.shape[0] * block.shape[1] * block.shape[2], block.shape[3])


def norm_rows(values, gain, offset):
    center = values - jnp.mean(values, axis=-1, keepdims=True)
    spread = jnp.mean(center * center, axis=-1, keepdims=True)
    return center * lax.rsqrt(spread + 1e-05) * gain + offset


def lanes_of(head):
    lane = lax.broadcasted_iota(jnp.int32, (1, PAIR), 1)
    return (lane // HALF) == head


def block_diagonal():
    row = lax.broadcasted_iota(jnp.int32, (PAIR, PAIR), 0)
    lane = lax.broadcasted_iota(jnp.int32, (PAIR, PAIR), 1)
    return (row // HALF) == (lane // HALF)


def pair_span(index):
    return pl.ds(pl.multiple_of(index * PAIR, PAIR), PAIR)


def band_span(index):
    return pl.ds(pl.multiple_of(index * BAND, BAND), BAND)


def dot_down(left, right):
    return lax.dot_general(left, right, (((0,), (0,)), ((), ())), preferred_element_type=jnp.float32)


def pack_message(left_ref, right_ref, scale_ref, row_ref, message):
    diagonal = block_diagonal()
    for j in range(4):
        parts = []
        for p in (2 * j, 2 * j + 1):
            lanes = slice(p * PAIR, (p + 1) * PAIR)
            scale = scale_ref[...]
            left = (left_ref[:, lanes].astype(jnp.float32) * scale).astype(jnp.bfloat16)
            parts.append(dot_down(left, right_ref[:, lanes]))
            if row_ref is None:
                total = jnp.sum(left.astype(jnp.float32), axis=0, keepdims=True)
            else:
                total = jnp.sum(left.astype(jnp.float32) * row_ref[:, lanes], axis=0, keepdims=True)
            for half in range(2):
                message[half, 256 + p : 257 + p, :] = total
        block = jnp.where(diagonal, parts[0], pltpu.roll(parts[1], HALF, 1))
        message[j // 2, (j % 2) * PAIR : (j % 2 + 1) * PAIR, :] = block


def unpack_message(message, p):
    diagonal = block_diagonal()
    j = p // 2
    block = message[j // 2, (j % 2) * PAIR : (j % 2 + 1) * PAIR, :]
    if p % 2:
        block = pltpu.roll(block, HALF, 1)
    block = jnp.where(diagonal, block, 0.0)
    row = message[0, 256 + p : 257 + p, :]
    column = jnp.transpose(jnp.broadcast_to(row, (PAIR, PAIR)))
    return block, jnp.where(diagonal, column, 0.0)


class Relay:
    def __init__(self, count, coef, own, across, part, spread, total, result, sems, places_):
        self.count, self.coef, self.own, self.across = count, coef, own, across
        self.part, self.spread, self.total, self.result = part, spread, total, result
        self.send, self.recv = sems
        self.z, self.x, self.y, self.c = places_
        self.pair = device(self.z, 1 - self.x, self.y, self.c)

    def swap(self):
        self.first = remote(self.own, self.across, self.send.at[0], self.recv.at[0], self.pair)
        self.first.start()

    def spread_out(self):
        self.first.wait_recv()
        self.part[...] = self.coef[0] * self.own[self.x] + self.coef[1] * self.across[self.x]
        self.copies = []
        for k in range(1, self.count):
            peer = device(lax.rem(self.z + k, self.count), self.x, self.y, self.c)
            copy = remote(self.part, self.spread.at[k - 1], self.send.at[k], self.recv.at[k], peer)
            copy.start()
            self.copies.append(copy)

    def join(self):
        total = jnp.zeros_like(self.part)
        for k, copy in enumerate(self.copies):
            copy.wait_recv()
            total = total + self.coef[4 + k] * self.spread[k]
        self.total[self.x] = total
        half = self.total.at[self.x]
        self.last = remote(half, half, self.send.at[self.count], self.recv.at[self.count], self.pair)
        self.last.start()

    def finish(self):
        self.last.wait_recv()
        for half in range(2):
            self.result[half] = self.coef[2] * self.total[half] + self.coef[3] * self.across[half]

    def wait_sends(self):
        for copy in [self.first, self.last] + self.copies:
            copy.wait_send()


def head_scores(q_ref, k_ref, keep_ref, lanes, head, band):
    rows = slice(band * BAND, (band + 1) * BAND)
    upto = slice(0, (band + 1) * BAND)
    query = jnp.where(lanes_of(head), q_ref[rows, lanes], 0)
    return dot(query, k_ref[upto, lanes], True) * keep_ref[rows, upto]


def attend_pair(p, q_ref, k_ref, v_ref, keep_ref, num_ref, den_ref):
    lanes = pair_span(p)
    group = q_ref.shape[0]
    value = v_ref[:, lanes]
    first = lanes_of(0)
    for band in range(group // BAND):
        rows = slice(band * BAND, (band + 1) * BAND)
        sums, totals = [], []
        for head in range(2):
            scores = head_scores(q_ref, k_ref, keep_ref, lanes, head, band)
            totals.append(jnp.sum(scores, axis=1, keepdims=True))
            sums.append(dot(scores.astype(jnp.bfloat16), value[: (band + 1) * BAND]))
        num_ref[rows, lanes] = jnp.where(first, sums[0], sums[1])
        den_ref[rows, lanes] = jnp.where(first, totals[0], totals[1])


def image_ends(lengths_ref, order_ref):
    images = lengths_ref.shape[1]
    ends, running = [], jnp.int32(0)
    for j in range(images):
        for i in range(images):
            running = running + jnp.where(order_ref[0, j] == i, lengths_ref[0, i], 0)
        ends.append(running)
    return ends


def segment_at(ends, positions):
    found = jnp.zeros_like(positions)
    for end in ends:
        found = found + jnp.where(positions >= end, 1, 0)
    return found


def same(left, right):
    return jnp.where(left == right, 1.0, 0.0)


def fill_masks(ends, start, group, keep_ref, flags_ref):
    for band in range(group // BAND):
        rows = slice(band * BAND, (band + 1) * BAND)
        down = lax.broadcasted_iota(jnp.int32, (BAND, group), 0) + band * BAND
        along = lax.broadcasted_iota(jnp.int32, (BAND, group), 1)
        mine = segment_at(ends, down + start)
        theirs = segment_at(ends, along + start)
        keep_ref[rows, :] = jnp.where(along <= down, same(mine, theirs), 0.0)
        narrow = mine[:, :PAIR]
        flags_ref[0, rows, :] = same(narrow, segment_at(ends, start - 1))
        flags_ref[1, rows, :] = same(narrow, segment_at(ends, start + group - 1))


def pass_at(ends, block, group):
    return same(segment_at(ends, block * group + group - 1), segment_at(ends, block * group - 1))


def forward_factors(ends, group, count, z, x):
    both = [pass_at(ends, 2 * z, group), pass_at(ends, 2 * z + 1, group)]
    near = [jnp.where(x == 0, both[1], 1.0), jnp.where(x == 0, 1.0, both[1])]
    near += [jnp.where(x == 0, 1.0, both[0]), jnp.where(x == 0, 0.0, 1.0)]
    running, far = jnp.float32(1.0), []
    for k in range(1, count):
        far.append(jnp.where(z - k >= 0, running, 0.0))
        there = jnp.maximum(z - k, 0)
        running = running * pass_at(ends, 2 * there, group) * pass_at(ends, 2 * there + 1, group)
    return near + far


def backward_factors(ends, group, count, z, x):
    both = [pass_at(ends, 2 * z, group), pass_at(ends, 2 * z + 1, group)]
    near = [jnp.where(x == 0, 1.0, both[0]), jnp.where(x == 0, both[0], 1.0)]
    near += [jnp.where(x == 0, both[1], 1.0), jnp.where(x == 0, 1.0, 0.0)]
    running, ahead = jnp.float32(1.0), []
    for k in range(1, count):
        ahead.append(jnp.where(z + k < count, running, 0.0))
        there = jnp.minimum(z + k, count - 1)
        running = running * pass_at(ends, 2 * there, group) * pass_at(ends, 2 * there + 1, group)
    return near + ahead[::-1]


def forward_kernel(
    count, aligned, x_ref, w_ref, small_ref, lengths_ref, order_ref,
    w_out, out_ref, rows_ref, low_ref, pre_ref, ratio_ref, left_ref, resid_ref, up_ref, act_ref, state_ref,
    w_all, stage, small_in, keep, flags, h1, q, k, v, num, den, o, resid, h2, act, turned, act_turned, message, across, part, spread, total_ref, state,
    load_sem, out_sem, zs, zr, ps, pr, ss, sr, rs, rr,
):
    z, x, y, c = places()
    straight, far = others_along_seq(z, x, y, c, count)
    pair = [device(z, 1 - x, y, c), device(z, x, 1 - y, c), device(z, x, y, 1 - c)]
    batches = w_ref.shape[0]
    rows, width = w_ref.shape[3:]
    group = x_ref.shape[0]
    bands = group // BAND
    loads = []
    for b in range(batches):
        for i in range(4):
            copy = pltpu.make_async_copy(
                w_ref.at[b, i // 2, i % 2],
                stage.at[b, pl.ds(i * rows, rows)],
                load_sem.at[b, i],
            )
            copy.start()
            loads.append(copy)
    greet(straight + far + pair[1:])
    small = []
    if aligned:
        for j, peer in enumerate(straight + far):
            small.append(remote(small_ref, small_in.at[z * 2 + x], ss.at[j], sr.at[j], peer))
            small[-1].start()
        small_in[z * 2 + x] = small_ref[...]
    spread_w = {}

    def cast_own(b):
        for i in range(4):
            loads[b * 4 + i].wait()
            for j in range(rows // CHUNK):
                span = slice(j * CHUNK, (j + 1) * CHUNK)
                at = slice(i * rows + j * CHUNK, i * rows + (j + 1) * CHUNK)
                w_all[b, i // 2, i % 2, z, x, span, :] = stage[b, at, :].astype(jnp.bfloat16)

    def send_own(b):
        for j in range(1, count):
            block = w_all.at[b, y, c, z, x]
            spread_w[b, j] = remote(block, block, zs.at[b, j - 1], zr.at[b, j - 1], straight[j - 1])
            spread_w[b, j].start()

    first, second, third, outs, waited = [], [], [], [], []
    plan = [(b, 0) for b in range(batches)]
    plan += [(b, j) for b in range(batches) for j in range(1, count)]
    total = len(plan)

    def send(kept, phase, index, block, peer):
        kept.append(remote(block, block, ps.at[phase, index], pr.at[phase, index], peer))
        kept[-1].start()

    def put_out(source, target):
        copy = pltpu.make_async_copy(source, target, out_sem.at[len(outs)])
        copy.start()
        outs.append(copy)
        return copy

    def tick(step):
        index = step
        if index < total:
            b, j = plan[index]
            there = lax.rem(z - j + count, count)
            if j:
                spread_w[b, j].wait_recv()
            send(first, 0, index, w_all.at[b, y, c, there, x], pair[(j + b) % 2 if j else 0])
            if j == min(1, count - 1) and b + 1 < batches:
                send_own(b + 1)
        index = step - 1
        if 0 <= index < total:
            b, j = plan[index]
            there = lax.rem(z - j + count, count)
            first[index].wait_recv()
            if j == 0:
                send(second, 1, index, w_all.at[b, y, c, z, 1 - x], pair[1])
            elif (j + b) % 2 == 0:
                send(second, 1, index, w_all.at[b, y, c, there], pair[1])
            else:
                send(second, 1, index, w_all.at[b, :, c, there, x], pair[0])
        index = step - 2
        if 0 <= index < total:
            b, j = plan[index]
            there = lax.rem(z - j + count, count)
            second[index].wait_recv()
            block = w_all.at[b, :, c, z, 1 - x] if j == 0 else w_all.at[b, :, c, there]
            send(third, 2, index, block, pair[2])
        index = step - 3
        if 0 <= index < total:
            b, j = plan[index]
            there = lax.rem(z - j + count, count)
            third[index].wait_recv()
            put_out(w_all.at[b, :, :, there], w_out.at[b, :, :, there])

    cast_own(0)
    send_own(0)
    tick(0)
    for b in range(1, batches):
        cast_own(b)
        tick(b)
    if aligned:
        for copy in small:
            copy.wait_recv()
        share_rows = 13 * 1024 // 128 // (count * 2)
        for j in range(13 * 8):
            rows_ref[j // 8 : j // 8 + 1, (j % 8) * 128 : (j % 8 + 1) * 128] = small_in[
                j // share_rows, j % share_rows : j % share_rows + 1, :
            ]
    else:
        rows_ref[0:13, :] = small_ref[...]

    def vector(index):
        return rows_ref[index : index + 1, :]

    def norm_one(i, carry):
        span = band_span(i)
        value = norm_rows(x_ref[span, :].astype(jnp.float32), vector(0), vector(1))
        h1[span, :] = value.astype(jnp.bfloat16)
        turned[0, :, span] = jnp.transpose(value).astype(jnp.bfloat16)
        return carry

    lax.fori_loop(0, bands, norm_one, 0)
    ends = image_ends(lengths_ref, order_ref)
    fill_masks(ends, (z * 2 + x) * group, group, keep, flags)
    factors = forward_factors(ends, group, count, z, x)
    ready = batches + count - 1 + 3
    for step in range(batches, ready):
        tick(step)

    def project(i, carry):
        span = band_span(i)
        left = h1[span, :]
        for index, low in ((0, q), (1, k)):
            pre = dot(left, matrix(w_all, 0, index)) + vector(4 + index)
            stage[index, span, :] = pre
            low[span, :] = jnp.where(pre > 0, pre + 1.0, jnp.exp(jnp.minimum(pre, 0.0))).astype(jnp.bfloat16)
        v[span, :] = (dot(left, matrix(w_all, 0, 2)) + vector(6)).astype(jnp.bfloat16)
        return carry

    lax.fori_loop(0, bands, project, 0)
    pack_message(k, v, flags.at[1], None, message)
    relay = Relay(count, factors, message, across, part, spread, total_ref, state, (rs, rr), (z, x, y, c))
    relay.swap()
    stored = [put_out(stage.at[0], pre_ref.at[0]), put_out(stage.at[1], pre_ref.at[1]), None]
    for index, low in enumerate((q, k, v)):
        put_out(low, low_ref.at[index])

    def attend(p, carry):
        attend_pair(p, q, k, v, keep, num, den)
        return carry

    pairs = width // PAIR
    step = ready
    lax.fori_loop(0, pairs // 4, attend, 0)
    tick(step)
    relay.spread_out()
    lax.fori_loop(pairs // 4, pairs // 2, attend, 0)
    tick(step + 1)
    lax.fori_loop(pairs // 2, pairs, attend, 0)
    relay.join()
    tick(step + 2)
    relay.finish()
    put_out(state, state_ref)
    for p in range(pairs):
        block, column = unpack_message(state, p)
        high, low = split_two(jnp.concatenate([block, column], axis=1))
        lanes = slice(p * PAIR, (p + 1) * PAIR)
        for i in range(bands):
            span = slice(i * BAND, (i + 1) * BAND)
            query = q[span, lanes]
            both = dot(query, high) + dot(query, low)
            flag = flags[0, span, :]
            top = num[span, lanes] + flag * both[:, :PAIR]
            bottom = den[span, lanes] + flag * both[:, PAIR:]
            num[span, lanes] = top
            den[span, lanes] = bottom
            o[span, lanes] = (top / bottom).astype(jnp.bfloat16)
    put_out(num, ratio_ref.at[0])
    put_out(den, ratio_ref.at[1])

    def close(i, carry):
        span = band_span(i)
        value = x_ref[span, :].astype(jnp.float32) + dot(o[span, :], matrix(w_all, 0, 3)) + vector(7)
        resid[span, :] = value
        hidden = norm_rows(value, vector(2), vector(3))
        h2[span, :] = hidden.astype(jnp.bfloat16)
        turned[2, :, span] = jnp.transpose(hidden).astype(jnp.bfloat16)
        turned[1, :, span] = jnp.transpose(o[span, :].astype(jnp.float32)).astype(jnp.bfloat16)
        return carry

    lax.fori_loop(0, bands, close, 0)
    put_out(turned, left_ref)
    put_out(resid, resid_ref)
    step = step + 3
    ready = batches + 2 * (count - 1) + 3
    while step < ready:
        tick(step)
        step += 1
    blocks = act.shape[0]
    turned_out = []
    for j in range(blocks):
        if j > 1:
            turned_out[j - 2].wait()
            waited.append(turned_out[j - 2])
        if stored[j % 3] is not None:
            stored[j % 3].wait()
            waited.append(stored[j % 3])

        def expand(i, carry):
            span = band_span(i)
            pre = dot(h2[span, :], matrix(w_all, 1, j)) + vector(9 + j)
            stage[j % 3, span, :] = pre
            value = jax.nn.gelu(pre)
            act[j, span, :] = value.astype(jnp.bfloat16)
            act_turned[j % 2, :, span] = jnp.transpose(value).astype(jnp.bfloat16)
            return carry

        lax.fori_loop(0, bands, expand, 0)
        stored[j % 3] = put_out(stage.at[j % 3], up_ref.at[j])
        turned_out.append(put_out(act_turned.at[j % 2], act_ref.at[j]))
        if step < total + 3:
            tick(step)
            step += 1
    while step < total + 3:
        tick(step)
        step += 1

    def project_down(i, carry):
        span = band_span(i)
        value = resid[span, :] + vector(8)
        for j in range(blocks):
            value += dot(act[j, span, :], matrix(w_all, 2, j))
        out_ref[span, :] = value.astype(jnp.bfloat16)
        return carry

    lax.fori_loop(0, bands, project_down, 0)
    for copy in outs:
        if not any(copy is other for other in waited):
            copy.wait()
    for copy in list(spread_w.values()) + first + second + third + small:
        copy.wait_send()
    relay.wait_sends()


def forward(x, weights, small, lengths, order, nseq, aligned):
    group, width = x.shape
    units, rows, _ = weights.shape
    count, batches = nseq // 2, units // 4
    steps = batches * count
    f32, bf16 = jnp.float32, jnp.bfloat16
    V, S = pltpu.VMEM, jax.ShapeDtypeStruct
    blocks = 4
    smem = pl.BlockSpec(memory_space=pltpu.SMEM)
    message = (2, 264, PAIR)
    return pl.pallas_call(
        functools.partial(forward_kernel, count, aligned),
        out_shape=(
            S((batches, 2, 2, count, 2, rows, width), bf16),
            S((group, width), bf16),
            S((16, width), f32),
            S((3, group, width), bf16),
            S((2, group, width), f32),
            S((2, group, width), f32),
            S((3, width, group), bf16),
            S((group, width), f32),
            S((blocks, group, width), f32),
            S((blocks, width, group), bf16),
            S(message, f32),
        ),
        in_specs=[VMEM, ANY, VMEM, smem, smem],
        out_specs=[ANY, VMEM, VMEM] + [ANY] * 8,
        scratch_shapes=[
            V((batches, 2, 2, count, 2, rows, width), bf16),
            V((3, group, width), f32),
            V(((nseq,) if aligned else ()) + small.shape, f32),
            V((group, group), f32),
            V((2, group, PAIR), f32),
            V((group, width), bf16),
            V((group, width), bf16),
            V((group, width), bf16),
            V((group, width), bf16),
            V((group, width), f32),
            V((group, width), f32),
            V((group, width), bf16),
            V((group, width), f32),
            V((group, width), bf16),
            V((blocks, group, width), bf16),
            V((3, width, group), bf16),
            V((2, width, group), bf16),
            V(message, f32),
            V(message, f32),
            V(message[1:], f32),
            V((count - 1,) + message[1:], f32),
            V(message, f32),
            V(message, f32),
            DMA((batches, 4)),
            DMA((steps + 20,)),
            DMA((batches, count - 1)),
            DMA((batches, count - 1)),
            DMA((3, steps)),
            DMA((3, steps)),
            DMA((nseq - 1,)),
            DMA((nseq - 1,)),
            DMA((count + 1,)),
            DMA((count + 1,)),
        ],
        compiler_params=pltpu.CompilerParams(
            collective_id=0, has_side_effects=True, vmem_limit_bytes=VMEM_LIMIT
        ),
    )(x, weights.reshape(batches, 2, 2, rows, width), small, lengths, order)


def gelu_slope(values):
    cube = 0.044715 * values * values
    bend = jnp.tanh(0.7978845608028654 * values * (1.0 + cube))
    return 0.5 * (1.0 + bend) + 0.5 * values * (1.0 - bend * bend) * (
        0.7978845608028654 * (1.0 + 3.0 * cube)
    )


def norm_back(values, upstream, gain):
    center = values - jnp.mean(values, axis=-1, keepdims=True)
    spread = jnp.mean(center * center, axis=-1, keepdims=True)
    scale = lax.rsqrt(spread + 1e-05)
    unit = center * scale
    inner = upstream * gain
    back = inner - jnp.mean(inner, axis=-1, keepdims=True)
    back = scale * (back - unit * jnp.mean(inner * unit, axis=-1, keepdims=True))
    return back, unit


def pick_message(message, p):
    down = pl.ds(pl.multiple_of(((p // 2) % 2) * PAIR, PAIR), PAIR)
    block = message[p // 4, down, :]
    block = jnp.where(p % 2 == 1, pltpu.roll(block, HALF, 1), block)
    block = jnp.where(block_diagonal(), block, 0.0)
    return split_two(block), message[0, pl.ds(256 + p, 1), :]


class Sums:
    def __init__(self, count, place, wide, product, bufs, sems, sums_ref):
        self.count = count
        self.z, self.x, self.y, self.c = z, x, y, c = place
        self.wide, self.product, self.sums_ref = wide, product, sums_ref
        (self.core_out, self.core_in, self.own, self.first_out, self.first_in, self.kept_one,
         self.second_out, self.second_in, self.kept_two, self.far_out, self.far_in) = bufs
        (self.cs, self.cr, self.fs, self.fr, self.es, self.er, self.zs, self.zr,
         self.credit_core, self.credit_first, self.credit_second) = sems
        self.pair = [device(z, 1 - x, y, c), device(z, x, 1 - y, c), device(z, x, y, 1 - c)]
        self.steps = [(b, k) for b in (2, 1, 0) for k in range(count)]
        self.total = len(self.steps)
        self.cores, self.firsts, self.seconds, self.fars = [], [], [], {}
        self.rows = sums_ref.shape[1]
        self.beat = 0
        self.done = {name: 0 for name in "abcde"}
        self.stamp = {}
        self.needs = {"a": (("b", 1),), "b": (("c", 2),), "c": (("d", 2),)}

    def there(self, i):
        return lax.rem(self.z + 1 + self.steps[i][1], self.count)

    def parts(self, i):
        return (0, 1) if self.steps[i][0] in self.wide else (0,)

    def span(self, ref, i):
        return ref if len(self.parts(i)) == 2 else ref.at[pl.ds(0, 1)]

    def far_slots(self, i):
        b, k = self.steps[i]
        before = (self.count - 1) * sum(len(self.parts(j * self.count)) for j in range(2 - b))
        return pl.ds(before + k * len(self.parts(i)), len(self.parts(i)))

    def give(self, semaphore, peer):
        pl.semaphore_signal(semaphore, inc=1, device_id=peer, device_id_type=MESH)

    def take(self, semaphore):
        pl.semaphore_wait(semaphore, 1)

    def store(self, value, targets):
        high = value.astype(jnp.bfloat16)
        targets[0][...] = high
        if len(targets) == 2:
            targets[1][...] = (value - high.astype(jnp.float32)).astype(jnp.bfloat16)

    def add(self, i, base, got, send, keep):
        def body(index, carry):
            at = pl.ds(pl.multiple_of(index * CHUNK, CHUNK), CHUNK)
            value = base[at, :]
            for part in got:
                value = value + part[at, :].astype(jnp.float32)
            if keep is not None:
                keep[at, :] = value
            else:
                self.store(value, [ref.at[at] for ref in send])
            return carry

        lax.fori_loop(0, self.rows // CHUNK, body, 0)

    def stage_a(self, i):
        slot = i % 2
        batch = self.steps[i][0]
        if i >= 2:
            self.cores[i - 2].wait_send()
        for yy in range(2):
            value = self.product(i, batch, yy, 1 - self.c)
            for xx in range(2):
                rows = slice(xx * self.rows, (xx + 1) * self.rows)
                self.store(value[rows], [self.core_out.at[slot, h, yy, xx] for h in self.parts(i)])
        if i >= 2:
            self.take(self.credit_core)
        source, target = self.span(self.core_out.at[slot], i), self.span(self.core_in.at[slot], i)
        self.cores.append(remote(source, target, self.cs.at[i], self.cr.at[i], self.pair[2]))
        self.cores[i].start()
        for yy in range(2):
            value = self.product(i, batch, yy, self.c)
            for xx in range(2):
                self.own[yy, xx] = value[xx * self.rows : (xx + 1) * self.rows]

    def stage_b(self, i):
        slot = i % 2
        k = self.steps[i][1]
        x, y = self.x, self.y
        self.cores[i].wait_recv()
        if i >= 3:
            self.firsts[i - 3].wait_send()
        out = self.first_out.at[i % 3]
        for j in range(2):
            away, near = ((1 - y, j), (y, j)) if k % 2 == 0 else ((j, 1 - x), (j, x))
            for at, send, keep in (
                (away, [out.at[h, j] for h in self.parts(i)], None),
                (near, None, self.kept_one.at[i % 2, j]),
            ):
                got = [self.core_in.at[slot, h, at[0], at[1]] for h in self.parts(i)]
                self.add(i, self.own.at[at[0], at[1]], got, send, keep)
        if i + 2 < self.total:
            self.give(self.credit_core, self.pair[2])
        if i >= 4:
            self.take(self.credit_first.at[i % 2])
        peer = self.pair[1 - k % 2]
        source, target = self.span(out, i), self.span(self.first_in.at[i % 4], i)
        self.firsts.append(remote(source, target, self.fs.at[i], self.fr.at[i], peer))
        self.firsts[i].start()

    def stage_c(self, i):
        k = self.steps[i][1]
        mine = self.x if k % 2 == 0 else self.y
        self.firsts[i].wait_recv()
        if i >= 3:
            self.seconds[i - 3].wait_send()
        out = self.second_out.at[i % 3]
        got = self.first_in.at[i % 4]
        self.add(i, self.kept_one.at[i % 2, 1 - mine], [got.at[h, 1 - mine] for h in self.parts(i)],
                 [out.at[h] for h in self.parts(i)], None)
        self.add(i, self.kept_one.at[i % 2, mine], [got.at[h, mine] for h in self.parts(i)], None, self.kept_two.at[i % 2])
        if i + 4 < self.total:
            self.give(self.credit_first.at[i % 2], self.pair[1 - k % 2])
        if i >= 4:
            self.take(self.credit_second.at[i % 2])
        source, target = self.span(out, i), self.span(self.second_in.at[i % 4], i)
        self.seconds.append(remote(source, target, self.es.at[i], self.er.at[i], self.pair[k % 2]))
        self.seconds[i].start()

    def stage_d(self, i):
        b, k = self.steps[i]
        self.seconds[i].wait_recv()
        got = [self.second_in.at[i % 4, h] for h in self.parts(i)]
        if k < self.count - 1:
            if i >= self.count:
                self.fars[i - self.count].wait_send()
            out = self.far_out.at[k]
            self.add(i, self.kept_two.at[i % 2], got, [out.at[h] for h in self.parts(i)], None)
            peer = device(self.there(i), self.x, self.y, self.c)
            source, target = self.span(out, i), self.far_in.at[self.far_slots(i)]
            self.fars[i] = remote(source, target, self.zs.at[b, k], self.zr.at[b, k], peer)
            self.fars[i].start()
        else:
            self.add(i, self.kept_two.at[i % 2], got, None, self.sums_ref.at[b])
        if i + 4 < self.total:
            self.give(self.credit_second.at[i % 2], self.pair[k % 2])

    def stage_e(self, i):
        b, k = self.steps[i]
        if k < self.count - 1:
            return
        for j in range(self.count - 1):
            self.fars[i - self.count + 1 + j].wait_recv()
            start = self.far_slots(i - self.count + 1 + j).start
            got = [self.far_in.at[start + h] for h in self.parts(i)]
            self.add(i, self.sums_ref.at[b], got, None, self.sums_ref.at[b])

    def run(self, name):
        i = self.done[name]
        for other, back in self.needs.get(name, ()):
            while self.done[other] <= i - back:
                self.run(other)
        getattr(self, "stage_" + name)(i)
        self.done[name] = i + 1
        self.stamp[name, i] = self.beat

    def pump(self, make=False):
        self.beat += 1
        for before, name, lag in (("d", "e", 2), ("c", "d", 2), ("b", "c", 2), ("a", "b", 1)):
            while self.done[name] < self.done[before]:
                if self.beat - self.stamp[before, self.done[name]] < lag:
                    break
                self.run(name)
        if make:
            self.run("a")

    def wait_sends(self):
        for copy in self.cores[-2:] + self.firsts[-3:] + self.seconds[-3:]:
            copy.wait_send()
        for i, copy in self.fars.items():
            if i >= self.total - self.count:
                copy.wait_send()


def backward_kernel(
    count, aligned, x_ref, dy_ref, w_ref, rows_ref, low_ref, pre_ref, ratio_ref, left_ref, resid_ref, up_ref, act_ref,
    state, lengths_ref, order_ref,
    grad_ref, sums_ref, small_out,
    core_out, core_in, own, first_out, first_in, kept_one, second_out, second_in, kept_two, far_out, far_in,
    big, left, wbuf, ubuf, acc, da, dq_low, dnum, dden, keep, flags, gs,
    message, across, part, spread, total_ref, state_back, sm_send, sm_recv, sm_part, sm_pair,
    load_sem, lt_sem, cs, cr, fs, fr, es, er, zs, zr, credit_core, credit_first, credit_second, rs, rr, ms, mr,
):
    place = z, x, y, c = places()
    straight, far = others_along_seq(z, x, y, c, count)
    pair = [device(z, 1 - x, y, c), device(z, x, 1 - y, c), device(z, x, y, 1 - c)]
    group, width = dy_ref.shape
    bands = group // BAND
    pairs = width // PAIR
    block_rows = 2 * sums_ref.shape[1]
    f32, bf16 = jnp.float32, jnp.bfloat16
    issued = []

    def load(source, target):
        copy = pltpu.make_async_copy(source, target, load_sem.at[len(issued)])
        copy.start()
        issued.append(copy)
        return copy

    def load_left(i):
        b = sums.steps[i][0]
        at = pl.ds(pl.multiple_of(sums.there(i) * block_rows, block_rows), block_rows)
        slot = left.at[i % 2]
        if b == 2:
            pieces = [(act_ref.at[:, at], slot)]
        elif b == 1:
            pieces = [(left_ref.at[pl.ds(2, 1), at], slot.at[pl.ds(0, 1)])]
        else:
            pieces = [(left_ref.at[pl.ds(0, 2), at], slot.at[pl.ds(0, 2)])]
        copies = [pltpu.make_async_copy(s, t, lt_sem.at[i]) for s, t in pieces]
        for copy in copies:
            copy.start()
        return copies

    lefts = {}

    def product(i, batch, yy, cc):
        unit = 2 * yy + cc
        if batch == 2:
            lhs, rhs = left[i % 2, unit], dy_ref[...]
        elif batch == 1:
            lhs, rhs = left[i % 2, 0], big[unit]
        else:
            lhs, rhs = left[i % 2, yy * cc], big[unit]
        return dot(lhs, rhs)

    sums = Sums(
        count, place, (0,), product,
        (core_out, core_in, own, first_out, first_in, kept_one, second_out, second_in, kept_two, far_out, far_in),
        (cs, cr, fs, fr, es, er, zs, zr, credit_core, credit_first, credit_second), sums_ref,
    )

    def pump(make=False):
        i = sums.done["a"]
        if make:
            for copy in lefts[i]:
                copy.wait()
            if i + 1 < sums.total:
                lefts[i + 1] = load_left(i + 1)
        sums.pump(make)

    def make_until(limit):
        while sums.done["a"] < limit:
            pump(True)

    lefts[0] = load_left(0)
    blocks = big.shape[0]
    w_loads = {(2, j): load(w_ref.at[8 + j], wbuf.at[j]) for j in range(2)}
    u_loads = {j: load(up_ref.at[j], ubuf.at[j]) for j in range(2)}
    resid_load = load(resid_ref, grad_ref)
    greet(straight + far + pair[1:])
    ends = image_ends(lengths_ref, order_ref)
    fill_masks(ends, (z * 2 + x) * group, group, keep, flags)
    factors = backward_factors(ends, group, count, z, x)
    gs[...] = jnp.zeros_like(gs)

    def add_row(index, value, lanes=slice(None)):
        gs[index : index + 1, lanes] = gs[index : index + 1, lanes] + jnp.sum(
            value.astype(f32), axis=0, keepdims=True
        )

    def unit_of(slot):
        return wbuf[slot].reshape(width, width)

    for i in range(bands):
        add_row(8, dy_ref[i * BAND : (i + 1) * BAND, :])
    for j in range(blocks):
        if j != 2:
            pump(True)
        w_loads[2, j].wait()
        u_loads[j].wait()

        def hidden_back(i, carry):
            span = band_span(i)
            back = dot(dy_ref[span, :], unit_of(j % 2), True)
            back = (back * gelu_slope(ubuf[j % 2, span, :])).astype(bf16)
            big[j, span, :] = back
            add_row(9 + j, back)
            return carry

        lax.fori_loop(0, bands, hidden_back, 0)
        if j + 2 < blocks:
            w_loads[2, j + 2] = load(w_ref.at[8 + j + 2], wbuf.at[j % 2])
            u_loads[j + 2] = load(up_ref.at[j + 2], ubuf.at[j % 2])
        else:
            w_loads[1, j - 2] = load(w_ref.at[4 + j - 2], wbuf.at[j % 2])
            u_loads[j + 2] = load(ratio_ref.at[j - 2], ubuf.at[j % 2])
    for j in range(blocks):
        if j % 2:
            pump(True)
        w_loads[1, j].wait()

        def up_back(i, carry):
            span = band_span(i)
            back = dot(big[j, span, :], unit_of(j % 2), True)
            acc[span, :] = back if j == 0 else acc[span, :] + back
            return carry

        lax.fori_loop(0, bands, up_back, 0)
        if j + 2 < blocks:
            w_loads[1, j + 2] = load(w_ref.at[4 + j + 2], wbuf.at[j % 2])
        elif j + 2 == blocks:
            w_loads[0, 3] = load(w_ref.at[3], wbuf.at[0])
        else:
            low_loads = [load(low_ref.at[0], wbuf.at[1, 0]), load(low_ref.at[1], wbuf.at[1, 1])]
    resid_load.wait()
    w_loads[0, 3].wait()

    def middle_back(i, carry):
        span = band_span(i)
        upstream = acc[span, :]
        back, unit = norm_back(grad_ref[span, :], upstream, rows_ref[2:3, :])
        add_row(2, upstream * unit)
        add_row(3, upstream)
        total = dy_ref[span, :].astype(f32) + back
        grad_ref[span, :] = total
        low = total.astype(bf16)
        da[span, :] = low
        add_row(7, low)
        acc[span, :] = dot(low, unit_of(0), True)
        return carry

    for i in range(bands):
        middle_back(i, 0)
        if i == 0:
            pump(True)
    low_loads.append(load(low_ref.at[2], wbuf.at[0, 0]))
    u_loads[blocks].wait()
    u_loads[blocks + 1].wait()

    def ratio_back(p, carry):
        lanes = pair_span(p)
        first = lanes_of(0)
        for i in range(bands):
            span = slice(i * BAND, (i + 1) * BAND)
            inverse = 1.0 / ubuf[1, span, lanes]
            scaled = acc[span, lanes] * inverse
            dnum[span, lanes] = scaled.astype(bf16)
            weighted = scaled * ubuf[0, span, lanes] * inverse
            one = jnp.sum(jnp.where(first, weighted, 0.0), axis=1, keepdims=True)
            two = jnp.sum(jnp.where(first, 0.0, weighted), axis=1, keepdims=True)
            dden[span, lanes] = -jnp.where(first, one, two)
        return carry

    lax.fori_loop(0, pairs, ratio_back, 0)
    for copy in low_loads:
        copy.wait()
    query, key, value = wbuf.at[1, 0], wbuf.at[1, 1], wbuf.at[0, 0]
    pack_message(query, dnum, flags.at[0], dden, message)
    relay = Relay(count, factors, message, across, part, spread, total_ref, state_back, (rs, rr), place)
    relay.swap()
    pump(True)
    pre_load = load(pre_ref.at[0], acc)
    pre_load.wait()

    def attend_back(p, carry):
        lanes = pair_span(p)
        (state_high, state_low), totals = pick_message(state, p)
        lane = lax.broadcasted_iota(jnp.int32, (1, PAIR), 1) % HALF
        for band in range(bands):
            span = slice(band * BAND, (band + 1) * BAND)
            upto = (band + 1) * BAND
            back = dnum[span, lanes]
            below = dden[span, lanes]
            high, low = split_two(pltpu.roll(below, HALF, 1))
            extra = jnp.where(lane == 0, high, jnp.where(lane == 1, low, jnp.zeros_like(low)))
            asked = query[span, lanes]
            keys = key[0:upto, lanes]
            held = value[0:upto, lanes]
            kept = keep[span, 0:upto]
            found, key_back, value_back = [], 0.0, 0.0
            for head in range(2):
                mine = lanes_of(head)
                masked = jnp.where(mine, asked, 0)
                scores = (dot(masked, keys, True) * kept).astype(bf16)
                scores_back = dot(jnp.where(mine, back, extra), jnp.where(mine, held, 1), True)
                scores_back = (scores_back * kept).astype(bf16)
                found.append(dot(scores_back, keys))
                key_back = key_back + dot_down(scores_back, masked)
                value_back = value_back + dot_down(scores, jnp.where(mine, back, 0))
            across_blocks = dot(back, state_high, True) + dot(back, state_low, True) + below * totals
            query_back = jnp.where(lanes_of(0), found[0], found[1]) + flags[0, span, :] * across_blocks
            pre = acc[span, lanes]
            slope = jnp.where(pre > 0, 1.0, jnp.exp(jnp.minimum(pre, 0.0)))
            dq_low[span, lanes] = (query_back * slope).astype(bf16)
            for index, total in ((0, key_back), (1, value_back)):
                if band:
                    ubuf[index, 0 : upto - BAND, lanes] = (
                        ubuf[index, 0 : upto - BAND, lanes] + total[: upto - BAND]
                    )
                ubuf[index, span, lanes] = total[upto - BAND :]
        return carry

    quarter = pairs // 4
    early = sums.total - count
    for part in range(4):
        lax.fori_loop(part * quarter, (part + 1) * quarter, attend_back, 0)
        if part == 0:
            relay.spread_out()
        elif part == 2:
            relay.join()
        pump(sums.done["a"] < early)
    pre_load = load(pre_ref.at[1], acc)
    make_until(early)
    relay.finish()
    pre_load.wait()

    def attend_close(p, carry):
        lanes = pair_span(p)
        (back_high, back_low), totals = pick_message(state_back, p)
        for i in range(bands):
            span = slice(i * BAND, (i + 1) * BAND)
            flag = flags[1, span, :]
            held, keys = value[span, lanes], key[span, lanes]
            key_back = ubuf[0, span, lanes] + flag * (
                dot(held, back_high, True) + dot(held, back_low, True) + totals
            )
            pre = acc[span, lanes]
            slope = jnp.where(pre > 0, 1.0, jnp.exp(jnp.minimum(pre, 0.0)))
            big[1, span, lanes] = (key_back * slope).astype(bf16)
            value_back = ubuf[1, span, lanes] + flag * (dot(keys, back_high) + dot(keys, back_low))
            big[2, span, lanes] = value_back.astype(bf16)
            big[0, span, lanes] = dq_low[span, lanes]
            big[3, span, lanes] = da[span, lanes]
        for index in range(3):
            total = jnp.sum(big[index, :, lanes].astype(f32), axis=0, keepdims=True)
            gs[4 + index : 5 + index, lanes] = total
        return carry

    lax.fori_loop(0, pairs, attend_close, 0)
    x_load = load(x_ref, dq_low)
    w_loads[0, 0] = load(w_ref.at[0], wbuf.at[0])
    w_loads[0, 1] = load(w_ref.at[1], wbuf.at[1])
    for j in range(3):
        pump(True)
        w_loads[0, j].wait()

        def input_back(i, carry):
            span = band_span(i)
            back = dot(big[j, span, :], unit_of(j % 2), True)
            acc[span, :] = back if j == 0 else acc[span, :] + back
            return carry

        lax.fori_loop(0, bands, input_back, 0)
        if j == 0:
            w_loads[0, 2] = load(w_ref.at[2], wbuf.at[0])

    x_load.wait()

    def outer_back(i, carry):
        span = band_span(i)
        upstream = acc[span, :]
        back, unit = norm_back(dq_low[span, :].astype(f32), upstream, rows_ref[0:1, :])
        add_row(0, upstream * unit)
        add_row(1, upstream)
        grad_ref[span, :] = grad_ref[span, :] + back
        return carry

    lax.fori_loop(0, bands, outer_back, 0)
    small, tail = [], []
    if aligned:
        share_rows = 13 * 1024 // 128 // (count * 2)
        for j in range(13 * 8):
            sm_send[j // share_rows, j % share_rows : j % share_rows + 1, :] = gs[
                j // 8 : j // 8 + 1, (j % 8) * 128 : (j % 8 + 1) * 128
            ]
        seqs = [lax.rem(z + k, count) * 2 + x for k in range(1, count)]
        seqs += [lax.rem(z + k, count) * 2 + 1 - x for k in range(count)]
        for k, (peer, there) in enumerate(zip(straight + far, seqs)):
            small.append(remote(sm_send.at[there], sm_recv.at[k], ms.at[k], mr.at[k], peer))
            small[-1].start()
    make_until(sums.total)
    if aligned:
        total = sm_send[z * 2 + x]
        for k, copy in enumerate(small):
            copy.wait_recv()
            total = total + sm_recv[k]
        sm_part[0] = total
        for j in range(2):
            index = len(small) + j
            copy = remote(sm_part.at[j], sm_pair.at[j], ms.at[index], mr.at[index], pair[1 + j])
            copy.start()
            tail.append(copy)
            pump()
            copy.wait_recv()
            if j == 0:
                sm_part[1] = sm_part[0] + sm_pair[0]
            else:
                small_out[...] = sm_part[1] + sm_pair[1]
    else:
        small_out[...] = gs[...]
    while sums.done["e"] < sums.total:
        pump()
    sums.wait_sends()
    relay.wait_sends()
    for copy in small + tail:
        copy.wait_send()


def backward(x, dy, w, rows, low, pre, ratio, left, resid, up, act, state, lengths, order, nseq, aligned):
    group, width = x.shape
    count, batches = nseq // 2, 3
    share_rows = width // nseq
    steps = batches * count
    f32, bf16 = jnp.float32, jnp.bfloat16
    V, S, R = pltpu.VMEM, jax.ShapeDtypeStruct, pltpu.SemaphoreType.REGULAR
    smem = pl.BlockSpec(memory_space=pltpu.SMEM)
    message = (2, 264, PAIR)
    blocks = up.shape[0]
    piece = (share_rows, width)
    small = (16, 128)
    return pl.pallas_call(
        functools.partial(backward_kernel, count, aligned),
        out_shape=(
            S((group, width), f32),
            S((batches,) + piece, f32),
            S(small if aligned else (16, width), f32),
        ),
        in_specs=[ANY, VMEM, ANY, VMEM] + [ANY] * 7 + [VMEM, smem, smem],
        out_specs=[VMEM, VMEM, VMEM],
        scratch_shapes=[
            V((2, 2, 2, 2) + piece, bf16),
            V((2, 2, 2, 2) + piece, bf16),
            V((2, 2) + piece, f32),
            V((3, 2, 2) + piece, bf16),
            V((4, 2, 2) + piece, bf16),
            V((2, 2) + piece, f32),
            V((3, 2) + piece, bf16),
            V((4, 2) + piece, bf16),
            V((2,) + piece, f32),
            V((count - 1, 2) + piece, bf16),
            V(((batches + 1) * (count - 1),) + piece, bf16),
            V((blocks, group, width), bf16),
            V((2, blocks, 2 * share_rows, group), bf16),
            V((2, width // group, group, width), bf16),
            V((2, group, width), f32),
            V((group, width), f32),
            V((group, width), bf16),
            V((group, width), bf16),
            V((group, width), bf16),
            V((group, width), f32),
            V((group, group), f32),
            V((2, group, PAIR), f32),
            V((16, width), f32),
            V(message, f32),
            V(message, f32),
            V(message[1:], f32),
            V((count - 1,) + message[1:], f32),
            V(message, f32),
            V(message, f32),
            V((nseq,) + small, f32),
            V((nseq - 1,) + small, f32),
            V((2,) + small, f32),
            V((2,) + small, f32),
            DMA((32,)),
            DMA((steps,)),
            DMA((steps,)),
            DMA((steps,)),
            DMA((steps,)),
            DMA((steps,)),
            DMA((steps,)),
            DMA((steps,)),
            DMA((batches, count - 1)),
            DMA((batches, count - 1)),
            R,
            R((2,)),
            R((2,)),
            DMA((count + 1,)),
            DMA((count + 1,)),
            DMA((nseq + 1,)),
            DMA((nseq + 1,)),
        ],
        compiler_params=pltpu.CompilerParams(
            collective_id=1, has_side_effects=True, vmem_limit_bytes=VMEM_LIMIT
        ),
    )(x, dy, w.reshape(-1, width // group, group, width), rows, low, pre, ratio, left, resid, up, act, state, lengths, order)


STEP = 10


def padded(vector):
    short = 2048 - vector.shape[-1]
    edges = [(0, 0)] * (vector.ndim - 1) + [(0, short)]
    return jnp.pad(vector, edges).reshape(vector.shape[:-1] + (16, 128))


def local(
    tokens, cotangent, lengths, order, weights, momentum, small_params, moment_one, moment_two
):
    width = tokens.shape[2]
    nseq = lax.axis_size("seq")
    share = small_params.shape[0]
    rounded = lax.reduce_precision(small_params, 8, 7)
    aligned = share % 128 == 0
    if aligned:
        shared = padded(rounded)
    else:
        shared = lax.all_gather(rounded, "seq", axis=0, tiled=True).reshape(-1, width)
    (gathered, block_out, rows, *kept) = forward(
        tokens[0], weights, shared, lengths, order, nseq, aligned
    )
    input_grad, sums, row_small = backward(
        tokens[0], cotangent[0], gathered, rows, *kept, lengths, order, nseq, aligned
    )
    if aligned:
        row_small = row_small.reshape(2048)[:share]
    else:
        row_small = lax.psum_scatter(
            row_small[:13].reshape(-1), "seq", scatter_dimension=0, tiled=True
        )
        row_small = lax.psum(row_small, "stream")
    row_units, update = muon(sums, momentum, nseq)
    new_momentum = 0.5 * momentum + row_units
    blocks = (weights.shape[0] - 4) // 2
    rates = jnp.array([0.5] * 3 + [4.0] + [0.5] * blocks + [0.25] * blocks, dtype=jnp.float32)
    new_weights = weights - rates[:, None, None] * (update.astype(jnp.float32) + 0.01 * weights)
    first_new = 0.9 * moment_one + 0.1 * row_small
    second_new = 0.95 * moment_two + 0.05 * row_small * row_small
    adjusted = first_new / (1.0 - 0.9**STEP) / (jnp.sqrt(second_new / (1.0 - 0.95**STEP)) + 1e-08)
    new_small = small_params - 0.05 * (adjusted + 0.01 * small_params)
    return (
        block_out[None], input_grad[None], new_weights, new_momentum, new_small, first_new, second_new,
    )


def solution(mesh):
    in_specs = (
        P("stream", "seq", None),
        P("stream", "seq", None),
        P("stream", None),
        P("stream", None),
        P(None, "seq", None),
        P(None, "seq", None),
        P("seq"),
        P("seq"),
        P("seq"),
    )
    out_specs = (
        P("stream", "seq", None),
        P("stream", "seq", None),
        P(None, "seq", None),
        P(None, "seq", None),
        P("seq"),
        P("seq"),
        P("seq"),
    )
    return jax.shard_map(local, mesh=mesh, in_specs=in_specs, out_specs=out_specs, check_vma=False)
```

```python
import functools

import jax
import jax.numpy as jnp
from jax import lax
from jax.experimental import pallas as pl
from jax.experimental.pallas import tpu as pltpu
from jax.sharding import PartitionSpec as P

MESH = pl.DeviceIdType.MESH
DMA = pltpu.SemaphoreType.DMA
ANY = pl.BlockSpec(memory_space=pl.ANY)
VMEM = pl.BlockSpec(memory_space=pltpu.VMEM)
VMEM_LIMIT = 62 << 20


def places():
    seq = lax.axis_index("seq")
    stream = lax.axis_index("stream")
    return seq // 2, seq % 2, stream // 2, stream % 2


def device(z, x, y, c):
    return {"seq": z * 2 + x, "stream": y * 2 + c}


def greet(peers):
    barrier = pltpu.get_barrier_semaphore()
    for peer in peers:
        pl.semaphore_signal(barrier, inc=1, device_id=peer, device_id_type=MESH)
    pl.semaphore_wait(barrier, len(peers))


def remote(source, target, sent, received, peer):
    return pltpu.make_async_remote_copy(
        src_ref=source,
        dst_ref=target,
        send_sem=sent,
        recv_sem=received,
        device_id=peer,
        device_id_type=MESH,
    )


def others_along_seq(z, x, y, c, count):
    straight = [device(lax.rem(z + k, count), x, y, c) for k in range(1, count)]
    across = [device(lax.rem(z + k, count), 1 - x, y, c) for k in range(count)]
    return straight, across


CHUNK = 32


BAND = 256


def split_two(values):
    high = values.astype(jnp.bfloat16)
    return high, (values - high.astype(jnp.float32)).astype(jnp.bfloat16)


def dot(left, right, transposed=False):
    dims = (((1,), (1 if transposed else 0,)), ((), ()))
    return lax.dot_general(left, right, dims, preferred_element_type=jnp.float32)


LAG = (2, 4, 5)
HALF = 64
PAIR = 128


def matrix(w_ref, batch, index):
    block = w_ref[batch, index // 2, index % 2]
    return block.reshape(block.shape[0] * block.shape[1] * block.shape[2], block.shape[3])


def norm_rows(values, gain, offset):
    center = values - jnp.mean(values, axis=-1, keepdims=True)
    spread = jnp.mean(center * center, axis=-1, keepdims=True)
    return center * lax.rsqrt(spread + 1e-05) * gain + offset


def lanes_of(head):
    lane = lax.broadcasted_iota(jnp.int32, (1, PAIR), 1)
    return (lane // HALF) == head


def block_diagonal():
    row = lax.broadcasted_iota(jnp.int32, (PAIR, PAIR), 0)
    lane = lax.broadcasted_iota(jnp.int32, (PAIR, PAIR), 1)
    return (row // HALF) == (lane // HALF)


def pair_span(index):
    return pl.ds(pl.multiple_of(index * PAIR, PAIR), PAIR)


def band_span(index):
    return pl.ds(pl.multiple_of(index * BAND, BAND), BAND)


def dot_down(left, right):
    return lax.dot_general(left, right, (((0,), (0,)), ((), ())), preferred_element_type=jnp.float32)


def pack_message(left_ref, right_ref, scale_ref, row_ref, message):
    diagonal = block_diagonal()
    for j in range(4):
        parts = []
        for p in (2 * j, 2 * j + 1):
            lanes = slice(p * PAIR, (p + 1) * PAIR)
            scale = scale_ref[...]
            left = (left_ref[:, lanes].astype(jnp.float32) * scale).astype(jnp.bfloat16)
            parts.append(dot_down(left, right_ref[:, lanes]))
            if row_ref is None:
                total = jnp.sum(left.astype(jnp.float32), axis=0, keepdims=True)
            else:
                total = jnp.sum(left.astype(jnp.float32) * row_ref[:, lanes], axis=0, keepdims=True)
            for half in range(2):
                message[half, 256 + p : 257 + p, :] = total
        block = jnp.where(diagonal, parts[0], pltpu.roll(parts[1], HALF, 1))
        message[j // 2, (j % 2) * PAIR : (j % 2 + 1) * PAIR, :] = block


def unpack_message(message, p):
    diagonal = block_diagonal()
    j = p // 2
    block = message[j // 2, (j % 2) * PAIR : (j % 2 + 1) * PAIR, :]
    if p % 2:
        block = pltpu.roll(block, HALF, 1)
    block = jnp.where(diagonal, block, 0.0)
    row = message[0, 256 + p : 257 + p, :]
    column = jnp.transpose(jnp.broadcast_to(row, (PAIR, PAIR)))
    return block, jnp.where(diagonal, column, 0.0)


class Relay:
    def __init__(self, count, coef, own, across, part, spread, total, result, sems, places_):
        self.count, self.coef, self.own, self.across = count, coef, own, across
        self.part, self.spread, self.total, self.result = part, spread, total, result
        self.send, self.recv = sems
        self.z, self.x, self.y, self.c = places_
        self.pair = device(self.z, 1 - self.x, self.y, self.c)

    def swap(self):
        self.first = remote(self.own, self.across, self.send.at[0], self.recv.at[0], self.pair)
        self.first.start()

    def spread_out(self):
        self.first.wait_recv()
        self.part[...] = self.coef[0] * self.own[self.x] + self.coef[1] * self.across[self.x]
        self.copies = []
        for k in range(1, self.count):
            peer = device(lax.rem(self.z + k, self.count), self.x, self.y, self.c)
            copy = remote(self.part, self.spread.at[k - 1], self.send.at[k], self.recv.at[k], peer)
            copy.start()
            self.copies.append(copy)

    def join(self):
        total = jnp.zeros_like(self.part)
        for k, copy in enumerate(self.copies):
            copy.wait_recv()
            total = total + self.coef[4 + k] * self.spread[k]
        self.total[self.x] = total
        half = self.total.at[self.x]
        self.last = remote(half, half, self.send.at[self.count], self.recv.at[self.count], self.pair)
        self.last.start()

    def finish(self):
        self.last.wait_recv()
        for half in range(2):
            self.result[half] = self.coef[2] * self.total[half] + self.coef[3] * self.across[half]

    def wait_sends(self):
        for copy in [self.first, self.last] + self.copies:
            copy.wait_send()


def head_scores(q_ref, k_ref, keep_ref, lanes, head, band):
    rows = slice(band * BAND, (band + 1) * BAND)
    upto = slice(0, (band + 1) * BAND)
    query = jnp.where(lanes_of(head), q_ref[rows, lanes], 0)
    return dot(query, k_ref[upto, lanes], True) * keep_ref[rows, upto]


def attend_pair(p, q_ref, k_ref, v_ref, keep_ref, num_ref, den_ref):
    lanes = pair_span(p)
    group = q_ref.shape[0]
    value = v_ref[:, lanes]
    first = lanes_of(0)
    for band in range(group // BAND):
        rows = slice(band * BAND, (band + 1) * BAND)
        sums, totals = [], []
        for head in range(2):
            scores = head_scores(q_ref, k_ref, keep_ref, lanes, head, band)
            totals.append(jnp.sum(scores, axis=1, keepdims=True))
            sums.append(dot(scores.astype(jnp.bfloat16), value[: (band + 1) * BAND]))
        num_ref[rows, lanes] = jnp.where(first, sums[0], sums[1])
        den_ref[rows, lanes] = jnp.where(first, totals[0], totals[1])


def image_ends(lengths_ref, order_ref):
    images = lengths_ref.shape[1]
    ends, running = [], jnp.int32(0)
    for j in range(images):
        for i in range(images):
            running = running + jnp.where(order_ref[0, j] == i, lengths_ref[0, i], 0)
        ends.append(running)
    return ends


def segment_at(ends, positions):
    found = jnp.zeros_like(positions)
    for end in ends:
        found = found + jnp.where(positions >= end, 1, 0)
    return found


def same(left, right):
    return jnp.where(left == right, 1.0, 0.0)


def fill_masks(ends, start, group, keep_ref, flags_ref):
    for band in range(group // BAND):
        rows = slice(band * BAND, (band + 1) * BAND)
        down = lax.broadcasted_iota(jnp.int32, (BAND, group), 0) + band * BAND
        along = lax.broadcasted_iota(jnp.int32, (BAND, group), 1)
        mine = segment_at(ends, down + start)
        theirs = segment_at(ends, along + start)
        keep_ref[rows, :] = jnp.where(along <= down, same(mine, theirs), 0.0)
        narrow = mine[:, :PAIR]
        flags_ref[0, rows, :] = same(narrow, segment_at(ends, start - 1))
        flags_ref[1, rows, :] = same(narrow, segment_at(ends, start + group - 1))


def pass_at(ends, block, group):
    return same(segment_at(ends, block * group + group - 1), segment_at(ends, block * group - 1))


def forward_factors(ends, group, count, z, x):
    both = [pass_at(ends, 2 * z, group), pass_at(ends, 2 * z + 1, group)]
    near = [jnp.where(x == 0, both[1], 1.0), jnp.where(x == 0, 1.0, both[1])]
    near += [jnp.where(x == 0, 1.0, both[0]), jnp.where(x == 0, 0.0, 1.0)]
    running, far = jnp.float32(1.0), []
    for k in range(1, count):
        far.append(jnp.where(z - k >= 0, running, 0.0))
        there = jnp.maximum(z - k, 0)
        running = running * pass_at(ends, 2 * there, group) * pass_at(ends, 2 * there + 1, group)
    return near + far


def backward_factors(ends, group, count, z, x):
    both = [pass_at(ends, 2 * z, group), pass_at(ends, 2 * z + 1, group)]
    near = [jnp.where(x == 0, 1.0, both[0]), jnp.where(x == 0, both[0], 1.0)]
    near += [jnp.where(x == 0, both[1], 1.0), jnp.where(x == 0, 1.0, 0.0)]
    running, ahead = jnp.float32(1.0), []
    for k in range(1, count):
        ahead.append(jnp.where(z + k < count, running, 0.0))
        there = jnp.minimum(z + k, count - 1)
        running = running * pass_at(ends, 2 * there, group) * pass_at(ends, 2 * there + 1, group)
    return near + ahead[::-1]


def forward_kernel(
    count, aligned, x_ref, w_ref, small_ref, lengths_ref, order_ref,
    w_out, out_ref, rows_ref, low_ref, pre_ref, ratio_ref, left_ref, resid_ref, up_ref, act_ref, state_ref,
    w_all, stage, small_in, keep, flags, h1, q, k, v, num, den, o, resid, h2, act, turned, act_turned, message, across, part, spread, total_ref, state,
    load_sem, out_sem, zs, zr, ps, pr, ss, sr, rs, rr,
):
    z, x, y, c = places()
    straight, far = others_along_seq(z, x, y, c, count)
    pair = [device(z, 1 - x, y, c), device(z, x, 1 - y, c), device(z, x, y, 1 - c)]
    batches = w_ref.shape[0]
    rows, width = w_ref.shape[3:]
    group = x_ref.shape[0]
    bands = group // BAND
    loads = []
    for b in range(batches):
        for i in range(4):
            copy = pltpu.make_async_copy(
                w_ref.at[b, i // 2, i % 2],
                stage.at[b, pl.ds(i * rows, rows)],
                load_sem.at[b, i],
            )
            copy.start()
            loads.append(copy)
    greet(straight + far + pair[1:])
    small = []
    if aligned:
        for j, peer in enumerate(straight + far):
            small.append(remote(small_ref, small_in.at[z * 2 + x], ss.at[j], sr.at[j], peer))
            small[-1].start()
        small_in[z * 2 + x] = small_ref[...]
    spread_w = {}

    def cast_own(b):
        for i in range(4):
            loads[b * 4 + i].wait()
            for j in range(rows // CHUNK):
                span = slice(j * CHUNK, (j + 1) * CHUNK)
                at = slice(i * rows + j * CHUNK, i * rows + (j + 1) * CHUNK)
                w_all[b, i // 2, i % 2, z, x, span, :] = stage[b, at, :].astype(jnp.bfloat16)

    def send_own(b):
        for j in range(1, count):
            block = w_all.at[b, y, c, z, x]
            spread_w[b, j] = remote(block, block, zs.at[b, j - 1], zr.at[b, j - 1], straight[j - 1])
            spread_w[b, j].start()

    first, second, third, outs, waited = [], [], [], [], []
    plan = [(b, 0) for b in range(batches)]
    plan += [(b, j) for b in range(batches) for j in range(1, count)]
    total = len(plan)

    def send(kept, phase, index, block, peer):
        kept.append(remote(block, block, ps.at[phase, index], pr.at[phase, index], peer))
        kept[-1].start()

    def put_out(source, target):
        copy = pltpu.make_async_copy(source, target, out_sem.at[len(outs)])
        copy.start()
        outs.append(copy)
        return copy

    def tick(step):
        index = step
        if index < total:
            b, j = plan[index]
            there = lax.rem(z - j + count, count)
            if j:
                spread_w[b, j].wait_recv()
            send(first, 0, index, w_all.at[b, y, c, there, x], pair[(j + b) % 2 if j else 0])
            if j == min(1, count - 1) and b + 1 < batches:
                send_own(b + 1)
        index = step - LAG[0]
        if 0 <= index < total:
            b, j = plan[index]
            there = lax.rem(z - j + count, count)
            first[index].wait_recv()
            if j == 0:
                send(second, 1, index, w_all.at[b, y, c, z, 1 - x], pair[1])
            elif (j + b) % 2 == 0:
                send(second, 1, index, w_all.at[b, y, c, there], pair[1])
            else:
                send(second, 1, index, w_all.at[b, :, c, there, x], pair[0])
        index = step - LAG[1]
        if 0 <= index < total:
            b, j = plan[index]
            there = lax.rem(z - j + count, count)
            second[index].wait_recv()
            block = w_all.at[b, :, c, z, 1 - x] if j == 0 else w_all.at[b, :, c, there]
            send(third, 2, index, block, pair[2])
        index = step - LAG[2]
        if 0 <= index < total:
            b, j = plan[index]
            there = lax.rem(z - j + count, count)
            third[index].wait_recv()
            put_out(w_all.at[b, :, :, there], w_out.at[b, :, :, there])

    cast_own(0)
    send_own(0)
    tick(0)
    for b in range(1, batches):
        cast_own(b)
        tick(b)
    if aligned:
        for copy in small:
            copy.wait_recv()
        share_rows = 13 * 1024 // 128 // (count * 2)
        for j in range(13 * 8):
            rows_ref[j // 8 : j // 8 + 1, (j % 8) * 128 : (j % 8 + 1) * 128] = small_in[
                j // share_rows, j % share_rows : j % share_rows + 1, :
            ]
    else:
        rows_ref[0:13, :] = small_ref[...]

    def vector(index):
        return rows_ref[index : index + 1, :]

    def norm_one(i, carry):
        span = band_span(i)
        value = norm_rows(x_ref[span, :].astype(jnp.float32), vector(0), vector(1))
        value = value.astype(jnp.bfloat16)
        h1[span, :] = value
        turned[0, :, span] = jnp.transpose(value.astype(jnp.float32) - vector(1)).astype(jnp.bfloat16)
        return carry

    lax.fori_loop(0, bands, norm_one, 0)
    ends = image_ends(lengths_ref, order_ref)
    fill_masks(ends, (z * 2 + x) * group, group, keep, flags)
    factors = forward_factors(ends, group, count, z, x)
    ready = batches + count - 1 + LAG[2]
    for step in range(batches, ready):
        tick(step)

    def project(i, carry):
        span = band_span(i)
        left = h1[span, :]
        for index, low in ((0, q), (1, k)):
            pre = dot(left, matrix(w_all, 0, index)) + vector(4 + index)
            stage[index, span, :] = pre
            low[span, :] = jnp.where(pre > 0, pre + 1.0, jnp.exp(jnp.minimum(pre, 0.0))).astype(jnp.bfloat16)
        v[span, :] = (dot(left, matrix(w_all, 0, 2)) + vector(6)).astype(jnp.bfloat16)
        return carry

    lax.fori_loop(0, bands, project, 0)
    guess = jnp.broadcast_to(vector(1), (16, width)).astype(jnp.bfloat16)
    guess = dot(guess, matrix(w_all, 0, 2))[0:1, :] + vector(6)
    rows_ref[13:14, :] = guess.astype(jnp.bfloat16).astype(jnp.float32)
    pack_message(k, v, flags.at[1], None, message)
    relay = Relay(count, factors, message, across, part, spread, total_ref, state, (rs, rr), (z, x, y, c))
    relay.swap()
    stored = [put_out(stage.at[0], pre_ref.at[0]), put_out(stage.at[1], pre_ref.at[1]), None]
    for index, low in enumerate((q, k, v)):
        put_out(low, low_ref.at[index])

    def attend(p, carry):
        attend_pair(p, q, k, v, keep, num, den)
        return carry

    pairs = width // PAIR
    step = ready
    lax.fori_loop(0, pairs // 4, attend, 0)
    tick(step)
    relay.spread_out()
    lax.fori_loop(pairs // 4, pairs // 2, attend, 0)
    tick(step + 1)
    lax.fori_loop(pairs // 2, pairs, attend, 0)
    relay.join()
    tick(step + 2)
    relay.finish()
    put_out(state, state_ref)
    for p in range(pairs):
        block, column = unpack_message(state, p)
        high, low = split_two(jnp.concatenate([block, column], axis=1))
        lanes = slice(p * PAIR, (p + 1) * PAIR)
        for i in range(bands):
            span = slice(i * BAND, (i + 1) * BAND)
            query = q[span, lanes]
            both = dot(query, high) + dot(query, low)
            flag = flags[0, span, :]
            top = num[span, lanes] + flag * both[:, :PAIR]
            bottom = den[span, lanes] + flag * both[:, PAIR:]
            num[span, lanes] = top
            den[span, lanes] = bottom
            o[span, lanes] = (top / bottom).astype(jnp.bfloat16)
    put_out(num, ratio_ref.at[0])
    put_out(den, ratio_ref.at[1])

    def close(i, carry):
        span = band_span(i)
        value = x_ref[span, :].astype(jnp.float32) + dot(o[span, :], matrix(w_all, 0, 3)) + vector(7)
        resid[span, :] = value
        hidden = norm_rows(value, vector(2), vector(3)).astype(jnp.bfloat16)
        h2[span, :] = hidden
        turned[2, :, span] = jnp.transpose(hidden.astype(jnp.float32) - vector(3)).astype(jnp.bfloat16)
        turned[1, :, span] = jnp.transpose(o[span, :].astype(jnp.float32) - vector(13)).astype(jnp.bfloat16)
        return carry

    lax.fori_loop(0, bands, close, 0)
    put_out(turned, left_ref)
    put_out(resid, resid_ref)
    step = step + 3
    ready = batches + 2 * (count - 1) + LAG[2]
    while step < ready:
        tick(step)
        step += 1
    blocks = act.shape[0]
    turned_out = []
    for j in range(blocks):
        if j > 1:
            turned_out[j - 2].wait()
            waited.append(turned_out[j - 2])
        if stored[j % 3] is not None:
            stored[j % 3].wait()
            waited.append(stored[j % 3])

        def expand(i, carry):
            span = band_span(i)
            pre = dot(h2[span, :], matrix(w_all, 1, j)) + vector(9 + j)
            stage[j % 3, span, :] = pre
            value = jax.nn.gelu(pre)
            act[j, span, :] = value.astype(jnp.bfloat16)
            act_turned[j % 2, :, span] = jnp.transpose(value).astype(jnp.bfloat16)
            return carry

        lax.fori_loop(0, bands, expand, 0)
        stored[j % 3] = put_out(stage.at[j % 3], up_ref.at[j])
        turned_out.append(put_out(act_turned.at[j % 2], act_ref.at[j]))
        if step < total + LAG[2]:
            tick(step)
            step += 1
    while step < total + LAG[2]:
        tick(step)
        step += 1

    def project_down(i, carry):
        span = band_span(i)
        value = resid[span, :] + vector(8)
        for j in range(blocks):
            value += dot(act[j, span, :], matrix(w_all, 2, j))
        out_ref[span, :] = value.astype(jnp.bfloat16)
        return carry

    lax.fori_loop(0, bands, project_down, 0)
    for copy in outs:
        if not any(copy is other for other in waited):
            copy.wait()
    for copy in list(spread_w.values()) + first + second + third + small:
        copy.wait_send()
    relay.wait_sends()


def forward(x, weights, small, lengths, order, nseq, aligned):
    group, width = x.shape
    units, rows, _ = weights.shape
    count, batches = nseq // 2, units // 4
    steps = batches * count
    f32, bf16 = jnp.float32, jnp.bfloat16
    V, S = pltpu.VMEM, jax.ShapeDtypeStruct
    blocks = 4
    smem = pl.BlockSpec(memory_space=pltpu.SMEM)
    message = (2, 264, PAIR)
    return pl.pallas_call(
        functools.partial(forward_kernel, count, aligned),
        out_shape=(
            S((batches, 2, 2, count, 2, rows, width), bf16),
            S((group, width), bf16),
            S((16, width), f32),
            S((3, group, width), bf16),
            S((2, group, width), f32),
            S((2, group, width), f32),
            S((3, width, group), bf16),
            S((group, width), f32),
            S((blocks, group, width), f32),
            S((blocks, width, group), bf16),
            S(message, f32),
        ),
        in_specs=[VMEM, ANY, VMEM, smem, smem],
        out_specs=[ANY, VMEM, VMEM] + [ANY] * 8,
        scratch_shapes=[
            V((batches, 2, 2, count, 2, rows, width), bf16),
            V((3, group, width), f32),
            V(((nseq,) if aligned else ()) + small.shape, f32),
            V((group, group), f32),
            V((2, group, PAIR), f32),
            V((group, width), bf16),
            V((group, width), bf16),
            V((group, width), bf16),
            V((group, width), bf16),
            V((group, width), f32),
            V((group, width), f32),
            V((group, width), bf16),
            V((group, width), f32),
            V((group, width), bf16),
            V((blocks, group, width), bf16),
            V((3, width, group), bf16),
            V((2, width, group), bf16),
            V(message, f32),
            V(message, f32),
            V(message[1:], f32),
            V((count - 1,) + message[1:], f32),
            V(message, f32),
            V(message, f32),
            DMA((batches, 4)),
            DMA((steps + 20,)),
            DMA((batches, count - 1)),
            DMA((batches, count - 1)),
            DMA((3, steps)),
            DMA((3, steps)),
            DMA((nseq - 1,)),
            DMA((nseq - 1,)),
            DMA((count + 1,)),
            DMA((count + 1,)),
        ],
        compiler_params=pltpu.CompilerParams(
            collective_id=0, has_side_effects=True, vmem_limit_bytes=VMEM_LIMIT
        ),
    )(x, weights.reshape(batches, 2, 2, rows, width), small, lengths, order)


def gelu_slope(values):
    cube = 0.044715 * values * values
    bend = jnp.tanh(0.7978845608028654 * values * (1.0 + cube))
    return 0.5 * (1.0 + bend) + 0.5 * values * (1.0 - bend * bend) * (
        0.7978845608028654 * (1.0 + 3.0 * cube)
    )


def norm_back(values, upstream, gain):
    center = values - jnp.mean(values, axis=-1, keepdims=True)
    spread = jnp.mean(center * center, axis=-1, keepdims=True)
    scale = lax.rsqrt(spread + 1e-05)
    unit = center * scale
    inner = upstream * gain
    back = inner - jnp.mean(inner, axis=-1, keepdims=True)
    back = scale * (back - unit * jnp.mean(inner * unit, axis=-1, keepdims=True))
    return back, unit


def pick_message(message, p):
    down = pl.ds(pl.multiple_of(((p // 2) % 2) * PAIR, PAIR), PAIR)
    block = message[p // 4, down, :]
    block = jnp.where(p % 2 == 1, pltpu.roll(block, HALF, 1), block)
    block = jnp.where(block_diagonal(), block, 0.0)
    return split_two(block), message[0, pl.ds(256 + p, 1), :]


SHIFTS = (0.0, 0.0, 0.1, 0.7, 0.7)
FINE = (False, False, False, False, True)


TALL = 512


def split_rows(ref, start, count):
    size = ref.shape[-2]
    return ref.at[start // size, pl.ds(pl.multiple_of(lax.rem(start, size), count), count)]


def orthogonalize(full, xh, xl, gram, gram_low, finished):
    size = full.shape[-1]
    bands = size // TALL

    def whole(ref):
        return ref[...].reshape(size, size)

    def band_of(ref, index):
        return split_rows(ref, index * TALL, TALL)

    def square(index, total):
        part = band_of(full, index)[...]
        return total + jnp.sum(part * part)

    norm = jnp.sqrt(lax.fori_loop(0, bands, square, jnp.float32(0.0)))
    scale = 1.0 / (norm + 1e-07)

    def begin(index, carry):
        part = band_of(full, index)[...] * scale
        band_of(full, index)[...] = part
        band_of(xh.at[0], index)[...] = part.astype(jnp.bfloat16)
        return carry

    lax.fori_loop(0, bands, begin, 0)
    turns = len(SHIFTS)
    for turn in range(turns):
        shift, fine = SHIFTS[turn], FINE[turn]
        now, later = xh.at[turn % 2], xh.at[1 - turn % 2]
        more = turn + 1 < turns and FINE[turn + 1]

        def form(index, carry):
            left = band_of(now, index)[...]
            block = dot(left, whole(now), True)
            if fine:
                block += dot(left, whole(xl), True) + dot(band_of(xl, index)[...], whole(now), True)
            if shift:
                across = lax.broadcasted_iota(jnp.int32, block.shape, 1)
                down = lax.broadcasted_iota(jnp.int32, block.shape, 0) + index * TALL
                block = jnp.where(across == down, block - shift, block)
            band_of(gram, index)[...] = block
            band_of(gram_low, index)[...] = block.astype(jnp.bfloat16)
            return carry

        lax.fori_loop(0, bands, form, 0)
        linear = -4.775 + 2.0 * 2.0315 * shift
        scaled = 3.4445 - 4.775 * shift + 2.0315 * shift * shift

        def advance(index, carry):
            poly = linear * band_of(gram, index)[...]
            poly = poly + 2.0315 * dot(band_of(gram_low, index)[...], whole(gram_low))
            if fine:
                high, low = split_two(poly)
                step = dot(high, whole(now)) + dot(high, whole(xl)) + dot(low, whole(now))
            else:
                step = dot(poly.astype(jnp.bfloat16), whole(now))
            moved = scaled * band_of(full, index)[...] + step
            if turn + 1 < turns:
                band_of(full, index)[...] = moved
            high, low = split_two(moved)
            band_of(later, index)[...] = high
            if more:
                band_of(xl, index)[...] = low
            if turn + 1 == turns:
                finished(index, TALL)
            return carry

        lax.fori_loop(0, bands, advance, 0)


LAGS = (("d", "e", 2), ("c", "d", 2), ("b", "c", 2), ("a", "b", 1))


class Sums:
    def __init__(self, count, place, product, bufs, sems, sums_ref):
        self.count = count
        self.z, self.x, self.y, self.c = z, x, y, c = place
        self.product, self.sums_ref = product, sums_ref
        (self.core_out, self.core_in, self.own, self.first_out, self.first_in, self.kept_one,
         self.second_out, self.second_in, self.kept_two, self.far_out, self.far_in) = bufs
        (self.cs, self.cr, self.fs, self.fr, self.es, self.er, self.zs, self.zr,
         self.credit_core, self.credit_first, self.credit_second) = sems
        self.pair = [device(z, 1 - x, y, c), device(z, x, 1 - y, c), device(z, x, y, 1 - c)]
        self.steps = [(b, k) for b in (2, 1, 0) for k in range(count)]
        self.total = len(self.steps)
        self.cores, self.firsts, self.seconds, self.fars = [], [], [], {}
        self.rows = sums_ref.shape[1]
        self.beat = 0
        self.done = {name: 0 for name in "abcde"}
        self.stamp = {}
        self.needs = {"a": (("b", 1),), "b": (("c", 2),), "c": (("d", 2),)}

    def there(self, i):
        return lax.rem(self.z + 1 + self.steps[i][1], self.count)

    def give(self, semaphore, peer):
        pl.semaphore_signal(semaphore, inc=1, device_id=peer, device_id_type=MESH)

    def take(self, semaphore):
        pl.semaphore_wait(semaphore, 1)

    def add(self, base, got, target):
        def body(index, carry):
            at = pl.ds(pl.multiple_of(index * CHUNK, CHUNK), CHUNK)
            target[at, :] = (base[at, :] + got[at, :].astype(jnp.float32)).astype(target.dtype)
            return carry

        lax.fori_loop(0, self.rows // CHUNK, body, 0)

    def stage_a(self, i):
        slot = i % 2
        batch = self.steps[i][0]
        if i >= 2:
            self.cores[i - 2].wait_send()
        for yy in range(2):
            value = self.product(i, batch, yy, 1 - self.c).astype(jnp.bfloat16)
            for xx in range(2):
                self.core_out[slot, yy, xx] = value[xx * self.rows : (xx + 1) * self.rows]
        if i >= 2:
            self.take(self.credit_core)
        source, target = self.core_out.at[slot], self.core_in.at[slot]
        self.cores.append(remote(source, target, self.cs.at[i], self.cr.at[i], self.pair[2]))
        self.cores[i].start()
        for yy in range(2):
            value = self.product(i, batch, yy, self.c)
            for xx in range(2):
                self.own[yy, xx] = value[xx * self.rows : (xx + 1) * self.rows]

    def stage_b(self, i):
        slot = i % 2
        k = self.steps[i][1]
        x, y = self.x, self.y
        self.cores[i].wait_recv()
        if i >= 3:
            self.firsts[i - 3].wait_send()
        out = self.first_out.at[i % 3]
        for j in range(2):
            away, near = ((1 - y, j), (y, j)) if k % 2 == 0 else ((j, 1 - x), (j, x))
            self.add(self.own.at[away], self.core_in.at[(slot,) + away], out.at[j])
            self.add(self.own.at[near], self.core_in.at[(slot,) + near], self.kept_one.at[i % 2, j])
        if i + 2 < self.total:
            self.give(self.credit_core, self.pair[2])
        if i >= 4:
            self.take(self.credit_first.at[i % 2])
        peer = self.pair[1 - k % 2]
        self.firsts.append(remote(out, self.first_in.at[i % 4], self.fs.at[i], self.fr.at[i], peer))
        self.firsts[i].start()

    def stage_c(self, i):
        k = self.steps[i][1]
        mine = self.x if k % 2 == 0 else self.y
        self.firsts[i].wait_recv()
        if i >= 3:
            self.seconds[i - 3].wait_send()
        out = self.second_out.at[i % 3]
        kept, got = self.kept_one.at[i % 2], self.first_in.at[i % 4]
        self.add(kept.at[1 - mine], got.at[1 - mine], out)
        self.add(kept.at[mine], got.at[mine], self.kept_two.at[i % 2])
        if i + 4 < self.total:
            self.give(self.credit_first.at[i % 2], self.pair[1 - k % 2])
        if i >= 4:
            self.take(self.credit_second.at[i % 2])
        copy = remote(out, self.second_in.at[i % 4], self.es.at[i], self.er.at[i], self.pair[k % 2])
        copy.start()
        self.seconds.append(copy)

    def stage_d(self, i):
        b, k = self.steps[i]
        self.seconds[i].wait_recv()
        kept, got = self.kept_two.at[i % 2], self.second_in.at[i % 4]
        if k < self.count - 1:
            if i >= self.count:
                self.fars[i - self.count].wait_send()
            out = self.far_out.at[k]
            self.add(kept, got, out)
            peer = device(self.there(i), self.x, self.y, self.c)
            self.fars[i] = remote(out, self.far_in.at[b, k], self.zs.at[b, k], self.zr.at[b, k], peer)
            self.fars[i].start()
        else:
            self.add(kept, got, self.sums_ref.at[b])
        if i + 4 < self.total:
            self.give(self.credit_second.at[i % 2], self.pair[k % 2])

    def stage_e(self, i):
        b, k = self.steps[i]
        if k < self.count - 1:
            return
        for j in range(self.count - 1):
            self.fars[i - self.count + 1 + j].wait_recv()
            self.add(self.sums_ref.at[b], self.far_in.at[b, j], self.sums_ref.at[b])

    def run(self, name):
        i = self.done[name]
        for other, back in self.needs.get(name, ()):
            while self.done[other] <= i - back:
                self.run(other)
        getattr(self, "stage_" + name)(i)
        self.done[name] = i + 1
        self.stamp[name, i] = self.beat

    def pump(self, make=False):
        self.beat += 1
        for before, name, lag in LAGS:
            while self.done[name] < self.done[before]:
                if self.beat - self.stamp[before, self.done[name]] < lag:
                    break
                self.run(name)
        if make:
            self.run("a")

    def wait_sends(self):
        for copy in self.cores[-2:] + self.firsts[-3:] + self.seconds[-3:]:
            copy.wait_send()
        for i, copy in self.fars.items():
            if i >= self.total - self.count:
                copy.wait_send()


class Totals:
    def __init__(self, count, place, own, got, kept, send, recv):
        z, x, y, c = place
        self.peers = [
            [device(z, 1 - x, y, c)],
            [device(lax.rem(z + k, count), x, y, c) for k in range(1, count)],
            [device(z, x, 1 - y, c)],
            [device(z, x, y, 1 - c)],
        ]
        self.own, self.got, self.kept, self.sems = own, got, kept, (send, recv)
        self.stage, self.copies, self.pending = 0, [], []

    def source(self):
        return self.own if self.stage == 0 else self.kept.at[self.stage - 1]

    def send(self, stage):
        self.stage, self.pending = stage, []
        for peer in self.peers[stage]:
            index = len(self.copies)
            copy = remote(
                self.source(), self.got.at[index], self.sems[0].at[index], self.sems[1].at[index], peer
            )
            copy.start()
            self.copies.append(copy)
            self.pending.append(index)

    def receive(self):
        total = self.source()[...]
        for index in self.pending:
            self.copies[index].wait_recv()
            total = total + self.got[index]
        self.kept[self.stage] = total

    def value(self):
        return self.kept[self.stage]

    def wait_sends(self):
        for copy in self.copies:
            copy.wait_send()


def restore_mean(target, rows_ref, totals, b, place):
    z, x, y, c = place
    rows, width = target.shape
    stream = y * 2 + c
    across = lax.broadcasted_iota(jnp.int32, (width, rows), 1) + (z * 2 + x) * rows
    chosen = jnp.where(lax.broadcasted_iota(jnp.int32, (width, rows), 0) == across, 1.0, 0.0)
    if b == 0:
        vector = jnp.where(stream == 3, rows_ref[13:14, :], rows_ref[1:2, :])
    else:
        vector = rows_ref[3:4, :]
    head = lax.broadcasted_iota(jnp.int32, (16, width), 0)
    left = jnp.where(head < 3, jnp.broadcast_to(vector, (16, width)), 0.0).astype(jnp.bfloat16)
    left = dot(left, chosen.astype(jnp.bfloat16)).astype(jnp.bfloat16)
    at = (4 if b == 0 else 9) + stream
    row = jnp.sum(jnp.where(head == at, totals[...], 0.0), axis=0, keepdims=True)
    high = row.astype(jnp.bfloat16).astype(jnp.float32)
    middle = (row - high).astype(jnp.bfloat16).astype(jnp.float32)
    right = jnp.where(head == 0, high, jnp.where(head == 1, middle, jnp.where(head == 2, row - high - middle, 0.0)))
    target[...] = target[...] + dot_down(left, right.astype(jnp.bfloat16))


def backward_kernel(
    count, x_ref, dy_ref, w_ref, rows_ref, low_ref, pre_ref, ratio_ref, left_ref, resid_ref, up_ref, act_ref,
    state, lengths_ref, order_ref, mom_ref,
    grad_ref, small_out, all_ref, ortho_ref,
    core_out, core_in, own, first_out, first_in, kept_one, second_out, second_in, kept_two, far_out, far_in,
    sums_ref, mom_own, full, big, left, wbuf, ubuf, acc, extra, dden, keep, flags, gs, gs_early,
    message, across, part, spread, total_ref, state_back, small_got, small_sum, early_got, early_sum,
    load_sem, lt_sem, cs, cr, fs, fr, es, er, zs, zr, credit_core, credit_first, credit_second, rs, rr, ms, mr,
    hs, hr, vs, vr, self_sem, ys, yr, os_, or_, js, jr, ks, kr,
):
    place = z, x, y, c = places()
    straight, far = others_along_seq(z, x, y, c, count)
    pair = [device(z, 1 - x, y, c), device(z, x, 1 - y, c), device(z, x, y, 1 - c)]
    group, width = dy_ref.shape
    bands = group // BAND
    pairs = width // PAIR
    block_rows = 2 * sums_ref.shape[1]
    f32, bf16 = jnp.float32, jnp.bfloat16
    issued = []
    dnum, da = extra.at[0], extra.at[1]
    dq_low = dnum
    nseq, batches = count * 2, sums_ref.shape[0]
    rows = sums_ref.shape[1]
    seq = z * 2 + x
    owner = [2 * b + c + 1 for b in range(batches)]
    is_owner = (seq == owner[0]) | (seq == owner[1]) | (seq == owner[2])

    def load(source, target):
        copy = pltpu.make_async_copy(source, target, load_sem.at[len(issued)])
        copy.start()
        issued.append(copy)
        return copy

    def load_left(i):
        b = sums.steps[i][0]
        at = pl.ds(pl.multiple_of(sums.there(i) * block_rows, block_rows), block_rows)
        slot = left.at[i % 2]
        if b == 2:
            pieces = [(act_ref.at[:, at], slot)]
        elif b == 1:
            pieces = [(left_ref.at[pl.ds(2, 1), at], slot.at[pl.ds(0, 1)])]
        else:
            pieces = [(left_ref.at[pl.ds(0, 2), at], slot.at[pl.ds(0, 2)])]
        copies = [pltpu.make_async_copy(s, t, lt_sem.at[i]) for s, t in pieces]
        for copy in copies:
            copy.start()
        return copies

    lefts = {}

    def product(i, batch, yy, cc):
        unit = 2 * yy + cc
        if batch == 2:
            lhs, rhs = left[i % 2, unit], dy_ref[...]
        elif batch == 1:
            lhs, rhs = left[i % 2, 0], big[unit]
        else:
            lhs, rhs = left[i % 2, yy * cc], big[unit]
        return dot(lhs, rhs)

    sums = Sums(
        count, place, product,
        (core_out, core_in, own, first_out, first_in, kept_one, second_out, second_in, kept_two, far_out, far_in),
        (cs, cr, fs, fr, es, er, zs, zr, credit_core, credit_first, credit_second), sums_ref,
    )

    placed, mom_loads = [], []

    def moved_copy(b):
        target = {"seq": owner[b], "stream": y * 2 + c}
        return remote(sums_ref.at[b], split_rows(full, seq * rows, rows), vs.at[b], vr.at[seq], target)

    def place_batch(b, totals):
        if totals is not None:
            restore_mean(sums_ref.at[b], rows_ref, totals, b, place)
        mom_loads[-1].wait()
        placed.append(b)

        def body(index, carry):
            at = pl.ds(pl.multiple_of(index * CHUNK, CHUNK), CHUNK)
            sums_ref[b, at, :] = 0.5 * mom_own[at, :] + sums_ref[b, at, :]
            return carry

        lax.fori_loop(0, rows // CHUNK, body, 0)
        if b:
            mom_loads.append(load(mom_ref.at[b - 1, y, c], mom_own))

        @pl.when(seq != owner[b])
        def _():
            moved_copy(b).start()

        @pl.when(seq == owner[b])
        def _():
            split_rows(full, seq * rows, rows)[...] = sums_ref[b]

    def pump(make=False):
        i = sums.done["a"]
        if make:
            for copy in lefts[i]:
                copy.wait()
            if i + 1 < sums.total:
                lefts[i + 1] = load_left(i + 1)
        sums.pump(make)
        if sums.done["e"] >= count and 2 not in placed:
            place_batch(2, None)

    def make_until(limit):
        while sums.done["a"] < limit:
            pump(True)

    lefts[0] = load_left(0)
    blocks = big.shape[0]
    w_loads = {(2, j): load(w_ref.at[8 + j], wbuf.at[j]) for j in range(2)}
    u_loads = {j: load(up_ref.at[j], ubuf.at[j]) for j in range(2)}
    resid_load = load(resid_ref, grad_ref)
    mom_loads.append(load(mom_ref.at[2, y, c], mom_own))
    greet(straight + far + pair[1:])
    ends = image_ends(lengths_ref, order_ref)
    fill_masks(ends, (z * 2 + x) * group, group, keep, flags)
    factors = backward_factors(ends, group, count, z, x)
    gs[...] = jnp.zeros_like(gs)

    def add_row(index, value, lanes=slice(None)):
        gs[index : index + 1, lanes] = gs[index : index + 1, lanes] + jnp.sum(
            value.astype(f32), axis=0, keepdims=True
        )

    def unit_of(slot):
        return wbuf[slot].reshape(width, width)

    for i in range(bands):
        add_row(8, dy_ref[i * BAND : (i + 1) * BAND, :])
    for j in range(blocks):
        if j != 2:
            pump(True)
        w_loads[2, j].wait()
        u_loads[j].wait()

        def hidden_back(i, carry):
            span = band_span(i)
            back = dot(dy_ref[span, :], unit_of(j % 2), True)
            back = (back * gelu_slope(ubuf[j % 2, span, :])).astype(bf16)
            big[j, span, :] = back
            add_row(9 + j, back)
            return carry

        lax.fori_loop(0, bands, hidden_back, 0)
        if j + 2 < blocks:
            w_loads[2, j + 2] = load(w_ref.at[8 + j + 2], wbuf.at[j % 2])
            u_loads[j + 2] = load(up_ref.at[j + 2], ubuf.at[j % 2])
        else:
            w_loads[1, j - 2] = load(w_ref.at[4 + j - 2], wbuf.at[j % 2])
            u_loads[j + 2] = load(ratio_ref.at[j - 2], ubuf.at[j % 2])
    for j in range(blocks):
        if j % 2:
            pump(True)
        w_loads[1, j].wait()

        def up_back(i, carry):
            span = band_span(i)
            back = dot(big[j, span, :], unit_of(j % 2), True)
            acc[span, :] = back if j == 0 else acc[span, :] + back
            return carry

        lax.fori_loop(0, bands, up_back, 0)
        if j + 2 < blocks:
            w_loads[1, j + 2] = load(w_ref.at[4 + j + 2], wbuf.at[j % 2])
        elif j + 2 == blocks:
            w_loads[0, 3] = load(w_ref.at[3], wbuf.at[0])
        else:
            low_loads = [load(low_ref.at[0], wbuf.at[1, 0]), load(low_ref.at[1], wbuf.at[1, 1])]
    resid_load.wait()
    w_loads[0, 3].wait()

    def middle_back(i, carry):
        span = band_span(i)
        upstream = acc[span, :]
        back, unit = norm_back(grad_ref[span, :], upstream, rows_ref[2:3, :])
        add_row(2, upstream * unit)
        add_row(3, upstream)
        total = dy_ref[span, :].astype(f32) + back
        grad_ref[span, :] = total
        low = total.astype(bf16)
        da[span, :] = low
        add_row(7, low)
        acc[span, :] = dot(low, unit_of(0), True)
        return carry

    for i in range(bands):
        middle_back(i, 0)
        if i == 0:
            pump(True)
    low_loads.append(load(low_ref.at[2], wbuf.at[0, 0]))
    gs_early[...] = gs[...]
    early = Totals(count, place, gs_early, early_got, early_sum, hs, hr)
    early.send(0)
    u_loads[blocks].wait()
    u_loads[blocks + 1].wait()

    def ratio_back(p, carry):
        lanes = pair_span(p)
        first = lanes_of(0)
        for i in range(bands):
            span = slice(i * BAND, (i + 1) * BAND)
            inverse = 1.0 / ubuf[1, span, lanes]
            scaled = acc[span, lanes] * inverse
            dnum[span, lanes] = scaled.astype(bf16)
            weighted = scaled * ubuf[0, span, lanes] * inverse
            one = jnp.sum(jnp.where(first, weighted, 0.0), axis=1, keepdims=True)
            two = jnp.sum(jnp.where(first, 0.0, weighted), axis=1, keepdims=True)
            dden[span, lanes] = -jnp.where(first, one, two)
        return carry

    lax.fori_loop(0, pairs, ratio_back, 0)
    for copy in low_loads:
        copy.wait()
    query, key, value = wbuf.at[1, 0], wbuf.at[1, 1], wbuf.at[0, 0]
    pack_message(query, dnum, flags.at[0], dden, message)
    relay = Relay(count, factors, message, across, part, spread, total_ref, state_back, (rs, rr), place)
    relay.swap()
    pump(True)
    pre_load = load(pre_ref.at[0], acc)
    pre_load.wait()

    def attend_back(p, carry):
        lanes = pair_span(p)
        (state_high, state_low), totals = pick_message(state, p)
        lane = lax.broadcasted_iota(jnp.int32, (1, PAIR), 1) % HALF
        for band in range(bands):
            span = slice(band * BAND, (band + 1) * BAND)
            upto = (band + 1) * BAND
            back = dnum[span, lanes]
            below = dden[span, lanes]
            high, low = split_two(pltpu.roll(below, HALF, 1))
            extra = jnp.where(lane == 0, high, jnp.where(lane == 1, low, jnp.zeros_like(low)))
            asked = query[span, lanes]
            keys = key[0:upto, lanes]
            held = value[0:upto, lanes]
            kept = keep[span, 0:upto]
            found, key_back, value_back = [], 0.0, 0.0
            for head in range(2):
                mine = lanes_of(head)
                masked = jnp.where(mine, asked, 0)
                scores = (dot(masked, keys, True) * kept).astype(bf16)
                scores_back = dot(jnp.where(mine, back, extra), jnp.where(mine, held, 1), True)
                scores_back = (scores_back * kept).astype(bf16)
                found.append(dot(scores_back, keys))
                key_back = key_back + dot_down(scores_back, masked)
                value_back = value_back + dot_down(scores, jnp.where(mine, back, 0))
            across_blocks = dot(back, state_high, True) + dot(back, state_low, True) + below * totals
            query_back = jnp.where(lanes_of(0), found[0], found[1]) + flags[0, span, :] * across_blocks
            pre = acc[span, lanes]
            slope = jnp.where(pre > 0, 1.0, jnp.exp(jnp.minimum(pre, 0.0)))
            dq_low[span, lanes] = (query_back * slope).astype(bf16)
            for index, total in ((0, key_back), (1, value_back)):
                if band:
                    ubuf[index, 0 : upto - BAND, lanes] = (
                        ubuf[index, 0 : upto - BAND, lanes] + total[: upto - BAND]
                    )
                ubuf[index, span, lanes] = total[upto - BAND :]
        return carry

    quarter = pairs // 4
    limit = sums.total - count
    for part in range(4):
        lax.fori_loop(part * quarter, (part + 1) * quarter, attend_back, 0)
        if part == 0:
            relay.spread_out()
        elif part == 2:
            relay.join()
        pump(sums.done["a"] < limit)
        early.receive()
        if part < 3:
            early.send(part + 1)
    pre_load = load(pre_ref.at[1], acc)
    make_until(limit)
    relay.finish()
    pre_load.wait()

    def attend_close(p, carry):
        lanes = pair_span(p)
        (back_high, back_low), totals = pick_message(state_back, p)
        for i in range(bands):
            span = slice(i * BAND, (i + 1) * BAND)
            flag = flags[1, span, :]
            held, keys = value[span, lanes], key[span, lanes]
            key_back = ubuf[0, span, lanes] + flag * (
                dot(held, back_high, True) + dot(held, back_low, True) + totals
            )
            pre = acc[span, lanes]
            slope = jnp.where(pre > 0, 1.0, jnp.exp(jnp.minimum(pre, 0.0)))
            big[1, span, lanes] = (key_back * slope).astype(bf16)
            value_back = ubuf[1, span, lanes] + flag * (dot(keys, back_high) + dot(keys, back_low))
            big[2, span, lanes] = value_back.astype(bf16)
            big[0, span, lanes] = dq_low[span, lanes]
            big[3, span, lanes] = da[span, lanes]
        for index in range(3):
            total = jnp.sum(big[index, :, lanes].astype(f32), axis=0, keepdims=True)
            gs[4 + index : 5 + index, lanes] = total
        return carry

    lax.fori_loop(0, pairs, attend_close, 0)
    x_load = load(x_ref, dq_low)
    w_loads[0, 0] = load(w_ref.at[0], wbuf.at[0])
    w_loads[0, 1] = load(w_ref.at[1], wbuf.at[1])
    for j in range(3):
        pump(True)
        w_loads[0, j].wait()

        def input_back(i, carry):
            span = band_span(i)
            back = dot(big[j, span, :], unit_of(j % 2), True)
            acc[span, :] = back if j == 0 else acc[span, :] + back
            return carry

        lax.fori_loop(0, bands, input_back, 0)
        if j == 0:
            w_loads[0, 2] = load(w_ref.at[2], wbuf.at[0])

    x_load.wait()

    def outer_back(i, carry):
        span = band_span(i)
        upstream = acc[span, :]
        back, unit = norm_back(dq_low[span, :].astype(f32), upstream, rows_ref[0:1, :])
        add_row(0, upstream * unit)
        add_row(1, upstream)
        grad_ref[span, :] = grad_ref[span, :] + back
        return carry

    lax.fori_loop(0, bands, outer_back, 0)
    totals = Totals(count, place, gs, small_got, small_sum, ms, mr)
    totals.send(0)
    pump(sums.done["a"] < sums.total)
    for stage in range(1, 4):
        totals.receive()
        totals.send(stage)
        pump()
    make_until(sums.total)
    totals.receive()
    small_out[...] = totals.value()
    while sums.done["e"] < sums.total:
        pump()
        if sums.done["e"] >= 2 * count and 1 not in placed:
            place_batch(1, early_sum.at[3])
    place_batch(0, small_out)
    sums.wait_sends()
    relay.wait_sends()
    totals.wait_sends()
    early.wait_sends()
    keep_own = pltpu.make_async_copy(sums_ref, all_ref.at[:, y, c], self_sem.at[0])
    keep_own.start()
    over = remote(sums_ref, all_ref.at[:, y, c], ys.at[0], yr.at[0], pair[1])
    over.start()
    mine = (seq - c - 1) // 2

    def result(where):
        return split_rows(wbuf.at[1], where * rows, rows)

    def give_back(where, k):
        peer = {"seq": where, "stream": y * 2 + c}
        return remote(result(where), ortho_ref.at[mine, y, c], os_.at[k], or_.at[mine], peer)

    def keep_rows():
        return pltpu.make_async_copy(result(seq), ortho_ref.at[mine, y, c], self_sem.at[1])

    def finished(part, height):
        for k in range(height // rows):
            where = part * (height // rows) + k

            @pl.when(where != seq)
            def _():
                give_back(where, where).start()

            @pl.when(where == seq)
            def _():
                keep_rows().start()

    @pl.when(is_owner)
    def _():
        for k in range(1, nseq):
            there = lax.rem(seq + k, nseq)
            block = split_rows(full, there * rows, rows)
            remote(sums_ref.at[0], block, vs.at[0], vr.at[there], pair[1]).wait_recv()
        orthogonalize(full, wbuf, big.at[pl.ds(0, width // group)], ubuf, extra, finished)

    keep_own.wait()
    over.wait_recv()
    share = remote(all_ref.at[:, :, c], all_ref.at[:, :, c], ys.at[1], yr.at[1], pair[2])
    share.start()
    hops, lasts = [], []
    for b in (2, 1, 0):
        target = ortho_ref.at[b, y, c]

        @pl.when(seq == owner[b])
        def _():
            keep_rows().wait()

        @pl.when(seq != owner[b])
        def _():
            remote(result(seq), target, os_.at[0], or_.at[b], pair[1]).wait_recv()

        hop = remote(target, target, js.at[b], jr.at[b], pair[1])
        hop.start()
        hops.append(hop)
    for b, hop in zip((2, 1, 0), hops):
        hop.wait_recv()
        target = ortho_ref.at[b, :, c]
        last = remote(target, target, ks.at[b], kr.at[b], pair[2])
        last.start()
        lasts.append(last)
    for last in lasts:
        last.wait_recv()
    share.wait_recv()
    for copy in [over, share] + hops + lasts:
        copy.wait_send()
    for b in range(batches):

        @pl.when(seq != owner[b])
        def _():
            moved_copy(b).wait_send()

    @pl.when(is_owner)
    def _():
        for k in range(1, nseq):
            there = lax.rem(seq + k, nseq)
            give_back(there, there).wait_send()


def backward(x, dy, w, rows, low, pre, ratio, left, resid, up, act, state, lengths, order, momentum, nseq):
    group, width = x.shape
    count, batches = nseq // 2, 3
    share_rows = width // nseq
    steps = batches * count
    f32, bf16 = jnp.float32, jnp.bfloat16
    V, S, R = pltpu.VMEM, jax.ShapeDtypeStruct, pltpu.SemaphoreType.REGULAR
    smem = pl.BlockSpec(memory_space=pltpu.SMEM)
    message = (2, 264, PAIR)
    blocks = up.shape[0]
    piece = (share_rows, width)
    return pl.pallas_call(
        functools.partial(backward_kernel, count),
        out_shape=(
            S((group, width), f32),
            S((16, width), f32),
            S((batches, 2, 2) + piece, f32),
            S((batches, 2, 2) + piece, bf16),
        ),
        in_specs=[ANY, VMEM, ANY, VMEM] + [ANY] * 7 + [VMEM, smem, smem, ANY],
        out_specs=[VMEM, VMEM, ANY, ANY],
        scratch_shapes=[
            V((2, 2, 2) + piece, bf16),
            V((2, 2, 2) + piece, bf16),
            V((2, 2) + piece, f32),
            V((3, 2) + piece, bf16),
            V((4, 2) + piece, bf16),
            V((2, 2) + piece, f32),
            V((3,) + piece, bf16),
            V((4,) + piece, bf16),
            V((2,) + piece, f32),
            V((count - 1,) + piece, bf16),
            V((batches, count - 1) + piece, bf16),
            V((batches,) + piece, f32),
            V(piece, f32),
            V((width // group, group, width), f32),
            V((blocks, group, width), bf16),
            V((2, blocks, 2 * share_rows, group), bf16),
            V((2, width // group, group, width), bf16),
            V((2, group, width), f32),
            V((group, width), f32),
            V((2, group, width), bf16),
            V((group, width), f32),
            V((group, group), f32),
            V((2, group, PAIR), f32),
            V((16, width), f32),
            V((16, width), f32),
            V(message, f32),
            V(message, f32),
            V(message[1:], f32),
            V((count - 1,) + message[1:], f32),
            V(message, f32),
            V(message, f32),
            V((count + 2, 16, width), f32),
            V((4, 16, width), f32),
            V((count + 2, 16, width), f32),
            V((4, 16, width), f32),
            DMA((32,)),
            DMA((steps,)),
            DMA((steps,)),
            DMA((steps,)),
            DMA((steps,)),
            DMA((steps,)),
            DMA((steps,)),
            DMA((steps,)),
            DMA((batches, count - 1)),
            DMA((batches, count - 1)),
            R,
            R((2,)),
            R((2,)),
            DMA((count + 1,)),
            DMA((count + 1,)),
            DMA((count + 2,)),
            DMA((count + 2,)),
            DMA((count + 2,)),
            DMA((count + 2,)),
            DMA((batches,)),
            DMA((nseq,)),
            DMA((2,)),
            DMA((2,)),
            DMA((2,)),
            DMA((nseq,)),
            DMA((batches,)),
            DMA((batches,)),
            DMA((batches,)),
            DMA((batches,)),
            DMA((batches,)),
        ],
        compiler_params=pltpu.CompilerParams(
            collective_id=1, has_side_effects=True, vmem_limit_bytes=VMEM_LIMIT
        ),
    )(x, dy, w.reshape(-1, width // group, group, width), rows, low, pre, ratio, left, resid, up, act, state, lengths, order,
      momentum.reshape((batches, 2, 2) + piece))


STEP = 10


def padded(vector):
    short = 2048 - vector.shape[-1]
    edges = [(0, 0)] * (vector.ndim - 1) + [(0, short)]
    return jnp.pad(vector, edges).reshape(vector.shape[:-1] + (16, 128))


def local(
    tokens, cotangent, lengths, order, weights, momentum, small_params, moment_one, moment_two
):
    width = tokens.shape[2]
    nseq = lax.axis_size("seq")
    share = small_params.shape[0]
    rounded = lax.reduce_precision(small_params, 8, 7)
    aligned = share % 128 == 0
    if aligned:
        shared = padded(rounded)
    else:
        shared = lax.all_gather(rounded, "seq", axis=0, tiled=True).reshape(-1, width)
    (gathered, block_out, rows, *kept) = forward(
        tokens[0], weights, shared, lengths, order, nseq, aligned
    )
    input_grad, totals, new_momentum, update = backward(
        tokens[0], cotangent[0], gathered, rows, *kept, lengths, order, momentum, nseq
    )
    start = lax.axis_index("seq") * share
    row_small = lax.dynamic_slice(totals[:13].reshape(-1), (start,), (share,))
    new_momentum, update = new_momentum.reshape(weights.shape), update.reshape(weights.shape)
    blocks = (weights.shape[0] - 4) // 2
    rates = jnp.array([0.5] * 3 + [4.0] + [0.5] * blocks + [0.25] * blocks, dtype=jnp.float32)
    new_weights = weights - rates[:, None, None] * (update.astype(jnp.float32) + 0.01 * weights)
    first_new = 0.9 * moment_one + 0.1 * row_small
    second_new = 0.95 * moment_two + 0.05 * row_small * row_small
    adjusted = first_new / (1.0 - 0.9**STEP) / (jnp.sqrt(second_new / (1.0 - 0.95**STEP)) + 1e-08)
    new_small = small_params - 0.05 * (adjusted + 0.01 * small_params)
    return (
        block_out[None], input_grad[None], new_weights, new_momentum, new_small, first_new, second_new,
    )


def solution(mesh):
    in_specs = (
        P("stream", "seq", None),
        P("stream", "seq", None),
        P("stream", None),
        P("stream", None),
        P(None, "seq", None),
        P(None, "seq", None),
        P("seq"),
        P("seq"),
        P("seq"),
    )
    out_specs = (
        P("stream", "seq", None),
        P("stream", "seq", None),
        P(None, "seq", None),
        P(None, "seq", None),
        P("seq"),
        P("seq"),
        P("seq"),
    )
    return jax.shard_map(local, mesh=mesh, in_specs=in_specs, out_specs=out_specs, check_vma=False)
```

```python
import functools

import jax
import jax.numpy as jnp
from jax import lax
from jax.experimental import pallas as pl
from jax.experimental.pallas import tpu as pltpu
from jax.sharding import PartitionSpec as P

MESH = pl.DeviceIdType.MESH
DMA = pltpu.SemaphoreType.DMA
ANY = pl.BlockSpec(memory_space=pl.ANY)
VMEM = pl.BlockSpec(memory_space=pltpu.VMEM)
VMEM_LIMIT = 62 << 20


def places():
    seq = lax.axis_index("seq")
    stream = lax.axis_index("stream")
    return seq // 2, seq % 2, stream // 2, stream % 2


def device(z, x, y, c):
    return {"seq": z * 2 + x, "stream": y * 2 + c}


def greet(peers):
    barrier = pltpu.get_barrier_semaphore()
    for peer in peers:
        pl.semaphore_signal(barrier, inc=1, device_id=peer, device_id_type=MESH)
    pl.semaphore_wait(barrier, len(peers))


def remote(source, target, sent, received, peer):
    return pltpu.make_async_remote_copy(
        src_ref=source,
        dst_ref=target,
        send_sem=sent,
        recv_sem=received,
        device_id=peer,
        device_id_type=MESH,
    )


def others_along_seq(z, x, y, c, count):
    straight = [device(lax.rem(z + k, count), x, y, c) for k in range(1, count)]
    across = [device(lax.rem(z + k, count), 1 - x, y, c) for k in range(count)]
    return straight, across


CHUNK = 32


BAND = 256


def split_two(values):
    high = values.astype(jnp.bfloat16)
    return high, (values - high.astype(jnp.float32)).astype(jnp.bfloat16)


def dot(left, right, transposed=False):
    dims = (((1,), (1 if transposed else 0,)), ((), ()))
    return lax.dot_general(left, right, dims, preferred_element_type=jnp.float32)


LAG = (2, 4, 5)
HALF = 64
PAIR = 128


def matrix(w_ref, batch, index):
    block = w_ref[batch, index // 2, index % 2]
    return block.reshape(block.shape[0] * block.shape[1] * block.shape[2], block.shape[3])


def norm_rows(values, gain, offset):
    center = values - jnp.mean(values, axis=-1, keepdims=True)
    spread = jnp.mean(center * center, axis=-1, keepdims=True)
    return center * lax.rsqrt(spread + 1e-05) * gain + offset


def lanes_of(head):
    lane = lax.broadcasted_iota(jnp.int32, (1, PAIR), 1)
    return (lane // HALF) == head


def block_diagonal():
    row = lax.broadcasted_iota(jnp.int32, (PAIR, PAIR), 0)
    lane = lax.broadcasted_iota(jnp.int32, (PAIR, PAIR), 1)
    return (row // HALF) == (lane // HALF)


def pair_span(index):
    return pl.ds(pl.multiple_of(index * PAIR, PAIR), PAIR)


def band_span(index):
    return pl.ds(pl.multiple_of(index * BAND, BAND), BAND)


def dot_down(left, right):
    return lax.dot_general(left, right, (((0,), (0,)), ((), ())), preferred_element_type=jnp.float32)


def pack_message(left_ref, right_ref, scale_ref, row_ref, message):
    diagonal = block_diagonal()
    for j in range(4):
        parts = []
        for p in (2 * j, 2 * j + 1):
            lanes = slice(p * PAIR, (p + 1) * PAIR)
            scale = scale_ref[...]
            left = (left_ref[:, lanes].astype(jnp.float32) * scale).astype(jnp.bfloat16)
            parts.append(dot_down(left, right_ref[:, lanes]))
            if row_ref is None:
                total = jnp.sum(left.astype(jnp.float32), axis=0, keepdims=True)
            else:
                total = jnp.sum(left.astype(jnp.float32) * row_ref[:, lanes], axis=0, keepdims=True)
            for half in range(2):
                message[half, 256 + p : 257 + p, :] = total
        block = jnp.where(diagonal, parts[0], pltpu.roll(parts[1], HALF, 1))
        message[j // 2, (j % 2) * PAIR : (j % 2 + 1) * PAIR, :] = block


def unpack_message(message, p):
    diagonal = block_diagonal()
    j = p // 2
    block = message[j // 2, (j % 2) * PAIR : (j % 2 + 1) * PAIR, :]
    if p % 2:
        block = pltpu.roll(block, HALF, 1)
    block = jnp.where(diagonal, block, 0.0)
    row = message[0, 256 + p : 257 + p, :]
    column = jnp.transpose(jnp.broadcast_to(row, (PAIR, PAIR)))
    return block, jnp.where(diagonal, column, 0.0)


class Relay:
    def __init__(self, count, coef, own, across, part, spread, total, result, sems, places_):
        self.count, self.coef, self.own, self.across = count, coef, own, across
        self.part, self.spread, self.total, self.result = part, spread, total, result
        self.send, self.recv = sems
        self.z, self.x, self.y, self.c = places_
        self.pair = device(self.z, 1 - self.x, self.y, self.c)

    def swap(self):
        self.first = remote(self.own, self.across, self.send.at[0], self.recv.at[0], self.pair)
        self.first.start()

    def spread_out(self):
        self.first.wait_recv()
        self.part[...] = self.coef[0] * self.own[self.x] + self.coef[1] * self.across[self.x]
        self.copies = []
        for k in range(1, self.count):
            peer = device(lax.rem(self.z + k, self.count), self.x, self.y, self.c)
            copy = remote(self.part, self.spread.at[k - 1], self.send.at[k], self.recv.at[k], peer)
            copy.start()
            self.copies.append(copy)

    def join(self):
        total = jnp.zeros_like(self.part)
        for k, copy in enumerate(self.copies):
            copy.wait_recv()
            total = total + self.coef[4 + k] * self.spread[k]
        self.total[self.x] = total
        half = self.total.at[self.x]
        self.last = remote(half, half, self.send.at[self.count], self.recv.at[self.count], self.pair)
        self.last.start()

    def finish(self):
        self.last.wait_recv()
        for half in range(2):
            self.result[half] = self.coef[2] * self.total[half] + self.coef[3] * self.across[half]

    def wait_sends(self):
        for copy in [self.first, self.last] + self.copies:
            copy.wait_send()


def head_scores(q_ref, k_ref, keep_ref, lanes, head, band):
    rows = slice(band * BAND, (band + 1) * BAND)
    upto = slice(0, (band + 1) * BAND)
    query = jnp.where(lanes_of(head), q_ref[rows, lanes], 0)
    return dot(query, k_ref[upto, lanes], True) * keep_ref[rows, upto]


def attend_pair(p, q_ref, k_ref, v_ref, keep_ref, num_ref, den_ref):
    lanes = pair_span(p)
    group = q_ref.shape[0]
    value = v_ref[:, lanes]
    first = lanes_of(0)
    for band in range(group // BAND):
        rows = slice(band * BAND, (band + 1) * BAND)
        sums, totals = [], []
        for head in range(2):
            scores = head_scores(q_ref, k_ref, keep_ref, lanes, head, band)
            totals.append(jnp.sum(scores, axis=1, keepdims=True))
            sums.append(dot(scores.astype(jnp.bfloat16), value[: (band + 1) * BAND]))
        num_ref[rows, lanes] = jnp.where(first, sums[0], sums[1])
        den_ref[rows, lanes] = jnp.where(first, totals[0], totals[1])


def image_ends(lengths_ref, order_ref):
    images = lengths_ref.shape[1]
    ends, running = [], jnp.int32(0)
    for j in range(images):
        for i in range(images):
            running = running + jnp.where(order_ref[0, j] == i, lengths_ref[0, i], 0)
        ends.append(running)
    return ends


def segment_at(ends, positions):
    found = jnp.zeros_like(positions)
    for end in ends:
        found = found + jnp.where(positions >= end, 1, 0)
    return found


def same(left, right):
    return jnp.where(left == right, 1.0, 0.0)


def fill_masks(ends, start, group, keep_ref, flags_ref):
    for band in range(group // BAND):
        rows = slice(band * BAND, (band + 1) * BAND)
        down = lax.broadcasted_iota(jnp.int32, (BAND, group), 0) + band * BAND
        along = lax.broadcasted_iota(jnp.int32, (BAND, group), 1)
        mine = segment_at(ends, down + start)
        theirs = segment_at(ends, along + start)
        keep_ref[rows, :] = jnp.where(along <= down, same(mine, theirs), 0.0)
        narrow = mine[:, :PAIR]
        flags_ref[0, rows, :] = same(narrow, segment_at(ends, start - 1))
        flags_ref[1, rows, :] = same(narrow, segment_at(ends, start + group - 1))


def pass_at(ends, block, group):
    return same(segment_at(ends, block * group + group - 1), segment_at(ends, block * group - 1))


def forward_factors(ends, group, count, z, x):
    both = [pass_at(ends, 2 * z, group), pass_at(ends, 2 * z + 1, group)]
    near = [jnp.where(x == 0, both[1], 1.0), jnp.where(x == 0, 1.0, both[1])]
    near += [jnp.where(x == 0, 1.0, both[0]), jnp.where(x == 0, 0.0, 1.0)]
    running, far = jnp.float32(1.0), []
    for k in range(1, count):
        far.append(jnp.where(z - k >= 0, running, 0.0))
        there = jnp.maximum(z - k, 0)
        running = running * pass_at(ends, 2 * there, group) * pass_at(ends, 2 * there + 1, group)
    return near + far


def backward_factors(ends, group, count, z, x):
    both = [pass_at(ends, 2 * z, group), pass_at(ends, 2 * z + 1, group)]
    near = [jnp.where(x == 0, 1.0, both[0]), jnp.where(x == 0, both[0], 1.0)]
    near += [jnp.where(x == 0, both[1], 1.0), jnp.where(x == 0, 1.0, 0.0)]
    running, ahead = jnp.float32(1.0), []
    for k in range(1, count):
        ahead.append(jnp.where(z + k < count, running, 0.0))
        there = jnp.minimum(z + k, count - 1)
        running = running * pass_at(ends, 2 * there, group) * pass_at(ends, 2 * there + 1, group)
    return near + ahead[::-1]


def forward_kernel(
    count, aligned, x_ref, w_ref, small_ref, lengths_ref, order_ref,
    w_out, out_ref, rows_ref, low_ref, pre_ref, ratio_ref, left_ref, resid_ref, up_ref, act_ref, state_ref,
    w_all, stage, small_in, keep, flags, h1, q, k, v, num, den, o, resid, h2, act, turned, act_turned, message, across, part, spread, total_ref, state,
    load_sem, out_sem, zs, zr, ps, pr, ss, sr, rs, rr,
):
    z, x, y, c = places()
    straight, far = others_along_seq(z, x, y, c, count)
    pair = [device(z, 1 - x, y, c), device(z, x, 1 - y, c), device(z, x, y, 1 - c)]
    batches = w_ref.shape[0]
    rows, width = w_ref.shape[3:]
    group = x_ref.shape[0]
    bands = group // BAND
    loads = []
    for b in range(batches):
        for i in range(4):
            copy = pltpu.make_async_copy(
                w_ref.at[b, i // 2, i % 2],
                stage.at[b, pl.ds(i * rows, rows)],
                load_sem.at[b, i],
            )
            copy.start()
            loads.append(copy)
    greet(straight + far + pair[1:])
    small = []
    if aligned:
        for j, peer in enumerate(straight + far):
            small.append(remote(small_ref, small_in.at[z * 2 + x], ss.at[j], sr.at[j], peer))
            small[-1].start()
        small_in[z * 2 + x] = small_ref[...]
    spread_w = {}

    def cast_own(b):
        for i in range(4):
            loads[b * 4 + i].wait()
            for j in range(rows // CHUNK):
                span = slice(j * CHUNK, (j + 1) * CHUNK)
                at = slice(i * rows + j * CHUNK, i * rows + (j + 1) * CHUNK)
                w_all[b, i // 2, i % 2, z, x, span, :] = stage[b, at, :].astype(jnp.bfloat16)

    def send_own(b):
        for j in range(1, count):
            block = w_all.at[b, y, c, z, x]
            spread_w[b, j] = remote(block, block, zs.at[b, j - 1], zr.at[b, j - 1], straight[j - 1])
            spread_w[b, j].start()

    first, second, third, outs, waited = [], [], [], [], []
    plan = [(b, 0) for b in range(batches)]
    plan += [(b, j) for b in range(batches) for j in range(1, count)]
    total = len(plan)

    def send(kept, phase, index, block, peer):
        kept.append(remote(block, block, ps.at[phase, index], pr.at[phase, index], peer))
        kept[-1].start()

    def put_out(source, target):
        copy = pltpu.make_async_copy(source, target, out_sem.at[len(outs)])
        copy.start()
        outs.append(copy)
        return copy

    def tick(step):
        index = step
        if index < total:
            b, j = plan[index]
            there = lax.rem(z - j + count, count)
            if j:
                spread_w[b, j].wait_recv()
            send(first, 0, index, w_all.at[b, y, c, there, x], pair[(j + b) % 2 if j else 0])
            if j == min(1, count - 1) and b + 1 < batches:
                send_own(b + 1)
        index = step - LAG[0]
        if 0 <= index < total:
            b, j = plan[index]
            there = lax.rem(z - j + count, count)
            first[index].wait_recv()
            if j == 0:
                send(second, 1, index, w_all.at[b, y, c, z, 1 - x], pair[1])
            elif (j + b) % 2 == 0:
                send(second, 1, index, w_all.at[b, y, c, there], pair[1])
            else:
                send(second, 1, index, w_all.at[b, :, c, there, x], pair[0])
        index = step - LAG[1]
        if 0 <= index < total:
            b, j = plan[index]
            there = lax.rem(z - j + count, count)
            second[index].wait_recv()
            block = w_all.at[b, :, c, z, 1 - x] if j == 0 else w_all.at[b, :, c, there]
            send(third, 2, index, block, pair[2])
        index = step - LAG[2]
        if 0 <= index < total:
            b, j = plan[index]
            there = lax.rem(z - j + count, count)
            third[index].wait_recv()
            put_out(w_all.at[b, :, :, there], w_out.at[b, :, :, there])

    cast_own(0)
    send_own(0)
    tick(0)
    for b in range(1, batches):
        cast_own(b)
        tick(b)
    if aligned:
        for copy in small:
            copy.wait_recv()
        share_rows = 13 * 1024 // 128 // (count * 2)
        for j in range(13 * 8):
            rows_ref[j // 8 : j // 8 + 1, (j % 8) * 128 : (j % 8 + 1) * 128] = small_in[
                j // share_rows, j % share_rows : j % share_rows + 1, :
            ]
    else:
        rows_ref[0:13, :] = small_ref[...]

    def vector(index):
        return rows_ref[index : index + 1, :]

    def norm_one(i, carry):
        span = band_span(i)
        value = norm_rows(x_ref[span, :].astype(jnp.float32), vector(0), vector(1))
        value = value.astype(jnp.bfloat16)
        h1[span, :] = value
        turned[0, :, span] = jnp.transpose(value.astype(jnp.float32) - vector(1)).astype(jnp.bfloat16)
        return carry

    lax.fori_loop(0, bands, norm_one, 0)
    ends = image_ends(lengths_ref, order_ref)
    fill_masks(ends, (z * 2 + x) * group, group, keep, flags)
    factors = forward_factors(ends, group, count, z, x)
    ready = batches + count - 1 + LAG[2]
    for step in range(batches, ready):
        tick(step)

    def project(i, carry):
        span = band_span(i)
        left = h1[span, :]
        for index, low in ((0, q), (1, k)):
            pre = dot(left, matrix(w_all, 0, index)) + vector(4 + index)
            stage[index, span, :] = pre
            low[span, :] = jnp.where(pre > 0, pre + 1.0, jnp.exp(jnp.minimum(pre, 0.0))).astype(jnp.bfloat16)
        v[span, :] = (dot(left, matrix(w_all, 0, 2)) + vector(6)).astype(jnp.bfloat16)
        return carry

    lax.fori_loop(0, bands, project, 0)
    guess = jnp.broadcast_to(vector(1), (16, width)).astype(jnp.bfloat16)
    guess = dot(guess, matrix(w_all, 0, 2))[0:1, :] + vector(6)
    rows_ref[13:14, :] = guess.astype(jnp.bfloat16).astype(jnp.float32)
    pack_message(k, v, flags.at[1], None, message)
    relay = Relay(count, factors, message, across, part, spread, total_ref, state, (rs, rr), (z, x, y, c))
    relay.swap()
    stored = [put_out(stage.at[0], pre_ref.at[0]), put_out(stage.at[1], pre_ref.at[1]), None]
    for index, low in enumerate((q, k, v)):
        put_out(low, low_ref.at[index])

    def attend(p, carry):
        attend_pair(p, q, k, v, keep, num, den)
        return carry

    pairs = width // PAIR
    step = ready
    lax.fori_loop(0, pairs // 4, attend, 0)
    tick(step)
    relay.spread_out()
    lax.fori_loop(pairs // 4, pairs // 2, attend, 0)
    tick(step + 1)
    lax.fori_loop(pairs // 2, pairs, attend, 0)
    relay.join()
    tick(step + 2)
    relay.finish()
    put_out(state, state_ref)
    for p in range(pairs):
        block, column = unpack_message(state, p)
        high, low = split_two(jnp.concatenate([block, column], axis=1))
        lanes = slice(p * PAIR, (p + 1) * PAIR)
        for i in range(bands):
            span = slice(i * BAND, (i + 1) * BAND)
            query = q[span, lanes]
            both = dot(query, high) + dot(query, low)
            flag = flags[0, span, :]
            top = num[span, lanes] + flag * both[:, :PAIR]
            bottom = den[span, lanes] + flag * both[:, PAIR:]
            num[span, lanes] = top
            den[span, lanes] = bottom
            o[span, lanes] = (top / bottom).astype(jnp.bfloat16)
    put_out(num, ratio_ref.at[0])
    put_out(den, ratio_ref.at[1])

    def close(i, carry):
        span = band_span(i)
        value = x_ref[span, :].astype(jnp.float32) + dot(o[span, :], matrix(w_all, 0, 3)) + vector(7)
        resid[span, :] = value
        hidden = norm_rows(value, vector(2), vector(3)).astype(jnp.bfloat16)
        h2[span, :] = hidden
        turned[2, :, span] = jnp.transpose(hidden.astype(jnp.float32) - vector(3)).astype(jnp.bfloat16)
        turned[1, :, span] = jnp.transpose(o[span, :].astype(jnp.float32) - vector(13)).astype(jnp.bfloat16)
        return carry

    lax.fori_loop(0, bands, close, 0)
    put_out(turned, left_ref)
    put_out(resid, resid_ref)
    step = step + 3
    ready = batches + 2 * (count - 1) + LAG[2]
    while step < ready:
        tick(step)
        step += 1
    blocks = act.shape[0]
    turned_out = []
    for j in range(blocks):
        if j > 1:
            turned_out[j - 2].wait()
            waited.append(turned_out[j - 2])
        if stored[j % 3] is not None:
            stored[j % 3].wait()
            waited.append(stored[j % 3])

        def expand(i, carry):
            span = band_span(i)
            pre = dot(h2[span, :], matrix(w_all, 1, j)) + vector(9 + j)
            stage[j % 3, span, :] = pre
            value = jax.nn.gelu(pre)
            act[j, span, :] = value.astype(jnp.bfloat16)
            act_turned[j % 2, :, span] = jnp.transpose(value).astype(jnp.bfloat16)
            return carry

        lax.fori_loop(0, bands, expand, 0)
        stored[j % 3] = put_out(stage.at[j % 3], up_ref.at[j])
        turned_out.append(put_out(act_turned.at[j % 2], act_ref.at[j]))
        if step < total + LAG[2]:
            tick(step)
            step += 1
    while step < total + LAG[2]:
        tick(step)
        step += 1

    def project_down(i, carry):
        span = band_span(i)
        value = resid[span, :] + vector(8)
        for j in range(blocks):
            value += dot(act[j, span, :], matrix(w_all, 2, j))
        out_ref[span, :] = value.astype(jnp.bfloat16)
        return carry

    lax.fori_loop(0, bands, project_down, 0)
    for copy in outs:
        if not any(copy is other for other in waited):
            copy.wait()
    for copy in list(spread_w.values()) + first + second + third + small:
        copy.wait_send()
    relay.wait_sends()


def forward(x, weights, small, lengths, order, nseq, aligned):
    group, width = x.shape
    units, rows, _ = weights.shape
    count, batches = nseq // 2, units // 4
    steps = batches * count
    f32, bf16 = jnp.float32, jnp.bfloat16
    V, S = pltpu.VMEM, jax.ShapeDtypeStruct
    blocks = 4
    smem = pl.BlockSpec(memory_space=pltpu.SMEM)
    message = (2, 264, PAIR)
    return pl.pallas_call(
        functools.partial(forward_kernel, count, aligned),
        out_shape=(
            S((batches, 2, 2, count, 2, rows, width), bf16),
            S((group, width), bf16),
            S((16, width), f32),
            S((3, group, width), bf16),
            S((2, group, width), f32),
            S((2, group, width), f32),
            S((3, width, group), bf16),
            S((group, width), f32),
            S((blocks, group, width), f32),
            S((blocks, width, group), bf16),
            S(message, f32),
        ),
        in_specs=[VMEM, ANY, VMEM, smem, smem],
        out_specs=[ANY, VMEM, VMEM] + [ANY] * 8,
        scratch_shapes=[
            V((batches, 2, 2, count, 2, rows, width), bf16),
            V((3, group, width), f32),
            V(((nseq,) if aligned else ()) + small.shape, f32),
            V((group, group), f32),
            V((2, group, PAIR), f32),
            V((group, width), bf16),
            V((group, width), bf16),
            V((group, width), bf16),
            V((group, width), bf16),
            V((group, width), f32),
            V((group, width), f32),
            V((group, width), bf16),
            V((group, width), f32),
            V((group, width), bf16),
            V((blocks, group, width), bf16),
            V((3, width, group), bf16),
            V((2, width, group), bf16),
            V(message, f32),
            V(message, f32),
            V(message[1:], f32),
            V((count - 1,) + message[1:], f32),
            V(message, f32),
            V(message, f32),
            DMA((batches, 4)),
            DMA((steps + 20,)),
            DMA((batches, count - 1)),
            DMA((batches, count - 1)),
            DMA((3, steps)),
            DMA((3, steps)),
            DMA((nseq - 1,)),
            DMA((nseq - 1,)),
            DMA((count + 1,)),
            DMA((count + 1,)),
        ],
        compiler_params=pltpu.CompilerParams(
            collective_id=0, has_side_effects=True, vmem_limit_bytes=VMEM_LIMIT
        ),
    )(x, weights.reshape(batches, 2, 2, rows, width), small, lengths, order)


def gelu_slope(values):
    cube = 0.044715 * values * values
    bend = jnp.tanh(0.7978845608028654 * values * (1.0 + cube))
    return 0.5 * (1.0 + bend) + 0.5 * values * (1.0 - bend * bend) * (
        0.7978845608028654 * (1.0 + 3.0 * cube)
    )


def norm_back(values, upstream, gain):
    center = values - jnp.mean(values, axis=-1, keepdims=True)
    spread = jnp.mean(center * center, axis=-1, keepdims=True)
    scale = lax.rsqrt(spread + 1e-05)
    unit = center * scale
    inner = upstream * gain
    back = inner - jnp.mean(inner, axis=-1, keepdims=True)
    back = scale * (back - unit * jnp.mean(inner * unit, axis=-1, keepdims=True))
    return back, unit


def pick_message(message, p):
    down = pl.ds(pl.multiple_of(((p // 2) % 2) * PAIR, PAIR), PAIR)
    block = message[p // 4, down, :]
    block = jnp.where(p % 2 == 1, pltpu.roll(block, HALF, 1), block)
    block = jnp.where(block_diagonal(), block, 0.0)
    return split_two(block), message[0, pl.ds(256 + p, 1), :]


SHIFTS = (0.0, 0.0, 0.1, 0.7, 0.7)
TALL = 256
SHORT = 256


def split_rows(ref, start, count):
    size = ref.shape[-2]
    return ref.at[start // size, pl.ds(pl.multiple_of(lax.rem(start, size), count), count)]


def orthogonalize(high_ref, low_ref, full, held, gram, gram_low, order, late, finished):
    size = full.shape[-1]

    def whole(ref):
        return ref[...].reshape(size, size)

    def band_of(ref, index, height=TALL):
        return split_rows(ref, index * height, height)

    def square(index, total):
        part = band_of(high_ref, index)[...].astype(jnp.float32)
        return total + jnp.sum(part * part)

    norm = jnp.sqrt(lax.fori_loop(0, size // TALL, square, jnp.float32(0.0)))
    scale = 1.0 / (norm + 1e-07)

    def begin(index, carry):
        part = band_of(high_ref, index)[...].astype(jnp.float32) * scale
        band_of(full, index)[...] = part
        band_of(held.at[0], index)[...] = part.astype(jnp.bfloat16)
        return carry

    lax.fori_loop(0, size // TALL, begin, 0)
    turns = len(SHIFTS)
    for turn in range(turns):
        shift, last = SHIFTS[turn], turn + 1 == turns
        now, later = held.at[turn % 2], held.at[1 - turn % 2]

        def form(index, carry):
            block = dot(band_of(now, index)[...], whole(now), True)
            if shift:
                across = lax.broadcasted_iota(jnp.int32, block.shape, 1)
                down = lax.broadcasted_iota(jnp.int32, block.shape, 0) + index * TALL
                block = jnp.where(across == down, block - shift, block)
            band_of(gram, index)[...] = block
            band_of(gram_low, index)[...] = block.astype(jnp.bfloat16)
            return carry

        lax.fori_loop(0, size // TALL, form, 0)
        linear = -4.775 + 2.0 * 2.0315 * shift
        scaled = 3.4445 - 4.775 * shift + 2.0315 * shift * shift
        height = SHORT if last else TALL

        def advance(index, carry):
            part = order(index, size // height) if last else index
            poly = linear * band_of(gram, part, height)[...]
            poly = poly + 2.0315 * dot(band_of(gram_low, part, height)[...], whole(gram_low))
            step = dot(poly.astype(jnp.bfloat16), whole(now))
            moved = scaled * band_of(full, part, height)[...] + step
            if not last:
                band_of(full, part, height)[...] = moved
            band_of(later, part, height)[...] = moved.astype(jnp.bfloat16)
            if last:
                finished(part, height)
            return carry

        lax.fori_loop(0, size // height, advance, 0)
        factor = scaled * (scale if turn == 0 else factor)
        if turn == 1:
            late()

            def join(index, carry):
                part = band_of(full, index)[...] + factor * band_of(low_ref, index)[...].astype(jnp.float32)
                band_of(full, index)[...] = part
                band_of(later, index)[...] = part.astype(jnp.bfloat16)
                return carry

            lax.fori_loop(0, size // TALL, join, 0)


LAGS = (("d", "e", 2), ("c", "d", 2), ("b", "c", 2), ("a", "b", 1))


class Sums:
    def __init__(self, count, place, product, bufs, sems, sums_ref):
        self.count = count
        self.z, self.x, self.y, self.c = z, x, y, c = place
        self.product, self.sums_ref = product, sums_ref
        (self.core_out, self.core_in, self.own, self.first_out, self.first_in, self.kept_one,
         self.second_out, self.second_in, self.kept_two, self.far_out, self.far_in) = bufs
        (self.cs, self.cr, self.fs, self.fr, self.es, self.er, self.zs, self.zr,
         self.credit_core, self.credit_first, self.credit_second) = sems
        self.pair = [device(z, 1 - x, y, c), device(z, x, 1 - y, c), device(z, x, y, 1 - c)]
        self.steps = [(b, k) for b in (2, 1, 0) for k in range(count)]
        self.total = len(self.steps)
        self.cores, self.firsts, self.seconds, self.fars = [], [], [], {}
        self.rows = sums_ref.shape[1]
        self.beat = 0
        self.done = {name: 0 for name in "abcde"}
        self.stamp = {}
        self.needs = {"a": (("b", 1),), "b": (("c", 2),), "c": (("d", 2),)}

    def there(self, i):
        return lax.rem(self.z + 1 + self.steps[i][1], self.count)

    def give(self, semaphore, peer):
        pl.semaphore_signal(semaphore, inc=1, device_id=peer, device_id_type=MESH)

    def take(self, semaphore):
        pl.semaphore_wait(semaphore, 1)

    def add(self, base, got, target):
        def body(index, carry):
            at = pl.ds(pl.multiple_of(index * CHUNK, CHUNK), CHUNK)
            target[at, :] = (base[at, :] + got[at, :].astype(jnp.float32)).astype(target.dtype)
            return carry

        lax.fori_loop(0, self.rows // CHUNK, body, 0)

    def stage_a(self, i):
        slot = i % 2
        batch = self.steps[i][0]
        if i >= 2:
            self.cores[i - 2].wait_send()
        for yy in range(2):
            value = self.product(i, batch, yy, 1 - self.c).astype(jnp.bfloat16)
            for xx in range(2):
                self.core_out[slot, yy, xx] = value[xx * self.rows : (xx + 1) * self.rows]
        if i >= 2:
            self.take(self.credit_core)
        source, target = self.core_out.at[slot], self.core_in.at[slot]
        self.cores.append(remote(source, target, self.cs.at[i], self.cr.at[i], self.pair[2]))
        self.cores[i].start()
        for yy in range(2):
            value = self.product(i, batch, yy, self.c)
            for xx in range(2):
                self.own[yy, xx] = value[xx * self.rows : (xx + 1) * self.rows]

    def stage_b(self, i):
        slot = i % 2
        k = self.steps[i][1]
        x, y = self.x, self.y
        self.cores[i].wait_recv()
        if i >= 3:
            self.firsts[i - 3].wait_send()
        out = self.first_out.at[i % 3]
        for j in range(2):
            away, near = ((1 - y, j), (y, j)) if k % 2 == 0 else ((j, 1 - x), (j, x))
            self.add(self.own.at[away], self.core_in.at[(slot,) + away], out.at[j])
            self.add(self.own.at[near], self.core_in.at[(slot,) + near], self.kept_one.at[i % 2, j])
        if i + 2 < self.total:
            self.give(self.credit_core, self.pair[2])
        if i >= 4:
            self.take(self.credit_first.at[i % 2])
        peer = self.pair[1 - k % 2]
        self.firsts.append(remote(out, self.first_in.at[i % 4], self.fs.at[i], self.fr.at[i], peer))
        self.firsts[i].start()

    def stage_c(self, i):
        k = self.steps[i][1]
        mine = self.x if k % 2 == 0 else self.y
        self.firsts[i].wait_recv()
        if i >= 3:
            self.seconds[i - 3].wait_send()
        out = self.second_out.at[i % 3]
        kept, got = self.kept_one.at[i % 2], self.first_in.at[i % 4]
        self.add(kept.at[1 - mine], got.at[1 - mine], out)
        self.add(kept.at[mine], got.at[mine], self.kept_two.at[i % 2])
        if i + 4 < self.total:
            self.give(self.credit_first.at[i % 2], self.pair[1 - k % 2])
        if i >= 4:
            self.take(self.credit_second.at[i % 2])
        copy = remote(out, self.second_in.at[i % 4], self.es.at[i], self.er.at[i], self.pair[k % 2])
        copy.start()
        self.seconds.append(copy)

    def stage_d(self, i):
        b, k = self.steps[i]
        self.seconds[i].wait_recv()
        kept, got = self.kept_two.at[i % 2], self.second_in.at[i % 4]
        if k < self.count - 1:
            if i >= self.count:
                self.fars[i - self.count].wait_send()
            out = self.far_out.at[k]
            self.add(kept, got, out)
            peer = device(self.there(i), self.x, self.y, self.c)
            self.fars[i] = remote(out, self.far_in.at[b, k], self.zs.at[b, k], self.zr.at[b, k], peer)
            self.fars[i].start()
        else:
            self.add(kept, got, self.sums_ref.at[b])
        if i + 4 < self.total:
            self.give(self.credit_second.at[i % 2], self.pair[k % 2])

    def stage_e(self, i):
        b, k = self.steps[i]
        if k < self.count - 1:
            return
        for j in range(self.count - 1):
            self.fars[i - self.count + 1 + j].wait_recv()
            self.add(self.sums_ref.at[b], self.far_in.at[b, j], self.sums_ref.at[b])

    def run(self, name):
        i = self.done[name]
        for other, back in self.needs.get(name, ()):
            while self.done[other] <= i - back:
                self.run(other)
        getattr(self, "stage_" + name)(i)
        self.done[name] = i + 1
        self.stamp[name, i] = self.beat

    def pump(self, make=False):
        self.beat += 1
        for before, name, lag in LAGS:
            while self.done[name] < self.done[before]:
                if self.beat - self.stamp[before, self.done[name]] < lag:
                    break
                self.run(name)
        if make:
            self.run("a")

    def wait_sends(self):
        for copy in self.cores[-2:] + self.firsts[-3:] + self.seconds[-3:]:
            copy.wait_send()
        for i, copy in self.fars.items():
            if i >= self.total - self.count:
                copy.wait_send()


class Totals:
    def __init__(self, count, place, own, got, kept, send, recv):
        z, x, y, c = place
        self.peers = [
            [device(z, 1 - x, y, c)],
            [device(lax.rem(z + k, count), x, y, c) for k in range(1, count)],
            [device(z, x, 1 - y, c)],
            [device(z, x, y, 1 - c)],
        ]
        self.own, self.got, self.kept, self.sems = own, got, kept, (send, recv)
        self.stage, self.copies, self.pending = 0, [], []

    def source(self):
        return self.own if self.stage == 0 else self.kept.at[self.stage - 1]

    def send(self, stage):
        self.stage, self.pending = stage, []
        for peer in self.peers[stage]:
            index = len(self.copies)
            copy = remote(
                self.source(), self.got.at[index], self.sems[0].at[index], self.sems[1].at[index], peer
            )
            copy.start()
            self.copies.append(copy)
            self.pending.append(index)

    def receive(self):
        total = self.source()[...]
        for index in self.pending:
            self.copies[index].wait_recv()
            total = total + self.got[index]
        self.kept[self.stage] = total

    def value(self):
        return self.kept[self.stage]

    def wait_sends(self):
        for copy in self.copies:
            copy.wait_send()


def restore_mean(target, rows_ref, totals, b, place):
    z, x, y, c = place
    rows, width = target.shape
    stream = y * 2 + c
    across = lax.broadcasted_iota(jnp.int32, (width, rows), 1) + (z * 2 + x) * rows
    chosen = jnp.where(lax.broadcasted_iota(jnp.int32, (width, rows), 0) == across, 1.0, 0.0)
    if b == 0:
        vector = jnp.where(stream == 3, rows_ref[13:14, :], rows_ref[1:2, :])
    else:
        vector = rows_ref[3:4, :]
    head = lax.broadcasted_iota(jnp.int32, (16, width), 0)
    left = jnp.where(head < 3, jnp.broadcast_to(vector, (16, width)), 0.0).astype(jnp.bfloat16)
    left = dot(left, chosen.astype(jnp.bfloat16)).astype(jnp.bfloat16)
    at = (4 if b == 0 else 9) + stream
    row = jnp.sum(jnp.where(head == at, totals[...], 0.0), axis=0, keepdims=True)
    high = row.astype(jnp.bfloat16).astype(jnp.float32)
    middle = (row - high).astype(jnp.bfloat16).astype(jnp.float32)
    right = jnp.where(head == 0, high, jnp.where(head == 1, middle, jnp.where(head == 2, row - high - middle, 0.0)))
    target[...] = target[...] + dot_down(left, right.astype(jnp.bfloat16))


def backward_kernel(
    count, x_ref, dy_ref, w_ref, rows_ref, low_ref, pre_ref, ratio_ref, left_ref, resid_ref, up_ref, act_ref,
    state, lengths_ref, order_ref, mom_ref,
    grad_ref, small_out, all_ref, ortho_ref,
    core_out, core_in, own, first_out, first_in, kept_one, second_out, second_in, kept_two, far_out, far_in,
    sums_ref, mom_own, staged, m_high, m_low, full, big, left, wbuf, ubuf, extra, keep, flags, gs, gs_early,
    message, across, part, spread, total_ref, state_back, small_got, small_sum, early_got, early_sum,
    load_sem, lt_sem, cs, cr, fs, fr, es, er, zs, zr, credit_core, credit_first, credit_second, rs, rr, ms, mr,
    hs, hr, vs, vr, self_sem, ys, yr, os_, or_, js, jr, ks, kr,
):
    place = z, x, y, c = places()
    straight, far = others_along_seq(z, x, y, c, count)
    pair = [device(z, 1 - x, y, c), device(z, x, 1 - y, c), device(z, x, y, 1 - c)]
    group, width = dy_ref.shape
    bands = group // BAND
    pairs = width // PAIR
    block_rows = 2 * sums_ref.shape[1]
    f32, bf16 = jnp.float32, jnp.bfloat16
    issued = []
    dnum, da = extra.at[0], extra.at[1]
    acc, dden = full.at[0], full.at[1]
    dq_low = dnum
    nseq, batches = count * 2, sums_ref.shape[0]
    rows = sums_ref.shape[1]
    seq = z * 2 + x
    owner = [jnp.where(c == 0, low, high) for low, high in ((2, 5), (3, 4), (1, 6))]
    is_owner = (seq == owner[0]) | (seq == owner[1]) | (seq == owner[2])

    def load(source, target):
        copy = pltpu.make_async_copy(source, target, load_sem.at[len(issued)])
        copy.start()
        issued.append(copy)
        return copy

    def load_left(i):
        b = sums.steps[i][0]
        at = pl.ds(pl.multiple_of(sums.there(i) * block_rows, block_rows), block_rows)
        slot = left.at[i % 2]
        if b == 2:
            pieces = [(act_ref.at[:, at], slot)]
        elif b == 1:
            pieces = [(left_ref.at[pl.ds(2, 1), at], slot.at[pl.ds(0, 1)])]
        else:
            pieces = [(left_ref.at[pl.ds(0, 2), at], slot.at[pl.ds(0, 2)])]
        copies = [pltpu.make_async_copy(s, t, lt_sem.at[i]) for s, t in pieces]
        for copy in copies:
            copy.start()
        return copies

    lefts = {}

    def product(i, batch, yy, cc):
        unit = 2 * yy + cc
        if batch == 2:
            lhs, rhs = left[i % 2, unit], dy_ref[...]
        elif batch == 1:
            lhs, rhs = left[i % 2, 0], big[unit]
        else:
            lhs, rhs = left[i % 2, yy * cc], big[unit]
        return dot(lhs, rhs)

    sums = Sums(
        count, place, product,
        (core_out, core_in, own, first_out, first_in, kept_one, second_out, second_in, kept_two, far_out, far_in),
        (cs, cr, fs, fr, es, er, zs, zr, credit_core, credit_first, credit_second), sums_ref,
    )

    placed, mom_loads = [], []

    halves = (m_high, m_low)

    def moved_copy(b, half):
        target = {"seq": owner[b], "stream": y * 2 + c}
        block = split_rows(halves[half], seq * rows, rows)
        return remote(staged.at[b, half], block, vs.at[b, half], vr.at[half, seq], target)

    def place_batch(b, totals):
        if totals is not None:
            restore_mean(sums_ref.at[b], rows_ref, totals, b, place)
        mom_loads[-1].wait()
        placed.append(b)

        def body(index, carry):
            at = pl.ds(pl.multiple_of(index * CHUNK, CHUNK), CHUNK)
            moved = 0.5 * mom_own[at, :] + sums_ref[b, at, :]
            sums_ref[b, at, :] = moved
            high, low = split_two(moved)
            staged[b, 0, at, :] = high
            staged[b, 1, at, :] = low
            return carry

        lax.fori_loop(0, rows // CHUNK, body, 0)
        if b:
            mom_loads.append(load(mom_ref.at[b - 1, y, c], mom_own))

        @pl.when(seq != owner[b])
        def _():
            moved_copy(b, 0).start()

        @pl.when(seq == owner[b])
        def _():
            for half in range(2):
                split_rows(halves[half], seq * rows, rows)[...] = staged[b, half]

    def pump(make=False):
        i = sums.done["a"]
        if make:
            for copy in lefts[i]:
                copy.wait()
            if i + 1 < sums.total:
                lefts[i + 1] = load_left(i + 1)
        sums.pump(make)
        if sums.done["e"] >= count and 2 not in placed:
            place_batch(2, None)

    def make_until(limit):
        while sums.done["a"] < limit:
            pump(True)

    lefts[0] = load_left(0)
    blocks = big.shape[0]
    w_loads = {(2, j): load(w_ref.at[8 + j], wbuf.at[j]) for j in range(2)}
    u_loads = {j: load(up_ref.at[j], ubuf.at[j]) for j in range(2)}
    resid_load = load(resid_ref, grad_ref)
    mom_loads.append(load(mom_ref.at[2, y, c], mom_own))
    greet(straight + far + pair[1:])
    ends = image_ends(lengths_ref, order_ref)
    fill_masks(ends, (z * 2 + x) * group, group, keep, flags)
    factors = backward_factors(ends, group, count, z, x)
    gs[...] = jnp.zeros_like(gs)

    def add_row(index, value, lanes=slice(None)):
        gs[index : index + 1, lanes] = gs[index : index + 1, lanes] + jnp.sum(
            value.astype(f32), axis=0, keepdims=True
        )

    def unit_of(slot):
        return wbuf[slot].reshape(width, width)

    for i in range(bands):
        add_row(8, dy_ref[i * BAND : (i + 1) * BAND, :])
    for j in range(blocks):
        if j != 2:
            pump(True)
        if j == 0:
            pump()
        w_loads[2, j].wait()
        u_loads[j].wait()

        def hidden_back(i, carry):
            span = band_span(i)
            back = dot(dy_ref[span, :], unit_of(j % 2), True)
            back = (back * gelu_slope(ubuf[j % 2, span, :])).astype(bf16)
            big[j, span, :] = back
            add_row(9 + j, back)
            return carry

        lax.fori_loop(0, bands, hidden_back, 0)
        if j + 2 < blocks:
            w_loads[2, j + 2] = load(w_ref.at[8 + j + 2], wbuf.at[j % 2])
            u_loads[j + 2] = load(up_ref.at[j + 2], ubuf.at[j % 2])
        else:
            w_loads[1, j - 2] = load(w_ref.at[4 + j - 2], wbuf.at[j % 2])
            u_loads[j + 2] = load(ratio_ref.at[j - 2], ubuf.at[j % 2])
    for j in range(blocks):
        if j % 2:
            pump(True)
        w_loads[1, j].wait()

        def up_back(i, carry):
            span = band_span(i)
            back = dot(big[j, span, :], unit_of(j % 2), True)
            acc[span, :] = back if j == 0 else acc[span, :] + back
            return carry

        lax.fori_loop(0, bands, up_back, 0)
        if j + 2 < blocks:
            w_loads[1, j + 2] = load(w_ref.at[4 + j + 2], wbuf.at[j % 2])
        elif j + 2 == blocks:
            w_loads[0, 3] = load(w_ref.at[3], wbuf.at[0])
        else:
            low_loads = [load(low_ref.at[0], wbuf.at[1, 0]), load(low_ref.at[1], wbuf.at[1, 1])]
    resid_load.wait()
    w_loads[0, 3].wait()

    def middle_back(i, carry):
        span = band_span(i)
        upstream = acc[span, :]
        back, unit = norm_back(grad_ref[span, :], upstream, rows_ref[2:3, :])
        add_row(2, upstream * unit)
        add_row(3, upstream)
        total = dy_ref[span, :].astype(f32) + back
        grad_ref[span, :] = total
        low = total.astype(bf16)
        da[span, :] = low
        add_row(7, low)
        acc[span, :] = dot(low, unit_of(0), True)
        return carry

    for i in range(bands):
        middle_back(i, 0)
        if i == 0:
            pump(True)
    low_loads.append(load(low_ref.at[2], wbuf.at[0, 0]))
    gs_early[...] = gs[...]
    early = Totals(count, place, gs_early, early_got, early_sum, hs, hr)
    early.send(0)
    u_loads[blocks].wait()
    u_loads[blocks + 1].wait()

    def ratio_back(p, carry):
        lanes = pair_span(p)
        first = lanes_of(0)
        for i in range(bands):
            span = slice(i * BAND, (i + 1) * BAND)
            inverse = 1.0 / ubuf[1, span, lanes]
            scaled = acc[span, lanes] * inverse
            dnum[span, lanes] = scaled.astype(bf16)
            weighted = scaled * ubuf[0, span, lanes] * inverse
            one = jnp.sum(jnp.where(first, weighted, 0.0), axis=1, keepdims=True)
            two = jnp.sum(jnp.where(first, 0.0, weighted), axis=1, keepdims=True)
            dden[span, lanes] = -jnp.where(first, one, two)
        return carry

    lax.fori_loop(0, pairs, ratio_back, 0)
    for copy in low_loads:
        copy.wait()
    query, key, value = wbuf.at[1, 0], wbuf.at[1, 1], wbuf.at[0, 0]
    pack_message(query, dnum, flags.at[0], dden, message)
    relay = Relay(count, factors, message, across, part, spread, total_ref, state_back, (rs, rr), place)
    relay.swap()
    pump(True)
    pre_load = load(pre_ref.at[0], acc)
    pre_load.wait()

    def attend_back(p, carry):
        lanes = pair_span(p)
        (state_high, state_low), totals = pick_message(state, p)
        lane = lax.broadcasted_iota(jnp.int32, (1, PAIR), 1) % HALF
        for band in range(bands):
            span = slice(band * BAND, (band + 1) * BAND)
            upto = (band + 1) * BAND
            back = dnum[span, lanes]
            below = dden[span, lanes]
            high, low = split_two(pltpu.roll(below, HALF, 1))
            extra = jnp.where(lane == 0, high, jnp.where(lane == 1, low, jnp.zeros_like(low)))
            asked = query[span, lanes]
            keys = key[0:upto, lanes]
            held = value[0:upto, lanes]
            kept = keep[span, 0:upto]
            found, key_back, value_back = [], 0.0, 0.0
            for head in range(2):
                mine = lanes_of(head)
                masked = jnp.where(mine, asked, 0)
                scores = (dot(masked, keys, True) * kept).astype(bf16)
                scores_back = dot(jnp.where(mine, back, extra), jnp.where(mine, held, 1), True)
                scores_back = (scores_back * kept).astype(bf16)
                found.append(dot(scores_back, keys))
                key_back = key_back + dot_down(scores_back, masked)
                value_back = value_back + dot_down(scores, jnp.where(mine, back, 0))
            across_blocks = dot(back, state_high, True) + dot(back, state_low, True) + below * totals
            query_back = jnp.where(lanes_of(0), found[0], found[1]) + flags[0, span, :] * across_blocks
            pre = acc[span, lanes]
            slope = jnp.where(pre > 0, 1.0, jnp.exp(jnp.minimum(pre, 0.0)))
            dq_low[span, lanes] = (query_back * slope).astype(bf16)
            for index, total in ((0, key_back), (1, value_back)):
                if band:
                    ubuf[index, 0 : upto - BAND, lanes] = (
                        ubuf[index, 0 : upto - BAND, lanes] + total[: upto - BAND]
                    )
                ubuf[index, span, lanes] = total[upto - BAND :]
        return carry

    quarter = pairs // 4
    limit = sums.total - count
    for part in range(4):
        lax.fori_loop(part * quarter, (part + 1) * quarter, attend_back, 0)
        if part == 0:
            relay.spread_out()
        elif part == 2:
            relay.join()
        pump(sums.done["a"] < limit)
        early.receive()
        if part < 3:
            early.send(part + 1)
    pre_load = load(pre_ref.at[1], acc)
    make_until(limit)
    relay.finish()
    pre_load.wait()

    def attend_close(p, carry):
        lanes = pair_span(p)
        (back_high, back_low), totals = pick_message(state_back, p)
        for i in range(bands):
            span = slice(i * BAND, (i + 1) * BAND)
            flag = flags[1, span, :]
            held, keys = value[span, lanes], key[span, lanes]
            key_back = ubuf[0, span, lanes] + flag * (
                dot(held, back_high, True) + dot(held, back_low, True) + totals
            )
            pre = acc[span, lanes]
            slope = jnp.where(pre > 0, 1.0, jnp.exp(jnp.minimum(pre, 0.0)))
            big[1, span, lanes] = (key_back * slope).astype(bf16)
            value_back = ubuf[1, span, lanes] + flag * (dot(keys, back_high) + dot(keys, back_low))
            big[2, span, lanes] = value_back.astype(bf16)
            big[0, span, lanes] = dq_low[span, lanes]
            big[3, span, lanes] = da[span, lanes]
        for index in range(3):
            total = jnp.sum(big[index, :, lanes].astype(f32), axis=0, keepdims=True)
            gs[4 + index : 5 + index, lanes] = total
        return carry

    lax.fori_loop(0, pairs, attend_close, 0)
    x_load = load(x_ref, dq_low)
    w_loads[0, 0] = load(w_ref.at[0], wbuf.at[0])
    w_loads[0, 1] = load(w_ref.at[1], wbuf.at[1])
    for j in range(3):
        pump(True)
        w_loads[0, j].wait()

        def input_back(i, carry):
            span = band_span(i)
            back = dot(big[j, span, :], unit_of(j % 2), True)
            acc[span, :] = back if j == 0 else acc[span, :] + back
            return carry

        lax.fori_loop(0, bands, input_back, 0)
        if j == 0:
            w_loads[0, 2] = load(w_ref.at[2], wbuf.at[0])

    x_load.wait()

    def outer_back(i, carry):
        span = band_span(i)
        upstream = acc[span, :]
        back, unit = norm_back(dq_low[span, :].astype(f32), upstream, rows_ref[0:1, :])
        add_row(0, upstream * unit)
        add_row(1, upstream)
        grad_ref[span, :] = grad_ref[span, :] + back
        return carry

    lax.fori_loop(0, bands, outer_back, 0)
    totals = Totals(count, place, gs, small_got, small_sum, ms, mr)
    totals.send(0)
    pump(sums.done["a"] < sums.total)
    for stage in range(1, 4):
        totals.receive()
        totals.send(stage)
        pump()
    make_until(sums.total)
    totals.receive()
    small_out[...] = totals.value()
    while sums.done["e"] < sums.total:
        pump()
        if sums.done["e"] >= 2 * count and 1 not in placed:
            place_batch(1, early_sum.at[3])
    place_batch(0, small_out)
    for b in range(batches):

        @pl.when(seq != owner[b])
        def _():
            moved_copy(b, 0).wait_send()
            moved_copy(b, 1).start()

    sums.wait_sends()
    relay.wait_sends()
    totals.wait_sends()
    early.wait_sends()
    keep_own = pltpu.make_async_copy(sums_ref, all_ref.at[:, y, c], self_sem.at[0])
    keep_own.start()
    over = remote(sums_ref, all_ref.at[:, y, c], ys.at[0], yr.at[0], pair[1])
    over.start()
    mine = jnp.where(seq == owner[1], 1, jnp.where(seq == owner[2], 2, 0))

    def result(where):
        return split_rows(wbuf.at[1], where * rows, rows)

    def give_back(where, k):
        peer = {"seq": where, "stream": y * 2 + c}
        return remote(result(where), ortho_ref.at[mine, y, c], os_.at[k], or_.at[mine], peer)

    def keep_rows():
        return pltpu.make_async_copy(result(seq), ortho_ref.at[mine, y, c], self_sem.at[1])

    def far_first(index, parts):
        return jnp.where(z * 2 >= count, index, parts - 1 - index)

    def finished(part, height):
        for k in range(height // rows):
            where = part * (height // rows) + k

            @pl.when(where != seq)
            def _():
                give_back(where, where).start()

            @pl.when(where == seq)
            def _():
                keep_rows().start()

    @pl.when(is_owner)
    def _():
        def arrive(half):
            for k in range(1, nseq):
                there = lax.rem(seq + k, nseq)
                block = split_rows(halves[half], there * rows, rows)
                remote(staged.at[0, 0], block, vs.at[0, 0], vr.at[half, there], pair[1]).wait_recv()

        arrive(0)
        orthogonalize(
            m_high, m_low, full, wbuf, ubuf, extra, far_first, lambda: arrive(1), finished
        )

    keep_own.wait()
    over.wait_recv()
    share = remote(all_ref.at[:, :, c], all_ref.at[:, :, c], ys.at[1], yr.at[1], pair[2])
    share.start()
    hops, lasts = [], []
    for b in (2, 1, 0):
        target = ortho_ref.at[b, y, c]

        @pl.when(seq == owner[b])
        def _():
            keep_rows().wait()

        @pl.when(seq != owner[b])
        def _():
            remote(result(seq), target, os_.at[0], or_.at[b], pair[1]).wait_recv()

        hop = remote(target, target, js.at[b], jr.at[b], pair[1])
        hop.start()
        hops.append(hop)
    for b, hop in zip((2, 1, 0), hops):
        hop.wait_recv()
        target = ortho_ref.at[b, :, c]
        last = remote(target, target, ks.at[b], kr.at[b], pair[2])
        last.start()
        lasts.append(last)
    for last in lasts:
        last.wait_recv()
    share.wait_recv()
    for copy in [over, share] + hops + lasts:
        copy.wait_send()
    for b in range(batches):

        @pl.when(seq != owner[b])
        def _():
            moved_copy(b, 1).wait_send()

    @pl.when(is_owner)
    def _():
        for k in range(1, nseq):
            there = lax.rem(seq + k, nseq)
            give_back(there, there).wait_send()


def backward(x, dy, w, rows, low, pre, ratio, left, resid, up, act, state, lengths, order, momentum, nseq):
    group, width = x.shape
    count, batches = nseq // 2, 3
    share_rows = width // nseq
    steps = batches * count
    f32, bf16 = jnp.float32, jnp.bfloat16
    V, S, R = pltpu.VMEM, jax.ShapeDtypeStruct, pltpu.SemaphoreType.REGULAR
    smem = pl.BlockSpec(memory_space=pltpu.SMEM)
    message = (2, 264, PAIR)
    blocks = up.shape[0]
    piece = (share_rows, width)
    return pl.pallas_call(
        functools.partial(backward_kernel, count),
        out_shape=(
            S((group, width), f32),
            S((16, width), f32),
            S((batches, 2, 2) + piece, f32),
            S((batches, 2, 2) + piece, bf16),
        ),
        in_specs=[ANY, VMEM, ANY, VMEM] + [ANY] * 7 + [VMEM, smem, smem, ANY],
        out_specs=[VMEM, VMEM, ANY, ANY],
        scratch_shapes=[
            V((2, 2, 2) + piece, bf16),
            V((2, 2, 2) + piece, bf16),
            V((2, 2) + piece, f32),
            V((3, 2) + piece, bf16),
            V((4, 2) + piece, bf16),
            V((2, 2) + piece, f32),
            V((3,) + piece, bf16),
            V((4,) + piece, bf16),
            V((2,) + piece, f32),
            V((count - 1,) + piece, bf16),
            V((batches, count - 1) + piece, bf16),
            V((batches,) + piece, f32),
            V(piece, f32),
            V((batches, 2) + piece, bf16),
            V((width // group, group, width), bf16),
            V((width // group, group, width), bf16),
            V((width // group, group, width), f32),
            V((blocks, group, width), bf16),
            V((2, blocks, 2 * share_rows, group), bf16),
            V((2, width // group, group, width), bf16),
            V((2, group, width), f32),
            V((2, group, width), bf16),
            V((group, group), f32),
            V((2, group, PAIR), f32),
            V((16, width), f32),
            V((16, width), f32),
            V(message, f32),
            V(message, f32),
            V(message[1:], f32),
            V((count - 1,) + message[1:], f32),
            V(message, f32),
            V(message, f32),
            V((count + 2, 16, width), f32),
            V((4, 16, width), f32),
            V((count + 2, 16, width), f32),
            V((4, 16, width), f32),
            DMA((32,)),
            DMA((steps,)),
            DMA((steps,)),
            DMA((steps,)),
            DMA((steps,)),
            DMA((steps,)),
            DMA((steps,)),
            DMA((steps,)),
            DMA((batches, count - 1)),
            DMA((batches, count - 1)),
            R,
            R((2,)),
            R((2,)),
            DMA((count + 1,)),
            DMA((count + 1,)),
            DMA((count + 2,)),
            DMA((count + 2,)),
            DMA((count + 2,)),
            DMA((count + 2,)),
            DMA((batches, 2)),
            DMA((2, nseq)),
            DMA((2,)),
            DMA((2,)),
            DMA((2,)),
            DMA((nseq,)),
            DMA((batches,)),
            DMA((batches,)),
            DMA((batches,)),
            DMA((batches,)),
            DMA((batches,)),
        ],
        compiler_params=pltpu.CompilerParams(
            collective_id=1, has_side_effects=True, vmem_limit_bytes=VMEM_LIMIT
        ),
    )(x, dy, w.reshape(-1, width // group, group, width), rows, low, pre, ratio, left, resid, up, act, state, lengths, order,
      momentum.reshape((batches, 2, 2) + piece))


STEP = 10


def padded(vector):
    short = 2048 - vector.shape[-1]
    edges = [(0, 0)] * (vector.ndim - 1) + [(0, short)]
    return jnp.pad(vector, edges).reshape(vector.shape[:-1] + (16, 128))


def local(
    tokens, cotangent, lengths, order, weights, momentum, small_params, moment_one, moment_two
):
    width = tokens.shape[2]
    nseq = lax.axis_size("seq")
    share = small_params.shape[0]
    rounded = lax.reduce_precision(small_params, 8, 7)
    aligned = share % 128 == 0
    if aligned:
        shared = padded(rounded)
    else:
        shared = lax.all_gather(rounded, "seq", axis=0, tiled=True).reshape(-1, width)
    (gathered, block_out, rows, *kept) = forward(
        tokens[0], weights, shared, lengths, order, nseq, aligned
    )
    input_grad, totals, new_momentum, update = backward(
        tokens[0], cotangent[0], gathered, rows, *kept, lengths, order, momentum, nseq
    )
    start = lax.axis_index("seq") * share
    row_small = lax.dynamic_slice(totals[:13].reshape(-1), (start,), (share,))
    new_momentum, update = new_momentum.reshape(weights.shape), update.reshape(weights.shape)
    blocks = (weights.shape[0] - 4) // 2
    rates = jnp.array([0.5] * 3 + [4.0] + [0.5] * blocks + [0.25] * blocks, dtype=jnp.float32)
    new_weights = weights - rates[:, None, None] * (update.astype(jnp.float32) + 0.01 * weights)
    first_new = 0.9 * moment_one + 0.1 * row_small
    second_new = 0.95 * moment_two + 0.05 * row_small * row_small
    adjusted = first_new / (1.0 - 0.9**STEP) / (jnp.sqrt(second_new / (1.0 - 0.95**STEP)) + 1e-08)
    new_small = small_params - 0.05 * (adjusted + 0.01 * small_params)
    return (
        block_out[None], input_grad[None], new_weights, new_momentum, new_small, first_new, second_new,
    )


def solution(mesh):
    in_specs = (
        P("stream", "seq", None),
        P("stream", "seq", None),
        P("stream", None),
        P("stream", None),
        P(None, "seq", None),
        P(None, "seq", None),
        P("seq"),
        P("seq"),
        P("seq"),
    )
    out_specs = (
        P("stream", "seq", None),
        P("stream", "seq", None),
        P(None, "seq", None),
        P(None, "seq", None),
        P("seq"),
        P("seq"),
        P("seq"),
    )
    return jax.shard_map(local, mesh=mesh, in_specs=in_specs, out_specs=out_specs, check_vma=False)
```
